32 devices in a mesh: gr: 4 (over z), gc: 8 (over y, x, core).
Axes of the slice: x: 2, y: 2, z: 4, core: 2. Of those that a mesh axis runs over, the one named last changes fastest.
Arguments:
- tokens: bfloat16 [32768, 768], P(('gr', 'gc')), may hold values from -6 to 6
- span_ids: int32 [64, 512], P(('gr', 'gc')), may hold values from 0 to 3, as said below
- mlm_pos: int32 [256, 24], P(('gr', 'gc')), may hold values from 0 to 511, as said below
- mlm_count: int32 [256], P(('gr', 'gc')), may hold values from 12 to 24
- mlm_grad: bfloat16 [256, 24, 768], P(('gr', 'gc')), may hold values from -0.59765625 to 0.59765625
- positive: int32 [256], replicated, may hold values from 0 to 255, as said below
- w_in: bfloat16 [768, 2304], replicated, may hold values from -0.21875 to 0.21875
- b_query: float32 [768], replicated, may hold values from -3 to 3
- b_value: float32 [768], replicated, may hold values from -0.6 to 0.6
- w_out: bfloat16 [768, 768], replicated, may hold values from -1.25 to 1.25
- b_out: float32 [768], replicated, may hold values from -1.2 to 1.2
- ln1_gain: float32 [768], replicated, may hold values from 0.25 to 1.75
- ln1_bias: float32 [768], replicated, may hold values from -1.2 to 1.2
- w_up: bfloat16 [768, 3072], replicated, may hold values from -0.21875 to 0.21875
- b_up: float32 [3072], replicated, may hold values from -3 to 3
- w_down: bfloat16 [3072, 768], replicated, may hold values from -0.109375 to 0.109375
- b_down: float32 [768], replicated, may hold values from -1.2 to 1.2
- ln2_gain: float32 [768], replicated, may hold values from 0.25 to 1.75
- ln2_bias: float32 [768], replicated, may hold values from -1.2 to 1.2
Outputs:
- layer_out: bfloat16 [32768, 768], P(('gr', 'gc'))
- grad_tokens: float32 [32768, 768], P(('gr', 'gc'))
- grad_w_in: float32 [768, 2304], replicated
- grad_b_query: float32 [768], replicated
- grad_b_value: float32 [768], replicated
- grad_w_out: float32 [768, 768], replicated
- grad_b_out: float32 [768], replicated
- grad_ln1_gain: float32 [768], replicated
- grad_ln1_bias: float32 [768], replicated
- grad_w_up: float32 [768, 3072], replicated
- grad_b_up: float32 [3072], replicated
- grad_w_down: float32 [3072, 768], replicated
- grad_b_down: float32 [768], replicated
- grad_ln2_gain: float32 [768], replicated
- grad_ln2_bias: float32 [768], replicated
- contrast_loss: float32 [], replicated
The draws below stay inside these ranges and needn't reach their ends.
Inputs may be any that keep to these rules, and one draw needn't show every extreme that they name: `span_ids`: along each row the span number never falls, starts at 0 and takes every value up to 3; each span holds at least 32 positions. `mlm_pos`: all 24 slots of a span hold distinct positions of that span in its row; only the first mlm_count of them are used. `positive`: A span's partner is never the span itself.
All inputs are finite; a program needn't handle non-finite values.
Results may differ from the reference program's by a relative error of at most 0.015.
Values may be sent and summed in bfloat16 or wider, within the bound.
No kernel may reach another device: no remote copies, remote signals or barrier semaphores. Data moves between devices by JAX's collectives and lax.ppermute only.
A program may use at most 192 MiB of HBM per device.

```python
from functools import partial
import jax
import jax.numpy as jnp
from jax import lax

D = 768
HEADS = 12
HEAD_DIM = 64
FF = 3072
ROW_LEN = 512
SPANS_ROW = 4
MAXM = 24
ROWS = 64
TOKENS = 32768
SPANS = 256


def span_bounds(key):
    key = jax.random.fold_in(key, 101)
    jitter = ROW_LEN * 3 // 32
    shifts = jax.random.randint(key, (ROWS, SPANS_ROW - 1), -jitter, jitter + 1)
    marks = jnp.arange(1, SPANS_ROW, dtype=jnp.int32) * (ROW_LEN // SPANS_ROW)
    return marks[None, :] + shifts


def draw_span_ids(key, part):
    bounds = span_bounds(key)
    places = jnp.arange(ROW_LEN, dtype=jnp.int32)
    return jnp.sum((places[None, :, None] >= bounds[:, None, :]).astype(jnp.int32), axis=-1).astype(jnp.int32)


def draw_mlm_pos(key, part):
    bounds = span_bounds(key)
    key = jax.random.fold_in(key, 2)
    lowest = jnp.concatenate([jnp.zeros((ROWS, 1), jnp.int32), bounds], axis=1)
    highest = jnp.concatenate([bounds, jnp.full((ROWS, 1), ROW_LEN, jnp.int32)], axis=1)
    places = jnp.arange(ROW_LEN, dtype=jnp.int32)
    inside = (places[None, None, :] >= lowest[:, :, None]) & (places[None, None, :] < highest[:, :, None])
    noise = jax.random.randint(key, (ROWS, SPANS_ROW, ROW_LEN), 0, 2 ** 20)
    ranking = jnp.where(inside, noise, 2 ** 21) * ROW_LEN + places[None, None, :]
    ordered = jnp.argsort(ranking, axis=-1, stable=True)[:, :, :MAXM]
    return ordered.reshape(ROWS * SPANS_ROW, MAXM).astype(jnp.int32)


def draw_mlm_count(key, part):
    key = jax.random.fold_in(key, 3)
    first_key, other_key, pick_key = jax.random.split(key, 3)
    factor_one = jax.random.randint(first_key, (SPANS,), 0, MAXM)
    factor_two = jax.random.randint(other_key, (SPANS,), 0, MAXM)
    counts = MAXM // 2 + factor_one * factor_two // (2 * MAXM)
    chosen = jax.random.randint(pick_key, (), 0, SPANS)
    return jnp.where(jnp.arange(SPANS, dtype=jnp.int32) == chosen, MAXM, counts).astype(jnp.int32)


def draw_positive(key, part):
    key = jax.random.fold_in(key, 4)
    offsets = jax.random.randint(key, (SPANS,), 1, SPANS)
    return ((jnp.arange(SPANS, dtype=jnp.int32) + offsets) % SPANS).astype(jnp.int32)


def steps_of(rng, dims, pieces, least, high):
    def one(axis_at, parts):
        steps = jax.random.uniform(jax.random.fold_in(jax.random.fold_in(rng, 6), axis_at), (parts,), jnp.float32, least / len(pieces), high / len(pieces))
        return jnp.repeat(jnp.exp(steps), dims[axis_at] // parts).reshape((-1,) + (1,) * (len(dims) - axis_at - 1))

    loudness = one(*pieces[0])
    for cut in pieces[1:]:
        loudness = loudness * one(*cut)
    return loudness


def bell_draw(own_key, shape, scale, most, cuts=(), held_as=jnp.bfloat16):
    level = steps_of(own_key, shape, cuts, -0.22, 0.18) if cuts else 1.0
    drawn = jax.random.normal(own_key, shape, jnp.float32) * scale * level
    return jnp.minimum(jnp.maximum(drawn, -most), most).astype(held_as)


def setup_inputs(seed: int = 0) -> dict:
    streams_of = jax.random.split(jax.random.key(seed), 20)
    return {
        "tokens": bell_draw(streams_of[0], (TOKENS, D), 1.0, 6.0, ((0, 32),)),
        "span_ids": draw_span_ids(jax.random.fold_in(streams_of[19], 71), 0),
        "mlm_pos": draw_mlm_pos(jax.random.fold_in(streams_of[19], 71), 0),
        "mlm_count": draw_mlm_count(jax.random.fold_in(streams_of[19], 71), 0),
        "mlm_grad": bell_draw(streams_of[4], (SPANS, MAXM, D), 0.1, 0.59765625, ((0, 32),)),
        "positive": draw_positive(jax.random.fold_in(streams_of[19], 71), 0),
        "w_in": bell_draw(streams_of[6], (D, 3 * D), D ** -0.5, 0.21875),
        "b_query": bell_draw(streams_of[7], (D,), 0.5, 3.0, (), jnp.float32),
        "b_value": bell_draw(streams_of[8], (D,), 0.1, 0.6, (), jnp.float32),
        "w_out": bell_draw(streams_of[9], (D, D), (D // 32) ** -0.5, 1.25),
        "b_out": bell_draw(streams_of[10], (D,), 0.2, 1.2, (), jnp.float32),
        "ln1_gain": jnp.clip(1.0 + 0.15 * jax.random.normal(streams_of[11], (D,), jnp.float32), 0.25, 1.75),
        "ln1_bias": bell_draw(streams_of[12], (D,), 0.2, 1.2, (), jnp.float32),
        "w_up": bell_draw(streams_of[13], (D, FF), D ** -0.5, 0.21875),
        "b_up": bell_draw(streams_of[14], (FF,), 0.5, 3.0, (), jnp.float32),
        "w_down": bell_draw(streams_of[15], (FF, D), FF ** -0.5, 0.109375),
        "b_down": bell_draw(streams_of[16], (D,), 0.2, 1.2, (), jnp.float32),
        "ln2_gain": jnp.clip(1.0 + 0.15 * jax.random.normal(streams_of[17], (D,), jnp.float32), 0.25, 1.75),
        "ln2_bias": bell_draw(streams_of[18], (D,), 0.2, 1.2, (), jnp.float32),
    }


@jax.custom_vjp
def low(v):
    return lax.optimization_barrier(v.astype(jnp.bfloat16)).astype(jnp.float32)

@jax.custom_vjp
def low_back(v):
    return v

def low_keep(v):
    return (low(v), None)

def low_pass(kept, grad):
    return (grad,)

def back_keep(v):
    return (v, None)

def back_low(kept, grad):
    return (low(grad),)
low.defvjp(low_keep, low_pass)
low_back.defvjp(back_keep, back_low)
HIGH = lax.Precision.HIGHEST
NEG = -1e+30
EPS = 1e-12

def low_both(values):
    return low(low_back(values))

def matmul(left, right):
    return jnp.dot(left, right, precision=HIGH)

def normalize(values):
    centre = values - lax.optimization_barrier(jnp.mean(values, axis=-1, keepdims=True))
    factor = lax.rsqrt(lax.optimization_barrier(jnp.mean(centre * centre, axis=-1, keepdims=True)) + EPS)
    return centre * factor

def encode_row(params, row_pair):
    row_tokens, labels = row_pair
    w_in, b_query, b_value, w_out, b_out, gain_one, bias_one, w_up, b_up, w_down, b_down, gain_two, bias_two = params
    length = row_tokens.shape[0]
    packed = low_both(matmul(row_tokens, w_in) + jnp.concatenate([b_query, jnp.zeros_like(b_query), b_value]))
    queries = packed[:, :D].reshape(length, HEADS, HEAD_DIM)
    key_rows = packed[:, D:2 * D].reshape(length, HEADS, HEAD_DIM)
    values = packed[:, 2 * D:].reshape(length, HEADS, HEAD_DIM)
    scores = jnp.einsum('qhd,khd->hqk', queries, key_rows, precision=HIGH) * HEAD_DIM ** (-0.5)
    same_span = labels[:, None] == labels[None, :]
    scores = low_back(jnp.where(same_span[None], scores, NEG))
    row_top = lax.optimization_barrier(jnp.max(scores, axis=-1, keepdims=True))
    exponent = jnp.exp(scores - row_top)
    weights = exponent / lax.optimization_barrier(jnp.sum(exponent, axis=-1, keepdims=True))
    mixed_rows = jnp.einsum('hqk,khd->qhd', low(weights), values, precision=HIGH).reshape(length, D)
    mixed_rows = low_both(mixed_rows)
    branch = low_back(matmul(mixed_rows, w_out) + b_out)
    middle = normalize(row_tokens + branch) * gain_one + bias_one
    before = low_back(matmul(low(middle), w_up) + b_up)
    hidden = low(jax.nn.gelu(before, approximate=False))
    second = middle + low_back(matmul(hidden, w_down) + b_down)
    return normalize(second) * gain_two + bias_two

def objective(tokens_full, params, span_ids, positive):
    row_tokens = tokens_full.reshape(ROWS, ROW_LEN, D)
    encoded = lax.map(jax.checkpoint(partial(encode_row, params)), (row_tokens, span_ids))
    flat_out = encoded.reshape(ROWS * ROW_LEN, D)
    levels = jnp.arange(SPANS_ROW, dtype=jnp.int32)
    starts = lax.optimization_barrier(jnp.sum((span_ids[:, None, :] < levels[None, :, None]).astype(jnp.int32), axis=-1))
    cls_index = (jnp.arange(ROWS, dtype=jnp.int32)[:, None] * ROW_LEN + starts).reshape(-1)
    cls_rows = low(flat_out[cls_index])
    similar = matmul(cls_rows, cls_rows.T) * (2.0 * D ** (-0.5))
    own_span = jnp.arange(SPANS, dtype=jnp.int32)[:, None] == jnp.arange(SPANS, dtype=jnp.int32)[None, :]
    similar = low_back(jnp.where(own_span, NEG, similar))
    row_top = lax.optimization_barrier(jnp.max(similar, axis=1, keepdims=True))
    log_rows = row_top[:, 0] + jnp.log(lax.optimization_barrier(jnp.sum(jnp.exp(similar - row_top), axis=1)))
    chosen = jnp.take_along_axis(similar, positive[:, None].astype(jnp.int32), axis=1)[:, 0]
    return (flat_out, jnp.mean(log_rows - chosen))

def reference(tokens, span_ids, mlm_pos, mlm_count, mlm_grad, positive, w_in, b_query, b_value, w_out, b_out, ln1_gain, ln1_bias, w_up, b_up, w_down, b_down, ln2_gain, ln2_bias):
    params = (w_in.astype(jnp.float32), b_query, b_value, w_out.astype(jnp.float32), b_out, ln1_gain, ln1_bias, w_up.astype(jnp.float32), b_up, w_down.astype(jnp.float32), b_down, ln2_gain, ln2_bias)
    tokens_full = tokens.astype(jnp.float32)

    def forward(tokens_in, params_in):
        return objective(tokens_in, params_in, span_ids, positive)
    (flat_out, contrast_loss), pull = jax.vjp(forward, tokens_full, params)
    slot_rows = (jnp.arange(SPANS, dtype=jnp.int32) // SPANS_ROW * ROW_LEN)[:, None] + mlm_pos
    live = jnp.arange(MAXM, dtype=jnp.int32)[None, :] < mlm_count[:, None]
    given = jnp.where(live[:, :, None], mlm_grad.astype(jnp.float32), 0.0).reshape(SPANS * MAXM, D)
    upstream = jnp.zeros((ROWS * ROW_LEN, D), jnp.float32).at[slot_rows.reshape(-1)].add(given)
    loss_weight = jnp.ones((), contrast_loss.dtype) * SPANS
    grad_tokens, grads = pull((upstream, loss_weight))
    return (flat_out.astype(jnp.bfloat16), grad_tokens, grads[0], grads[1], grads[2], grads[3], grads[4], grads[5], grads[6], grads[7], grads[8], grads[9], grads[10], grads[11], grads[12], contrast_loss)
```

```python
import functools
import jax
import jax.numpy as jnp
from jax import lax
from jax.experimental import pallas as pl
from jax.experimental.pallas import tpu as pltpu
from jax.sharding import PartitionSpec as P

D = 768
HEADS = 12
HEAD_DIM = 64
FF = 3072
BF = jnp.bfloat16
F32 = jnp.float32
EPS = 1e-12
FAR = 1e30
HALF_ROOT = 0.7071067811865476
DENSITY = 0.3989422804014327
NN = (((1,), (0,)), ((), ()))
NT = (((1,), (1,)), ((), ()))
TN = (((0,), (0,)), ((), ()))
VMEM_CAP = 60 * 1024 * 1024


def cost(us):
    return pl.CostEstimate(flops=int(us * 1.1e9), bytes_accessed=int(us * 3e6), transcendentals=0)


def mm(left, right, dims=NN):
    return lax.dot_general(left, right, dims, preferred_element_type=F32)


def lanes(shape):
    return lax.broadcasted_iota(jnp.int32, shape, len(shape) - 1)


def normalize(values):
    centre = values - jnp.mean(values, axis=-1, keepdims=True)
    factor = lax.rsqrt(jnp.mean(centre * centre, axis=-1, keepdims=True) + EPS)
    return centre * factor, factor


def norm_back(incoming, normed, factor, gain):
    scaled = incoming * gain
    return factor * (
        scaled
        - jnp.mean(scaled, axis=-1, keepdims=True)
        - normed * jnp.mean(scaled * normed, axis=-1, keepdims=True)
    )


def span_lanes(labels, length):
    rows = lax.broadcasted_iota(jnp.int32, (128, length), 0)
    hot = jnp.where(rows == jnp.broadcast_to(labels, (128, length)), 1.0, 0.0)
    return hot.T


def attend_kernel(labels_ref, tokens_ref, w_ref, bias_ref, packed_ref, mixed_ref, lse_ref):
    row = pl.program_id(0)
    length = tokens_ref.shape[0]
    for at in range(0, 3 * D, D):
        packed_ref[:, at : at + D] = (
            mm(tokens_ref[...], w_ref[:, at : at + D]) + bias_ref[:, at : at + D]
        ).astype(BF)
    hot = span_lanes(labels_ref[pl.ds(row, 1), :], length)
    lane = lanes((length, 128))
    mark_q = (hot * FAR).astype(BF)
    mark_k = jnp.where(lane < 4, hot - 1.0, 0.0).astype(BF)
    low_half = lane < HEAD_DIM
    lse_ref[...] = jnp.zeros_like(lse_ref)

    def pair(p, carry):
        at = pl.multiple_of(p * 128, 128)
        query = packed_ref[:, pl.ds(at, 128)] * jnp.asarray(HEAD_DIM ** (-0.5), BF)
        keys = jnp.concatenate([packed_ref[:, pl.ds(D + at, 128)], mark_k], axis=1)
        values = packed_ref[:, pl.ds(2 * D + at, 128)]
        outs = []
        logs = lse_ref[...]
        for half in range(2):
            own = low_half if half == 0 else jnp.logical_not(low_half)
            queries = jnp.concatenate(
                [jnp.where(own, query, jnp.zeros_like(query)), mark_q], axis=1
            )
            scores = mm(queries, keys, NT)
            top = jnp.max(scores, axis=1, keepdims=True)
            grown = jnp.exp(scores - top)
            total = jnp.sum(grown, axis=1, keepdims=True)
            outs.append(mm(grown.astype(BF), values) * (1.0 / total))
            logs = jnp.where(lane == 2 * p + half, top + jnp.log(total), logs)
        lse_ref[...] = logs
        mixed_ref[:, pl.ds(at, 128)] = jnp.where(low_half, outs[0], outs[1]).astype(BF)
        return carry

    lax.fori_loop(0, HEADS // 2, pair, 0)


def attend(labels, tokens, w_in, bias):
    rows, length = labels.shape
    count = rows * length
    return pl.pallas_call(
        attend_kernel,
        grid=(rows,),
        in_specs=[
            pl.BlockSpec((rows, length), lambda i: (0, 0)),
            pl.BlockSpec((length, D), lambda i: (i, 0)),
            pl.BlockSpec((D, 3 * D), lambda i: (0, 0), pipeline_mode=pl.Buffered(1)),
            pl.BlockSpec((1, 3 * D), lambda i: (0, 0)),
        ],
        out_specs=[
            pl.BlockSpec((length, 3 * D), lambda i: (i, 0)),
            pl.BlockSpec((length, D), lambda i: (i, 0)),
            pl.BlockSpec((length, 128), lambda i: (i, 0)),
        ],
        out_shape=[
            jax.ShapeDtypeStruct((count, 3 * D), BF),
            jax.ShapeDtypeStruct((count, D), BF),
            jax.ShapeDtypeStruct((count, 128), F32),
        ],
        compiler_params=pltpu.CompilerParams(vmem_limit_bytes=VMEM_CAP),
        cost_estimate=cost(20),
        name="attend",
    )(labels, tokens, w_in, bias)


def feed_kernel(
    starts_ref, tokens_ref, mixed_ref, w_out_ref, w_up_ref, w_down_ref, vec_ref, b_up_ref,
    low_ref, n1_ref, f1_ref, hidden_ref, slope_ref, n2_ref, f2_ref, out_ref, cls_ref,
):
    step = pl.program_id(0)
    b_out, gain_one, bias_one, b_down, gain_two, bias_two = (vec_ref[i : i + 1, :] for i in range(6))
    first = tokens_ref[...].astype(F32) + mm(mixed_ref[...], w_out_ref[...]) + b_out
    normed, factor = normalize(first)
    n1_ref[...] = normed.astype(BF)
    f1_ref[...] = jnp.broadcast_to(factor, f1_ref.shape)
    middle = normed * gain_one + bias_one
    low = middle.astype(BF)
    low_ref[...] = low
    total = middle + b_down
    for at in range(0, FF, D):
        before = mm(low, w_up_ref[:, at : at + D]) + b_up_ref[:, at : at + D]
        share = 0.5 * (1.0 + lax.erf(before * HALF_ROOT))
        hidden = (before * share).astype(BF)
        hidden_ref[:, at : at + D] = hidden
        slope_ref[:, at : at + D] = (
            share + before * jnp.exp(-0.5 * before * before) * DENSITY
        ).astype(BF)
        total = total + mm(hidden, w_down_ref[at : at + D, :])
    normed_two, factor_two = normalize(total)
    n2_ref[...] = normed_two.astype(BF)
    f2_ref[...] = jnp.broadcast_to(factor_two, f2_ref.shape)
    encoded = (normed_two * gain_two + bias_two).astype(BF)
    out_ref[...] = encoded
    size = tokens_ref.shape[0]
    spans = cls_ref.shape[0]
    place = lax.broadcasted_iota(jnp.int32, (spans, size), 1) + step * size
    pick = jnp.where(place == starts_ref[...], 1.0, 0.0).astype(BF)
    part = mm(pick, encoded)

    @pl.when(step == 0)
    def _():
        cls_ref[...] = part

    @pl.when(step != 0)
    def _():
        cls_ref[...] += part


def feed(starts, tokens, mixed, w_out, w_up, w_down, vecs, b_up, size=512):
    count = tokens.shape[0]
    spans = starts.shape[0]
    whole = lambda i: (0, 0)
    block = lambda i: (i, 0)
    once = pl.Buffered(1)
    return pl.pallas_call(
        feed_kernel,
        grid=(count // size,),
        in_specs=[
            pl.BlockSpec((spans, 1), whole),
            pl.BlockSpec((size, D), block),
            pl.BlockSpec((size, D), block),
            pl.BlockSpec((D, D), whole, pipeline_mode=once),
            pl.BlockSpec((D, FF), whole, pipeline_mode=once),
            pl.BlockSpec((FF, D), whole, pipeline_mode=once),
            pl.BlockSpec(vecs.shape, whole),
            pl.BlockSpec((1, FF), whole),
        ],
        out_specs=[
            pl.BlockSpec((size, D), block),
            pl.BlockSpec((size, D), block),
            pl.BlockSpec((size, 128), block),
            pl.BlockSpec((size, FF), block),
            pl.BlockSpec((size, FF), block),
            pl.BlockSpec((size, D), block),
            pl.BlockSpec((size, 128), block),
            pl.BlockSpec((size, D), block),
            pl.BlockSpec((spans, D), whole),
        ],
        out_shape=[
            jax.ShapeDtypeStruct((count, D), BF),
            jax.ShapeDtypeStruct((count, D), BF),
            jax.ShapeDtypeStruct((count, 128), F32),
            jax.ShapeDtypeStruct((count, FF), BF),
            jax.ShapeDtypeStruct((count, FF), BF),
            jax.ShapeDtypeStruct((count, D), BF),
            jax.ShapeDtypeStruct((count, 128), F32),
            jax.ShapeDtypeStruct((count, D), BF),
            jax.ShapeDtypeStruct((spans, D), F32),
        ],
        compiler_params=pltpu.CompilerParams(vmem_limit_bytes=VMEM_CAP),
        cost_estimate=cost(22),
        name="feed",
    )(starts, tokens, mixed, w_out, w_up, w_down, vecs, b_up)

NEG = -1e30


def split3(values):
    high = values.astype(BF)
    rest = values - high.astype(F32)
    mid = rest.astype(BF)
    return high, mid, (rest - mid.astype(F32)).astype(BF)


def contrast_kernel(
    me_ref, partner_ref, cls_ref, starts_ref, pos_ref, count_ref, given_ref, n2_ref, f2_ref, gain_ref,
    loss_ref, second_ref, branch_ref, sums_ref, table, own_grad,
):
    step = pl.program_id(0)
    devices, spans, _ = cls_ref.shape
    total = devices * spans
    me = me_ref[0]

    @pl.when(step == 0)
    def _():
        for r in range(devices):
            table[pl.ds(pl.multiple_of((r ^ me) * spans, spans), spans), :] = cls_ref[r].astype(F32)
        rows = table[...].astype(BF)
        scale = 2.0 * D ** (-0.5)
        similar = mm(rows, rows, NT) * scale
        own = lax.broadcasted_iota(jnp.int32, (total, total), 0)
        other = lax.broadcasted_iota(jnp.int32, (total, total), 1)
        similar = jnp.where(own == other, NEG, similar)
        partner = partner_ref[...] == other
        top = jnp.max(similar, axis=1, keepdims=True)
        log_rows = top + jnp.log(jnp.sum(jnp.exp(similar - top), axis=1, keepdims=True))
        chosen = jnp.sum(jnp.where(partner, similar, 0.0), axis=1, keepdims=True)
        loss = jnp.sum(log_rows - chosen, axis=0, keepdims=True) / total
        loss_ref[...] = jnp.broadcast_to(loss, loss_ref.shape)
        slope = (jnp.exp(similar - log_rows) - jnp.where(partner, 1.0, 0.0)).astype(BF)
        spot = lax.broadcasted_iota(jnp.int32, (spans, total), 0) + me * spans
        pick = jnp.where(spot == lax.broadcasted_iota(jnp.int32, (spans, total), 1), 1.0, 0.0).astype(BF)
        mine = mm(pick, slope).astype(BF)
        across = mm(pick, slope, NT).astype(BF)
        own_grad[...] = (mm(mine, rows) + mm(across, rows)) * scale

    size = n2_ref.shape[0]
    slots = given_ref.shape[0]
    each = slots // spans
    place = lax.broadcasted_iota(jnp.int32, (size, slots), 0) + step * size
    hot = jnp.where(place == pos_ref[...], 1.0, 0.0).astype(BF)
    upstream = mm(hot, given_ref[...])
    spot = lax.broadcasted_iota(jnp.int32, (size, spans), 0) + step * size
    hot_cls = jnp.where(spot == starts_ref[...], 1.0, 0.0).astype(BF)
    parts = split3(own_grad[...])
    upstream += mm(hot_cls, parts[0]) + (mm(hot_cls, parts[1]) + mm(hot_cls, parts[2]))
    normed = n2_ref[...].astype(F32)
    second = norm_back(upstream, normed, f2_ref[:, 0:1], gain_ref[...])
    branch = second.astype(BF)
    second_ref[...] = second
    branch_ref[...] = branch
    new = jnp.concatenate(
        [
            jnp.sum(upstream * normed, axis=0, keepdims=True),
            jnp.sum(upstream, axis=0, keepdims=True),
            jnp.sum(branch.astype(F32), axis=0, keepdims=True),
            jnp.zeros((5, D), F32),
        ],
        axis=0,
    )

    @pl.when(step == 0)
    def _():
        sums_ref[...] = new

    @pl.when(step != 0)
    def _():
        sums_ref[...] += new


def contrast(me, partner, cls, starts_row, pos, given, n2, f2, gain_two, size=256):
    count = n2.shape[0]
    devices, spans, _ = cls.shape
    slots = given.shape[0]
    whole = lambda i, me: (0, 0)
    block = lambda i, me: (i, 0)
    def body(me_ref, partner_ref, cls_ref, starts_ref, pos_ref, given_ref, *rest):
        contrast_kernel(me_ref, partner_ref, cls_ref, starts_ref, pos_ref, None, given_ref, *rest)
    return pl.pallas_call(
        body,
        grid_spec=pltpu.PrefetchScalarGridSpec(
            num_scalar_prefetch=1,
            grid=(count // size,),
            in_specs=[
                pl.BlockSpec((devices * spans, 1), whole),
                pl.BlockSpec((devices, spans, D), lambda i, me: (0, 0, 0)),
                pl.BlockSpec((1, spans), whole),
                pl.BlockSpec((1, slots), whole),
                pl.BlockSpec((slots, D), whole),
                pl.BlockSpec((size, D), block),
                pl.BlockSpec((size, 128), block),
                pl.BlockSpec((1, D), whole),
            ],
            out_specs=[
                pl.BlockSpec((8, 128), whole),
                pl.BlockSpec((size, D), block),
                pl.BlockSpec((size, D), block),
                pl.BlockSpec((8, D), whole),
            ],
            scratch_shapes=[pltpu.VMEM((devices * spans, D), F32), pltpu.VMEM((spans, D), F32)],
        ),
        out_shape=[
            jax.ShapeDtypeStruct((8, 128), F32),
            jax.ShapeDtypeStruct((count, D), F32),
            jax.ShapeDtypeStruct((count, D), BF),
            jax.ShapeDtypeStruct((8, D), F32),
        ],
        compiler_params=pltpu.CompilerParams(vmem_limit_bytes=VMEM_CAP),
        cost_estimate=cost(8),
        name="contrast",
    )(me, partner, cls, starts_row, pos, given, n2, f2, gain_two)


def tile_place(kind, j):
    order = (0, 1, 2, 3) if kind == 0 else (1, 0, 2, 3)
    out = 0
    for bit in order:
        out = out * 2 + ((j >> bit) & 1)
    return out


def grad_kernel(tile_rows, me_ref, *refs):
    out_ref = refs[-1]
    pieces = [
        mm(refs[i][...], refs[i + 1][...], TN).astype(BF) for i in range(0, len(refs) - 1, 2)
    ]
    joined = pieces[0] if len(pieces) == 1 else jnp.concatenate(pieces, axis=1)
    per = joined.shape[0] // (16 * tile_rows)
    for k in range(per):
        kind = k if per == 2 else pl.program_id(0)
        for j in range(16):
            at = (k * 16 + j) * tile_rows
            if per == 2:
                slot = tile_place(k, j) ^ me_ref[1 + k]
            else:
                slot = jnp.where(kind == 0, tile_place(0, j) ^ me_ref[1], tile_place(1, j) ^ me_ref[2])
            out_ref[k, slot] = joined[at : at + tile_rows, :]


def grad_down(me, hidden, branch, rel):
    count = hidden.shape[0]
    return pl.pallas_call(
        functools.partial(grad_kernel, 48),
        grid_spec=pltpu.PrefetchScalarGridSpec(
            num_scalar_prefetch=1,
            grid=(2,),
            in_specs=[
                pl.BlockSpec((count, D), lambda i, me: (0, (me[0] ^ rel) * 2 + i)),
                pl.BlockSpec((count, D), lambda i, me: (0, 0)),
            ],
            out_specs=pl.BlockSpec((1, 16, 48, D), lambda i, me: (i, 0, 0, 0)),
        ),
        out_shape=jax.ShapeDtypeStruct((2, 16, 48, D), BF),
        compiler_params=pltpu.CompilerParams(vmem_limit_bytes=VMEM_CAP),
        cost_estimate=cost(5),
        name="grad_down",
    )(me, hidden, branch)


def grad_up(me, low, d_before, rel):
    count = low.shape[0]
    return pl.pallas_call(
        functools.partial(grad_kernel, 48),
        grid_spec=pltpu.PrefetchScalarGridSpec(
            num_scalar_prefetch=1,
            grid=(2,),
            in_specs=[
                pl.BlockSpec((count, D), lambda i, me: (0, 0)),
                pl.BlockSpec((count, D), lambda i, me: (0, (me[0] ^ rel) * 2 + i)),
            ],
            out_specs=pl.BlockSpec((1, 16, 48, D), lambda i, me: (i, 0, 0, 0)),
        ),
        out_shape=jax.ShapeDtypeStruct((2, 16, 48, D), BF),
        compiler_params=pltpu.CompilerParams(vmem_limit_bytes=VMEM_CAP),
        cost_estimate=cost(5),
        name="grad_up",
    )(me, low, d_before)


def grad_in_kernel(me_ref, tokens_ref, one_ref, two_ref, mixed_ref, attn_ref, out_ref):
    length = one_ref.shape[0]
    left = mm(tokens_ref[:length, :], one_ref[...], TN) + mm(tokens_ref[length:, :], two_ref[...], TN)
    joined = jnp.concatenate(
        [left.astype(BF), mm(mixed_ref[...], attn_ref[...], TN).astype(BF)], axis=1
    )
    for k in range(2):
        for j in range(16):
            at = (k * 16 + j) * 24
            out_ref[k, tile_place(k, j) ^ me_ref[1 + k]] = joined[at : at + 24, :]


def grad_in(me, tokens, d_packed, mixed, d_attn, rel):
    count = tokens.shape[0]
    length = d_packed[0].shape[0]
    return pl.pallas_call(
        grad_in_kernel,
        grid_spec=pltpu.PrefetchScalarGridSpec(
            num_scalar_prefetch=1,
            grid=(1,),
            in_specs=[
                pl.BlockSpec((count, D), lambda i, me: (0, 0)),
                pl.BlockSpec((length, 3 * D // 2), lambda i, me: (0, me[0] ^ rel)),
                pl.BlockSpec((length, 3 * D // 2), lambda i, me: (0, me[0] ^ rel)),
                pl.BlockSpec((count, D), lambda i, me: (0, 0)),
                pl.BlockSpec((count, D // 2), lambda i, me: (0, me[0] ^ rel)),
            ],
            out_specs=pl.BlockSpec((2, 16, 24, 2 * D), lambda i, me: (0, 0, 0, 0)),
        ),
        out_shape=jax.ShapeDtypeStruct((2, 16, 24, 2 * D), BF),
        compiler_params=pltpu.CompilerParams(vmem_limit_bytes=VMEM_CAP),
        cost_estimate=cost(7),
        name="grad_in",
    )(me, tokens, *d_packed, mixed, d_attn)


def chain_kernel(
    branch_ref, second_ref, slope_ref, n1_ref, f1_ref, gain_ref, w_down_ref, w_up_ref, w_out_ref,
    before_ref, first_ref, attn_ref, mixed_ref, sums_ref, up_ref,
):
    step = pl.program_id(0)
    d_middle = second_ref[...]
    branch = branch_ref[...]
    parts = []
    for at in range(0, FF, D):
        d_hidden = mm(branch, w_down_ref[at : at + D, :], NT)
        d_before = (d_hidden * slope_ref[:, at : at + D].astype(F32)).astype(BF)
        before_ref[:, at : at + D] = d_before
        parts.append(jnp.sum(d_before.astype(F32), axis=0, keepdims=True))
        d_middle = d_middle + mm(d_before, w_up_ref[:, at : at + D], NT)
    normed = n1_ref[...].astype(F32)
    d_first = norm_back(d_middle, normed, f1_ref[:, 0:1], gain_ref[...])
    d_attn = d_first.astype(BF)
    first_ref[...] = d_first
    attn_ref[...] = d_attn
    mixed_ref[...] = mm(d_attn, w_out_ref[...], NT).astype(BF)
    new = jnp.concatenate(
        [
            jnp.sum(d_middle * normed, axis=0, keepdims=True),
            jnp.sum(d_middle, axis=0, keepdims=True),
            jnp.sum(d_attn.astype(F32), axis=0, keepdims=True),
        ]
        + parts
        + [jnp.zeros((1, D), F32)],
        axis=0,
    )

    @pl.when(step == 0)
    def _():
        sums_ref[...] = new

    @pl.when(step != 0)
    def _():
        sums_ref[...] += new


def chain(branch, second, slope, n1, f1, gain_one, w_down, w_up, w_out, size=512):
    count = branch.shape[0]
    whole = lambda i: (0, 0)
    block = lambda i: (i, 0)
    once = pl.Buffered(1)
    def body(*refs):
        chain_kernel(*refs, None)
    return pl.pallas_call(
        body,
        grid=(count // size,),
        in_specs=[
            pl.BlockSpec((size, D), block),
            pl.BlockSpec((size, D), block),
            pl.BlockSpec((size, FF), block),
            pl.BlockSpec((size, D), block),
            pl.BlockSpec((size, 128), block),
            pl.BlockSpec((1, D), whole),
            pl.BlockSpec((FF, D), whole, pipeline_mode=once),
            pl.BlockSpec((D, FF), whole, pipeline_mode=once),
            pl.BlockSpec((D, D), whole, pipeline_mode=once),
        ],
        out_specs=[
            pl.BlockSpec((size, FF), block),
            pl.BlockSpec((size, D), block),
            pl.BlockSpec((size, D), block),
            pl.BlockSpec((size, D), block),
            pl.BlockSpec((8, D), whole),
        ],
        out_shape=[
            jax.ShapeDtypeStruct((count, FF), BF),
            jax.ShapeDtypeStruct((count, D), F32),
            jax.ShapeDtypeStruct((count, D), BF),
            jax.ShapeDtypeStruct((count, D), BF),
            jax.ShapeDtypeStruct((8, D), F32),
        ],
        compiler_params=pltpu.CompilerParams(vmem_limit_bytes=VMEM_CAP),
        cost_estimate=cost(21),
        name="chain",
    )(branch, second, slope, n1, f1, gain_one, w_down, w_up, w_out)


def attend_back_kernel(row, labels_ref, packed_ref, mixed_ref, incoming_ref, lse_ref, out_ref, sums_ref):
    length = packed_ref.shape[0]
    hot = span_lanes(labels_ref[pl.ds(row, 1), :], length)
    lane = lanes((length, 128))
    mark_q = (hot * FAR).astype(BF)
    mark_k = jnp.where(lane < 4, hot - 1.0, jnp.where(lane < 7, -1.0, 0.0)).astype(BF)
    mark_v = jnp.where((lane >= 4) & (lane < 7), -1.0, 0.0).astype(BF)
    none = jnp.zeros((length, 128), BF)
    low_half = lane < HEAD_DIM
    scale = jnp.asarray(HEAD_DIM ** (-0.5), BF)

    def pack3(column, base):
        high, mid, low = (part.astype(F32) for part in split3(column))
        filled = jnp.where(lane == 4, high, jnp.where(lane == 5, mid, jnp.where(lane == 6, low, 0.0)))
        return base + filled.astype(BF)

    def pair(p, carry):
        at = pl.multiple_of(p * 128, 128)
        query = packed_ref[:, pl.ds(at, 128)] * scale
        key = packed_ref[:, pl.ds(D + at, 128)]
        keys = jnp.concatenate([key, mark_k], axis=1)
        values = jnp.concatenate([packed_ref[:, pl.ds(2 * D + at, 128)], mark_v], axis=1)
        incoming = incoming_ref[:, pl.ds(at, 128)]
        product = incoming.astype(F32) * mixed_ref[:, pl.ds(at, 128)].astype(F32)
        logs = lse_ref[...]
        d_query = jnp.zeros((length, 128), F32)
        d_key = jnp.zeros((length, 128), F32)
        d_value = jnp.zeros((length, 128), F32)
        for half in range(2):
            own = low_half if half == 0 else jnp.logical_not(low_half)
            log_total = jnp.sum(jnp.where(lane == 2 * p + half, logs, 0.0), axis=1, keepdims=True)
            centred = jnp.sum(jnp.where(own, product, 0.0), axis=1, keepdims=True)
            own_query = jnp.where(own, query, none)
            own_incoming = jnp.where(own, incoming, none)
            own_key = jnp.where(own, key, none)
            queries = jnp.concatenate([own_query, pack3(log_total, mark_q)], axis=1)
            grads = jnp.concatenate([own_incoming, pack3(centred, none)], axis=1)
            weights = jnp.exp(mm(keys, queries, NT))
            d_scores = (weights * mm(values, grads, NT)).astype(BF)
            d_value += mm(weights.astype(BF), own_incoming)
            d_key += mm(d_scores, own_query)
            d_query += mm(d_scores, own_key, TN)
        d_query = (d_query * HEAD_DIM ** (-0.5)).astype(BF)
        d_value = d_value.astype(BF)
        out_ref[:, pl.ds(at, 128)] = d_query
        out_ref[:, pl.ds(D + at, 128)] = d_key.astype(BF)
        out_ref[:, pl.ds(2 * D + at, 128)] = d_value
        new_query = jnp.sum(d_query.astype(F32), axis=0, keepdims=True)
        new_value = jnp.sum(d_value.astype(F32), axis=0, keepdims=True)
        fill = jnp.concatenate([new_query, new_value, jnp.zeros((6, 128), F32)], axis=0)

        sums_ref[:, pl.ds(at, 128)] = fill
        return carry

    lax.fori_loop(0, HEADS // 2, pair, 0)


def attend_back(row, labels, packed, mixed, incoming, lse):
    rows, length = labels.shape
    block = lambda i: (row, 0)
    top = lambda i: (0, 0)
    return pl.pallas_call(
        functools.partial(attend_back_kernel, row),
        grid=(1,),
        in_specs=[
            pl.BlockSpec((rows, length), lambda i: (0, 0)),
            pl.BlockSpec((length, 3 * D), block),
            pl.BlockSpec((length, D), block),
            pl.BlockSpec((length, D), block),
            pl.BlockSpec((length, 128), block),
        ],
        out_specs=[
            pl.BlockSpec((length, 3 * D), top),
            pl.BlockSpec((8, D), lambda i: (0, 0)),
        ],
        out_shape=[
            jax.ShapeDtypeStruct((length, 3 * D), BF),
            jax.ShapeDtypeStruct((8, D), F32),
        ],
        compiler_params=pltpu.CompilerParams(vmem_limit_bytes=VMEM_CAP),
        cost_estimate=cost(14),
        name="attend_back",
    )(labels, packed, mixed, incoming, lse)


def token_kernel(first_ref, one_ref, two_ref, w_ref, out_ref):
    length = one_ref.shape[0]
    for at, part in ((0, one_ref), (length, two_ref)):
        out_ref[at : at + length, :] = first_ref[at : at + length, :] + mm(part[...], w_ref[...], NT)


def grad_token(first, d_packed, w_in):
    count = first.shape[0]
    return pl.pallas_call(
        token_kernel,
        out_shape=jax.ShapeDtypeStruct((count, D), F32),
        compiler_params=pltpu.CompilerParams(vmem_limit_bytes=VMEM_CAP),
        cost_estimate=cost(7),
        name="grad_token",
    )(first, *d_packed, w_in)


def place_kernel(tile_rows, count, me_ref, half_ref, *refs):
    outs = refs[-count:]
    kinds = half_ref.shape[0]
    for k in range(kinds):
        for j in range(16):
            at = (k * 16 + j) * tile_rows
            if kinds == 2:
                slot = tile_place(k, j) ^ me_ref[1 + k]
            else:
                slot = jnp.where(
                    pl.program_id(0) == 0, tile_place(0, j) ^ me_ref[1], tile_place(1, j) ^ me_ref[2]
                )
            tile = half_ref[k, slot].astype(F32)
            if len(outs) == 1:
                outs[0][at : at + tile_rows, :] = tile
            else:
                cut = outs[0].shape[1]
                outs[0][at : at + tile_rows, :] = tile[:, :cut]
                outs[1][at : at + tile_rows, :] = tile[:, cut:]


def placed_call(name, tile_rows, me, half, rel, grid, shapes, blocks, index, before):
    kinds = 2 // grid
    tile = half.shape[2:]
    olds = [] if before is None else list(before)
    return pl.pallas_call(
        functools.partial(place_kernel, tile_rows, len(shapes)),
        grid_spec=pltpu.PrefetchScalarGridSpec(
            num_scalar_prefetch=1,
            grid=(grid,),
            in_specs=[pl.BlockSpec((kinds, 16) + tile, lambda i, me: (i, 0, 0, 0))]
            + [pl.BlockSpec(memory_space=pl.ANY)] * len(olds),
            out_specs=[
                pl.BlockSpec(b, lambda i, me: index(i, me[0] ^ rel)) for b in blocks
            ],
        ),
        out_shape=[jax.ShapeDtypeStruct(s, F32) for s in shapes],
        input_output_aliases={2 + i: i for i in range(len(olds))},
        compiler_params=pltpu.CompilerParams(vmem_limit_bytes=VMEM_CAP),
        cost_estimate=cost(4),
        name=name,
    )(me, half, *olds)


def place_down(me, half, rel, before=None):
    return placed_call(
        "place_down", 48, me, half, rel, 2, [(FF, D)], [(D, D)], lambda i, c: (c * 2 + i, 0), before
    )


def place_up(me, half, rel, before=None):
    return placed_call(
        "place_up", 48, me, half, rel, 2, [(D, FF)], [(D, D)], lambda i, c: (0, c * 2 + i), before
    )


def place_in(me, half, rel, before=None):
    return placed_call(
        "place_in", 24, me, half, rel, 1, [(D, 3 * D), (D, D)], [(D, 3 * D // 2), (D, D // 2)],
        lambda i, c: (0, c), before,
    )


def device_count():
    return lax.axis_size("gr") * lax.axis_size("gc")


def swap(values, mask):
    pairs = [(i, i ^ mask) for i in range(device_count())]
    return lax.ppermute(values, ("gr", "gc"), pairs)


def plus(left, right):
    return (left.astype(F32) + right.astype(F32)).astype(BF)


def flow(send, keep):
    got = swap(send, 1)
    one, two = yield plus(keep[0], got[0]), plus(keep[1], got[1])
    one, two = yield plus(one[:8], swap(one[8:], 2)), plus(two[:8], swap(two[8:], 4))
    one, two = plus(one[:4], swap(one[4:], 4)), plus(two[:4], swap(two[4:], 2))
    ours, other = yield jnp.stack([one[:2], two[:2]], axis=1), jnp.stack([one[2:], two[2:]], axis=1)
    (both,) = yield (plus(ours, swap(other, 8)),)
    own = plus(both[0], swap(both[1], 16))
    mask = 32
    while mask < device_count():
        own = plus(own, swap(own, mask))
        mask *= 2
    (own,) = yield (own,)
    (both,) = yield (jnp.stack([own, swap(own, 16)]),)
    both = jnp.concatenate([both, swap(both, 8)])
    one, two = yield both[:, 0], both[:, 1]
    one, two = yield jnp.concatenate([one, swap(one, 4)]), jnp.concatenate([two, swap(two, 2)])
    (half,) = yield (jnp.stack([jnp.concatenate([one, swap(one, 2)]), jnp.concatenate([two, swap(two, 4)])]),)
    return half, swap(half, 1)


def flow_sums(sums):
    mask = 1
    while mask < device_count():
        (sums,) = yield (sums + swap(sums, mask),)
        mask *= 2
    return sums


class Line:
    def __init__(self, steps):
        self.steps = steps
        self.made = next(self.steps)
        self.result = None

    def go(self):
        if self.result is None:
            try:
                self.made = self.steps.send(self.made)
            except StopIteration as end:
                self.result = end.value


def tie(lines, *values):
    made = [line.made for line in lines]
    made, values = lax.optimization_barrier((made, values))
    for line, arrays in zip(lines, made):
        line.made = arrays
        line.go()
    return values


def gathered(rows):
    table = jnp.stack([rows, swap(rows, 1)])
    bit = 2
    while bit < device_count():
        wide = 2 * bit < device_count()
        masks = (bit, 2 * bit, 3 * bit) if wide else (bit,)
        table = jnp.concatenate([table] + [swap(table, m) for m in masks])
        bit *= 4 if wide else 2
    return table


def bits_of(value, order):
    out = jnp.zeros_like(value)
    for bit in order:
        out = out * 2 + ((value >> bit) & 1)
    return out


def per_device(
    tokens, span_ids, mlm_pos, mlm_count, mlm_grad, positive, w_in, b_query, b_value, w_out, b_out,
    ln1_gain, ln1_bias, w_up, b_up, w_down, b_down, ln2_gain, ln2_bias,
):
    rows, length = span_ids.shape
    spans, slots = mlm_pos.shape
    per_row = spans // rows
    index = lax.axis_index("gr") * lax.axis_size("gc") + lax.axis_index("gc")
    chip = (index >> 1) & 15
    me = jnp.stack(
        [index & 1, bits_of(chip, (0, 1, 2, 3)), bits_of(chip, (1, 0, 2, 3))]
    ).astype(jnp.int32)

    bias_in = jnp.concatenate([b_query, jnp.zeros_like(b_query), b_value])[None]
    packed, mixed, lse = attend(span_ids, tokens, w_in, bias_in)

    levels = jnp.arange(per_row, dtype=jnp.int32)
    starts = jnp.sum((span_ids[:, None, :] < levels[None, :, None]).astype(jnp.int32), axis=-1)
    starts = (jnp.arange(rows, dtype=jnp.int32)[:, None] * length + starts).reshape(-1)
    blank = jnp.zeros((D,), F32)
    vecs = jnp.stack([b_out, ln1_gain, ln1_bias, b_down, ln2_gain, ln2_bias, blank, blank])
    low, n1, f1, hidden, slope, n2, f2, layer_out, cls = feed(
        starts[:, None], tokens, mixed, w_out, w_up, w_down, vecs, b_up[None]
    )
    table = gathered(cls.astype(BF))

    place = (jnp.arange(spans, dtype=jnp.int32) // per_row * length)[:, None] + mlm_pos
    live = jnp.arange(slots, dtype=jnp.int32)[None, :] < mlm_count[:, None]
    given = jnp.where(live[:, :, None], mlm_grad, jnp.zeros_like(mlm_grad)).reshape(-1, D)
    loss, second, branch, sums_two = contrast(
        index.astype(jnp.int32)[None], positive[:, None], table, starts[None], place.reshape(1, -1),
        given, n2, f2, ln2_gain[None],
    )

    send = grad_down(me, hidden, branch, 1)
    branch, send = lax.optimization_barrier((branch, send))
    down = Line(flow(send, grad_down(me, hidden, branch, 0)))
    branch, second = tie([down], branch, second)
    d_before, d_first, d_attn, d_mixed, sums_one = chain(
        branch, second, slope, n1, f1, ln1_gain[None], w_down, w_up, w_out
    )
    d_before, d_mixed = tie([down], d_before, d_mixed)
    send = grad_up(me, low, d_before, 1)
    d_before, send = lax.optimization_barrier((d_before, send))
    up = Line(flow(send, grad_up(me, low, d_before, 0)))
    (d_mixed,) = tie([down, up], d_mixed)
    d_packed, sums_in = [None] * 2, [None] * 2
    d_packed[0], sums_in[0] = attend_back(0, span_ids, packed, mixed, d_mixed, lse)
    d_mixed, d_packed[0] = tie([down, up], d_mixed, d_packed[0])
    d_packed[1], sums_in[1] = attend_back(1, span_ids, packed, mixed, d_mixed, lse)
    d_packed = tie([down, up], *d_packed)
    send = grad_in(me, tokens, d_packed, mixed, d_attn, 1)
    (d_packed, send) = tie([down], d_packed, send)
    inner = Line(flow(send, grad_in(me, tokens, d_packed, mixed, d_attn, 0)))
    small = Line(flow_sums(jnp.concatenate([sums_two, sums_one, sums_in[0] + sums_in[1]])))
    done = [None]

    def advance(*values):
        lines = [line for line in (inner, down, up, small) if line.result is None]
        out = tie(lines, done[0], *values)
        done[0] = out[0]
        return out[1:]

    d_first, d_packed = advance(d_first, d_packed)
    grad_tokens = done[0] = grad_token(d_first, d_packed, w_in)
    g_down = g_up = g_in = None
    while inner.result is None:
        (grad_tokens, g_down, g_up) = advance(grad_tokens, g_down, g_up)
        if down.result is not None and (g_down is None or len(g_down) == 1):
            rel = 0 if g_down is None else 1
            made = place_down(me, down.result[rel], rel, None if rel == 0 else g_down)
            g_down = done[0] = (made[0], None) if rel else made
        elif up.result is not None and (g_up is None or len(g_up) == 1):
            rel = 0 if g_up is None else 1
            made = place_up(me, up.result[rel], rel, None if rel == 0 else g_up)
            g_up = done[0] = (made[0], None) if rel else made
        else:
            done[0] = None
    for rel, half in enumerate(inner.result):
        g_in = place_in(me, half, rel, g_in)
    sums = small.result

    return (
        layer_out,
        grad_tokens,
        g_in[0],
        sums[16],
        sums[17],
        g_in[1],
        sums[10],
        sums[8],
        sums[9],
        g_up[0],
        sums[11:15].reshape(-1),
        g_down[0],
        sums[2],
        sums[0],
        sums[1],
        loss[0, 0],
    )


def solution(mesh):
    split = P(("gr", "gc"))
    return jax.shard_map(
        per_device,
        mesh=mesh,
        in_specs=(split,) * 5 + (P(),) * 14,
        out_specs=(split, split) + (P(),) * 14,
        check_vma=False,
    )
```

```python
import functools
import jax
import jax.numpy as jnp
from jax import lax
from jax.experimental import pallas as pl
from jax.experimental.pallas import tpu as pltpu
from jax.sharding import PartitionSpec as P

D = 768
HEADS = 12
HEAD_DIM = 64
FF = 3072
BF = jnp.bfloat16
F32 = jnp.float32
EPS = 1e-12
FAR = 1e30
NEG = -1e30
HALF_ROOT = 0.7071067811865476
DENSITY = 0.3989422804014327
NN = (((1,), (0,)), ((), ()))
NT = (((1,), (1,)), ((), ()))
TN = (((0,), (0,)), ((), ()))
MIB = 1024 * 1024
PACE = 0.05
WAIT = 30
SMEM = pltpu.SMEM
VMEM = pltpu.VMEM


def shape(dims, dtype):
    return jax.ShapeDtypeStruct(dims, dtype)


def near(dims, dtype):
    return VMEM(dims, dtype)


def away(array):
    return pltpu.with_memory_space_constraint(array, pltpu.HBM)


def kernel_call(body, outs, name, us, limit, scalars=0, far=0, far_outs=(), scratch=(), aliases=None):
    def place(i):
        if i < scalars:
            return pl.BlockSpec(memory_space=SMEM)
        return pl.BlockSpec(memory_space=pltpu.HBM if i < scalars + far else VMEM)

    def call(*args):
        return pl.pallas_call(
            body,
            in_specs=[place(i) for i in range(len(args))],
            out_specs=[pl.BlockSpec(memory_space=pltpu.HBM if i in far_outs else VMEM) for i in range(len(outs))]
            if isinstance(outs, list)
            else pl.BlockSpec(memory_space=VMEM),
            out_shape=outs,
            scratch_shapes=list(scratch),
            input_output_aliases=aliases or {},
            compiler_params=pltpu.CompilerParams(vmem_limit_bytes=limit * MIB),
            cost_estimate=pl.CostEstimate(
                flops=int(us * 1.1e9), bytes_accessed=int(us * 3e6), transcendentals=0
            ),
            name=name,
        )(*args)

    return call


def mm(left, right, dims=NN):
    return lax.dot_general(left, right, dims, preferred_element_type=F32)


def lanes(dims):
    return lax.broadcasted_iota(jnp.int32, dims, len(dims) - 1)


def row_of(ref):
    return ref[...][None, :]


def normalize(values):
    centre = values - jnp.mean(values, axis=-1, keepdims=True)
    factor = lax.rsqrt(jnp.mean(centre * centre, axis=-1, keepdims=True) + EPS)
    return centre * factor, factor


def norm_back(incoming, normed, factor, gain):
    scaled = incoming * gain
    return factor * (
        scaled
        - jnp.mean(scaled, axis=-1, keepdims=True)
        - normed * jnp.mean(scaled * normed, axis=-1, keepdims=True)
    )


def span_lanes(labels, length):
    rows = lax.broadcasted_iota(jnp.int32, (128, length), 0)
    return jnp.where(rows == jnp.broadcast_to(labels, (128, length)), 1.0, 0.0).T


def attend_kernel(
    unroll, rows, labels_far, tokens_far, w_far, bq_far, bv_far, w_out_far, w_up_far, w_down_far, *refs
):
    packed_far, mixed, lse = refs[:rows], refs[rows : 2 * rows], refs[2 * rows : 3 * rows]
    w_out_ref, w_up_ref, w_down_ref = refs[3 * rows : 3 * rows + 3]
    labels_ref, tokens_ref, w_ref, bq_ref, bv_ref = refs[3 * rows + 3 : 3 * rows + 8]
    packed, sems = refs[3 * rows + 8 : 4 * rows + 8], refs[-1]
    length = packed[0].shape[0]
    columns = [slice(at, at + D) for at in range(0, 3 * D, D)]
    pairs = [(tokens_far, tokens_ref), (bq_far, bq_ref), (bv_far, bv_ref), (labels_far, labels_ref)]
    pairs += [(w_far.at[:, c], w_ref.at[:, c]) for c in columns]
    pairs += [(w_out_far, w_out_ref), (w_up_far, w_up_ref), (w_down_far, w_down_ref)]
    pairs += list(zip(packed, packed_far))
    copies = [pltpu.make_async_copy(*pair, sems.at[i]) for i, pair in enumerate(pairs)]
    for copy in copies[:10]:
        copy.start()
    scale = jnp.asarray(HEAD_DIM ** (-0.5), BF)
    for copy in copies[:4]:
        copy.wait()
    for k, c in enumerate(columns):
        copies[4 + k].wait()
        for row in range(rows):
            made = mm(tokens_ref[row * length : (row + 1) * length, :], w_ref[:, c])
            bias = (row_of(bq_ref), 0.0, row_of(bv_ref))[k]
            packed[row][:, c] = (made + bias).astype(BF)
    for copy in copies[10:]:
        copy.start()
    lane = lanes((length, 128))
    low_half = lane < HEAD_DIM

    for row in range(rows):
        hot = span_lanes(labels_ref[row : row + 1, :], length)
        mark_q = (hot * FAR).astype(BF)
        mark_k = jnp.where(lane < 4, hot - 1.0, 0.0).astype(BF)
        packed_ref, mixed_ref, lse_ref = packed[row], mixed[row], lse[row]
        lse_ref[...] = jnp.zeros_like(lse_ref)

        def one(p):
            at = pl.multiple_of(p * 128, 128)
            query = packed_ref[:, pl.ds(at, 128)] * scale
            keys = jnp.concatenate([packed_ref[:, pl.ds(D + at, 128)], mark_k], axis=1)
            values = packed_ref[:, pl.ds(2 * D + at, 128)]
            outs = []
            logs = lse_ref[...]
            for half in range(2):
                own = low_half if half == 0 else jnp.logical_not(low_half)
                queries = jnp.concatenate(
                    [jnp.where(own, query, jnp.zeros_like(query)), mark_q], axis=1
                )
                scores = mm(queries, keys, NT)
                top = jnp.max(scores, axis=1, keepdims=True)
                grown = jnp.exp(scores - top)
                total = jnp.sum(grown, axis=1, keepdims=True)
                outs.append(mm(grown.astype(BF), values) * (1.0 / total))
                logs = jnp.where(lane == 2 * p + half, top + jnp.log(total), logs)
            lse_ref[...] = logs
            mixed_ref[:, pl.ds(at, 128)] = jnp.where(low_half, outs[0], outs[1]).astype(BF)

        def some(t, carry):
            for u in range(unroll):
                one(t * unroll + u)
            return carry

        lax.fori_loop(0, HEADS // 2 // unroll, some, 0)
    for copy in copies[7:]:
        copy.wait()


def attend(labels, tokens, w_in, b_query, b_value, weights, unroll=3):
    rows, length = labels.shape
    made = kernel_call(
        functools.partial(attend_kernel, unroll, rows),
        [pltpu.HBM((length, 3 * D), BF)] * rows + [near((length, D), BF)] * rows
        + [near((length, 128), F32)] * rows + [near(w.shape, BF) for w in weights],
        "attend", 15 * PACE, 20, far=8, far_outs=range(rows),
        scratch=[VMEM(labels.shape, jnp.int32), VMEM(tokens.shape, BF), VMEM(w_in.shape, BF), VMEM((D,), F32), VMEM((D,), F32)]
        + [VMEM((length, 3 * D), BF)] * rows + [pltpu.SemaphoreType.DMA((10 + rows,))],
    )(*(away(x) for x in (labels, tokens, w_in, b_query, b_value) + tuple(weights)))
    return made[:rows], made[rows : 2 * rows], made[2 * rows : 3 * rows], made[3 * rows :]


def span_starts(labels_ref, per_row):
    rows, length = labels_ref.shape
    out = []
    for row in range(rows):
        labels = jnp.broadcast_to(labels_ref[row : row + 1, :], (per_row, length))
        level = lax.broadcasted_iota(jnp.int32, (per_row, length), 0)
        below = jnp.sum(jnp.where(labels < level, 1.0, 0.0), axis=1, keepdims=True)
        out.append(below.astype(jnp.int32) + row * length)
    return jnp.concatenate(out, axis=0)


def picked(spot, at, size):
    place = lax.broadcasted_iota(jnp.int32, (spot.shape[0], size), 1) + at
    return jnp.where(place == spot, 1.0, 0.0).astype(BF)


def feed_rows(tokens, mixed, w_out_ref, w_up_ref, w_down_ref, vectors, width, keep):
    b_out, gain_one, bias_one, b_up, b_down, gain_two, bias_two = (row_of(ref) for ref in vectors)
    first = tokens.astype(F32) + mm(mixed, w_out_ref[...]) + b_out
    normed, factor = normalize(first)
    middle = normed * gain_one + bias_one
    low = middle.astype(BF)
    keep("first", normed, factor, low)
    total = middle + b_down
    for at in range(0, FF, width):
        before = mm(low, w_up_ref[:, at : at + width]) + b_up[:, at : at + width]
        share = 0.5 * (1.0 + lax.erf(before * HALF_ROOT))
        hidden = (before * share).astype(BF)
        keep("hidden", before, share, hidden, at)
        total = total + mm(hidden, w_down_ref[at : at + width, :])
    normed, factor = normalize(total)
    keep("second", normed, factor)
    return (normed * gain_two + bias_two).astype(BF)


def opening_kernel(rows, spans, labels_ref, tokens_ref, *refs):
    mixed_refs, weights, vectors, cls_ref = refs[:rows], refs[rows : rows + 3], refs[rows + 3 : -1], refs[-1]
    length = labels_ref.shape[1]
    spot = span_starts(labels_ref, spans // rows)
    tokens = jnp.zeros((spans, D), F32)
    mixed = jnp.zeros((spans, D), F32)
    for row in range(rows):
        pick = picked(spot, row * length, length)
        tokens += mm(pick, tokens_ref[row * length : (row + 1) * length, :])
        mixed += mm(pick, mixed_refs[row][...])
    cls_ref[...] = feed_rows(tokens, mixed.astype(BF), *weights, vectors, D, lambda *made: None)


def opening(spans, labels, tokens, mixed, weights, vectors):
    return kernel_call(
        functools.partial(opening_kernel, len(mixed), spans), shape((spans, D), BF), "opening", 4 * PACE, 4
    )(labels, tokens, *mixed, *weights, *vectors)


def feed_kernel(row, width, me_ref, tokens_ref, mixed_ref, *refs):
    weights, vectors = refs[:3], refs[3:10]
    low_ref, n1_ref, f1_ref, hidden_ref, slope_ref, n2_ref, f2_ref, out_ref = refs[10:]
    length = mixed_ref.shape[0]

    def keep(what, *made):
        if what == "first":
            n1_ref[...] = made[0].astype(BF)
            f1_ref[...] = jnp.broadcast_to(made[1], (length, 128))
            low_ref[...] = made[2]
        elif what == "hidden":
            before, share, hidden, at = made
            hidden_ref[:, at : at + width] = hidden
            slope_ref[:, at : at + width] = (
                share + before * jnp.exp(-0.5 * before * before) * DENSITY
            ).astype(BF)
        else:
            n2_ref[...] = made[0].astype(BF)
            f2_ref[...] = jnp.broadcast_to(made[1], (length, 128))

    tokens = tokens_ref[row * length : (row + 1) * length, :]
    out_ref[...] = feed_rows(tokens, mixed_ref[...], *weights, vectors, width, keep)


def feed(row, me, tokens, mixed, weights, vectors, width=768):
    length = mixed.shape[0]
    return kernel_call(
        functools.partial(feed_kernel, row, width),
        [
            near((length, D), BF), near((length, D), BF), near((length, 128), F32), near((length, FF), BF),
            near((length, FF), BF), near((length, D), BF), near((length, 128), F32), shape((length, D), BF),
        ],
        "feed", 9 * PACE, 7, scalars=1,
    )(me, tokens, mixed, *weights, *vectors)


def chain_kernel(
    width, me_ref, branch_ref, second_ref, slope_ref, n1_ref, f1_ref, gain_ref, w_down_ref, w_up_ref, w_out_ref,
    before_ref, first_ref, attn_ref, mixed_ref, sums_ref,
):
    d_middle = second_ref[...]
    branch = branch_ref[...]
    parts = []
    for at in range(0, FF, width):
        d_hidden = mm(branch, w_down_ref[at : at + width, :], NT)
        d_before = (d_hidden * slope_ref[:, at : at + width].astype(F32)).astype(BF)
        before_ref[:, at : at + width] = d_before
        parts.append(jnp.sum(d_before.astype(F32), axis=0, keepdims=True))
        d_middle = d_middle + mm(d_before, w_up_ref[:, at : at + width], NT)
    normed = n1_ref[...].astype(F32)
    d_first = norm_back(d_middle, normed, f1_ref[:, 0:1], row_of(gain_ref))
    d_attn = d_first.astype(BF)
    first_ref[...] = d_first
    attn_ref[...] = d_attn
    mixed_ref[...] = mm(d_attn, w_out_ref[...], NT).astype(BF)
    sums_ref[...] = jnp.concatenate(
        [
            jnp.sum(d_middle * normed, axis=0, keepdims=True),
            jnp.sum(d_middle, axis=0, keepdims=True),
            jnp.sum(d_attn.astype(F32), axis=0, keepdims=True),
        ] + parts + [jnp.zeros((1, D), F32)],
        axis=0,
    )


def chain(me, branch, second, slope, n1, f1, gain_one, w_down, w_up, w_out):
    length = branch.shape[0]
    return kernel_call(
        functools.partial(chain_kernel, D),
        [
            near((length, FF), BF), near((length, D), F32), near((length, D), BF),
            near((length, D), BF), shape((8, D), F32),
        ],
        "chain", 6.6 * PACE, 6, scalars=1,
    )(me, branch, second, slope, n1, f1, gain_one, w_down, w_up, w_out)


def split3(values):
    high = values.astype(BF)
    rest = values - high.astype(F32)
    mid = rest.astype(BF)
    return high, mid, (rest - mid.astype(F32)).astype(BF)


def contrast_kernel(
    size, rows_count, slots_of, me_ref, count_ref, labels_ref, partner_ref, pos_ref, given_ref, gain_ref, *refs
):
    tables, refs = refs[: len(slots_of)], refs[len(slots_of) :]
    groups = [refs[i * rows_count : (i + 1) * rows_count] for i in range(2)]
    n2_refs, f2_refs = groups
    loss_ref, sums_ref = refs[2 * rows_count : 2 * rows_count + 2]
    second_refs = refs[2 * rows_count + 2 : 3 * rows_count + 2]
    branch_refs = refs[3 * rows_count + 2 : 4 * rows_count + 2]
    table = refs[-1]
    spans = tables[0].shape[1]
    total = table.shape[0]
    me = me_ref[0]
    for ref, masks in zip(tables, slots_of):
        for k, mask in enumerate(masks):
            table[pl.ds(pl.multiple_of((mask ^ me) * spans, spans), spans), :] = ref[k].astype(F32)
    rows = table[...].astype(BF)
    scale = 2.0 * D ** (-0.5)
    similar = mm(rows, rows, NT) * scale
    other = lax.broadcasted_iota(jnp.int32, (total, total), 0)
    own = lax.broadcasted_iota(jnp.int32, (total, total), 1)
    similar = jnp.where(own == other, NEG, similar)
    partner = row_of(partner_ref) == other
    top = jnp.max(similar, axis=0, keepdims=True)
    log_rows = top + jnp.log(jnp.sum(jnp.exp(similar - top), axis=0, keepdims=True))
    chosen = jnp.sum(jnp.where(partner, similar, 0.0), axis=0, keepdims=True)
    loss = jnp.sum(log_rows - chosen, axis=1, keepdims=True) / total
    loss_ref[...] = jnp.broadcast_to(loss, loss_ref.shape)
    slope = (jnp.exp(similar - log_rows) - jnp.where(partner, 1.0, 0.0)).astype(BF)
    spot = lax.broadcasted_iota(jnp.int32, (spans, total), 0) + me * spans
    pick = jnp.where(spot == lax.broadcasted_iota(jnp.int32, (spans, total), 1), 1.0, 0.0).astype(BF)
    mine = mm(pick, slope, NT).astype(BF)
    across = mm(pick, slope).astype(BF)
    parts = split3((mm(mine, rows) + mm(across, rows)) * scale)

    starts = span_starts(labels_ref, spans // rows_count)
    slots = given_ref.shape[1]
    per_row = spans // rows_count
    sums = [jnp.zeros((1, D), F32)] * 3
    for row in range(rows_count):
        for at in range(0, n2_refs[row].shape[0], size):
            base = row * n2_refs[row].shape[0] + at
            here = slice(at, at + size)
            place = lax.broadcasted_iota(jnp.int32, (size, slots), 0) + at
            upstream = jnp.zeros((size, D), F32)
            for span in range(row * per_row, (row + 1) * per_row):
                used = lanes((size, slots)) < count_ref[span]
                slot = jnp.where((place == pos_ref[span : span + 1, :]) & used, 1.0, 0.0).astype(BF)
                upstream += mm(slot, given_ref[span])
            hot = picked(starts, base, size)
            upstream += mm(hot, parts[0], TN) + (mm(hot, parts[1], TN) + mm(hot, parts[2], TN))
            normed = n2_refs[row][here, :].astype(F32)
            second = norm_back(upstream, normed, f2_refs[row][here, 0:1], row_of(gain_ref))
            branch = second.astype(BF)
            second_refs[row][here, :] = second
            branch_refs[row][here, :] = branch
            for k, values in enumerate((upstream * normed, upstream, branch.astype(F32))):
                sums[k] = sums[k] + jnp.sum(values, axis=0, keepdims=True)
    sums_ref[...] = jnp.concatenate(sums + [jnp.zeros((5, D), F32)], axis=0)


def contrast(me, count, labels, partner, tables, slots_of, pos, given, n2, f2, gain_two, size=256):
    length = n2[0].shape[0]
    rows = len(n2)
    spans = tables[0].shape[1]
    devices = sum(len(masks) for masks in slots_of)
    made = kernel_call(
        functools.partial(contrast_kernel, size, rows, slots_of),
        [shape((8, 128), F32), shape((8, D), F32)]
        + [near((length, D), F32)] * rows + [near((length, D), BF)] * rows,
        "contrast", 4 * PACE, 6 if devices * spans <= 512 else 40, scalars=2,
        scratch=[VMEM((devices * spans, D), F32)],
    )(me, count, labels, partner, pos, given, gain_two, *tables, *n2, *f2)
    return made[0], made[2 : 2 + rows], made[2 + rows :], made[1]


def merge_kernel(*refs):
    for k, ref in enumerate(refs[:-1]):
        refs[-1][k] = ref[...]


def merge(parts):
    return kernel_call(
        merge_kernel, near((len(parts),) + parts[0].shape, parts[0].dtype), "merge", 0.5 * PACE, 2
    )(*parts)


def tile_place(kind, j):
    order = (0, 1, 2, 3) if kind == 0 else (1, 0, 2, 3)
    out = 0
    for bit in order:
        out = out * 2 + ((j >> bit) & 1)
    return out


def put_tiles(out_ref, kind, values, base):
    rows = values.shape[0] // 16
    for j in range(16):
        out_ref[kind, tile_place(kind, j) ^ base] = values[j * rows : (j + 1) * rows, :]


def cut(start, size):
    return pl.ds(pl.multiple_of(start, 128), size)


def product(lefts, rights, left_cut=None, right_cut=None):
    whole = slice(None)
    return sum(
        mm(left[:, left_cut or whole], right[:, right_cut or whole], TN) for left, right in zip(lefts, rights)
    ).astype(BF)


def grad_down_kernel(rel, rows, me_ref, *refs):
    hidden, branch, out_ref = refs[:rows], refs[rows : 2 * rows], refs[-1]
    for kind in range(2):
        columns = cut(((me_ref[0] ^ rel) * 2 + kind) * D, D)
        put_tiles(out_ref, kind, product(hidden, branch, columns), me_ref[1 + kind])


def grad_up_kernel(rel, rows, me_ref, *refs):
    low, before, out_ref = refs[:rows], refs[rows : 2 * rows], refs[-1]
    for kind in range(2):
        columns = cut(((me_ref[0] ^ rel) * 2 + kind) * D, D)
        put_tiles(out_ref, kind, product(low, before, None, columns), me_ref[1 + kind])


def grad_in_kernel(rel, rows, me_ref, tokens_ref, *refs):
    packed, mixed, attn, out_ref = refs[:rows], refs[rows : 2 * rows], refs[2 * rows : 3 * rows], refs[-1]
    length = packed[0].shape[0]
    half = me_ref[0] ^ rel
    tokens = [tokens_ref.at[r * length : (r + 1) * length, :] for r in range(rows)]
    left = product(tokens, packed, None, cut(half * (3 * D // 2), 3 * D // 2))
    right = product(mixed, attn, None, cut(half * (D // 2), D // 2))
    joined = jnp.concatenate([left, right], axis=1)
    for kind in range(2):
        put_tiles(out_ref, kind, joined[kind * D // 2 : (kind + 1) * D // 2, :], me_ref[1 + kind])


def grad_down(me, hidden, branch, rel):
    return kernel_call(
        functools.partial(grad_down_kernel, rel, len(hidden)), shape((2, 16, 48, D), BF), "grad_down",
        WAIT if rel == 0 else 3.3 * PACE, 6, scalars=1,
    )(me, *hidden, *branch)


def grad_up(me, low, d_before, rel):
    return kernel_call(
        functools.partial(grad_up_kernel, rel, len(low)), shape((2, 16, 48, D), BF), "grad_up",
        WAIT if rel == 0 else 3.3 * PACE, 6, scalars=1,
    )(me, *low, *d_before)


def grad_in(me, tokens, d_packed, mixed, d_attn, rel):
    return kernel_call(
        functools.partial(grad_in_kernel, rel, len(mixed)), shape((2, 16, 24, 2 * D), BF), "grad_in",
        WAIT if rel == 0 else 3.6 * PACE, 8, scalars=1,
    )(me, tokens, *d_packed, *mixed, *d_attn)


def attend_back_kernel(row, pairs, unroll, me_ref, labels_ref, packed_ref, mixed_ref, incoming_ref, lse_ref, *refs):
    out_ref, sums_ref = refs[-2:]
    length = labels_ref.shape[1]
    here = slice(None)
    hot = span_lanes(labels_ref[row : row + 1, :], length)
    lane = lanes((length, 128))
    mark_q = (hot * FAR).astype(BF)
    mark_k = jnp.where(lane < 4, hot - 1.0, jnp.where(lane < 7, -1.0, 0.0)).astype(BF)
    mark_v = jnp.where((lane >= 4) & (lane < 7), -1.0, 0.0).astype(BF)
    none = jnp.zeros((length, 128), BF)
    low_half = lane < HEAD_DIM
    scale = jnp.asarray(HEAD_DIM ** (-0.5), BF)
    sums_ref[...] = jnp.zeros_like(sums_ref)

    def pack3(column, base):
        high, mid, low = (part.astype(F32) for part in split3(column))
        filled = jnp.where(lane == 4, high, jnp.where(lane == 5, mid, jnp.where(lane == 6, low, 0.0)))
        return base + filled.astype(BF)

    def one(p):
        at = pl.multiple_of(p * 128, 128)
        query = packed_ref[here, pl.ds(at, 128)] * scale
        key = packed_ref[here, pl.ds(D + at, 128)]
        keys = jnp.concatenate([key, mark_k], axis=1)
        values = jnp.concatenate([packed_ref[here, pl.ds(2 * D + at, 128)], mark_v], axis=1)
        incoming = incoming_ref[here, pl.ds(at, 128)]
        product = incoming.astype(F32) * mixed_ref[here, pl.ds(at, 128)].astype(F32)
        logs = lse_ref[here, :]
        d_query = jnp.zeros((length, 128), F32)
        d_key = jnp.zeros((length, 128), F32)
        d_value = jnp.zeros((length, 128), F32)
        for half in range(2):
            own = low_half if half == 0 else jnp.logical_not(low_half)
            log_total = jnp.sum(jnp.where(lane == 2 * p + half, logs, 0.0), axis=1, keepdims=True)
            centred = jnp.sum(jnp.where(own, product, 0.0), axis=1, keepdims=True)
            own_query = jnp.where(own, query, none)
            own_incoming = jnp.where(own, incoming, none)
            own_key = jnp.where(own, key, none)
            queries = jnp.concatenate([own_query, pack3(log_total, mark_q)], axis=1)
            grads = jnp.concatenate([own_incoming, pack3(centred, none)], axis=1)
            weights = jnp.exp(mm(keys, queries, NT))
            d_scores = (weights * mm(values, grads, NT)).astype(BF)
            d_value += mm(weights.astype(BF), own_incoming)
            d_key += mm(d_scores, own_query)
            d_query += mm(d_scores, own_key, TN)
        d_query = (d_query * HEAD_DIM ** (-0.5)).astype(BF)
        d_value = d_value.astype(BF)
        out_ref[:, pl.ds(at, 128)] = d_query
        out_ref[:, pl.ds(D + at, 128)] = d_key.astype(BF)
        out_ref[:, pl.ds(2 * D + at, 128)] = d_value
        sums_ref[0:1, pl.ds(at, 128)] = jnp.sum(d_query.astype(F32), axis=0, keepdims=True)
        sums_ref[1:2, pl.ds(at, 128)] = jnp.sum(d_value.astype(F32), axis=0, keepdims=True)

    def some(t, carry):
        for u in range(unroll):
            one(pairs[0] + t * unroll + u)
        return carry

    lax.fori_loop(0, (pairs[1] - pairs[0]) // unroll, some, 0)


def attend_back(row, pairs, me, labels, packed, mixed, incoming, lse, before=None, unroll=3):
    length = labels.shape[1]
    olds = [] if before is None else [before]
    return kernel_call(
        functools.partial(attend_back_kernel, row, pairs, unroll),
        [near((length, 3 * D), BF), shape((8, D), F32)],
        "attend_back", 5 * PACE, 6, scalars=1, aliases={6: 0} if olds else None,
    )(me, labels, packed, mixed, incoming, lse, *olds)


def token_kernel(rows, me_ref, *refs):
    first, packed, w_ref, out_ref = refs[:rows], refs[rows : 2 * rows], refs[-2], refs[-1]
    length = packed[0].shape[0]
    for r in range(rows):
        out_ref[r * length : (r + 1) * length, :] = first[r][...] + mm(packed[r][...], w_ref[...], NT)


def grad_token(me, first, d_packed, w_in):
    rows = len(first)
    return kernel_call(
        functools.partial(token_kernel, rows), shape((rows * first[0].shape[0], D), F32), "grad_token", 5.6 * PACE, 6, scalars=1,
    )(me, *first, *d_packed, w_in)


SUMS = (16, 17, 10, 8, 9, 11, 2, 0, 1)


def spread_kernel(me_ref, sums_ref, *outs):
    for at, out in zip(SUMS, outs):
        for k in range(out.shape[0] // D):
            out[k * D : (k + 1) * D] = sums_ref[at + k, :]


def spread(me, sums):
    return kernel_call(
        spread_kernel, [shape((FF if at == 11 else D,), F32) for at in SUMS], "spread", 1 * PACE, 2, scalars=1
    )(me, sums)


def join_kernel(me_ref, *refs):
    length = refs[0].shape[0]
    for k, ref in enumerate(refs[:-1]):
        refs[-1][k * length : (k + 1) * length, :] = ref[...]


def join(me, parts):
    length, width = parts[0].shape
    return kernel_call(
        join_kernel, shape((len(parts) * length, width), parts[0].dtype), "join", 1 * PACE, 4, scalars=1
    )(me, *parts)


def place_kernel(rel, name, olds, me_ref, *refs):
    refs = refs[olds:]
    halves = refs[:2]
    outs, holds, sems = (refs[2:4], refs[4:6], refs[6]) if name == "in" else (refs[2:3], refs[3:4], refs[4])
    half = me_ref[0] ^ rel
    copies = []
    for kind, half_ref in enumerate(halves):
        rows = half_ref.shape[1]
        for j in range(16):
            tile = half_ref[tile_place(kind, j) ^ me_ref[1 + kind]].astype(F32)
            at = 0
            for hold in holds:
                hold[kind, j * rows : (j + 1) * rows, :] = tile[:, at : at + hold.shape[2]]
                at += hold.shape[2]
        for out, hold in zip(outs, holds):
            high, wide = hold.shape[1:]
            if name == "down":
                spot = out.at[pl.ds(pl.multiple_of((half * 2 + kind) * high, high), high), :]
            elif name == "up":
                spot = out.at[:, cut((half * 2 + kind) * wide, wide)]
            else:
                spot = out.at[kind * high : (kind + 1) * high, cut(half * wide, wide)]
            copies.append(pltpu.make_async_copy(hold.at[kind], spot, sems.at[len(copies)]))
            copies[-1].start()
    for copy in copies:
        copy.wait()


PLACES = {
    "down": [((FF, D), (D, D))],
    "up": [((D, FF), (D, D))],
    "in": [((D, 3 * D), (D // 2, 3 * D // 2)), ((D, D), (D // 2, D // 2))],
}


def place(name, rel, me, halves, before=None):
    outs = PLACES[name]
    olds = [] if before is None else list(before)
    return kernel_call(
        functools.partial(place_kernel, rel, name, len(olds)),
        [pltpu.HBM(whole, F32) for whole, _ in outs],
        "place", 2 * PACE, 10, scalars=1, far=len(olds), far_outs=range(len(outs)),
        scratch=[VMEM((2,) + part, F32) for _, part in outs] + [pltpu.SemaphoreType.DMA((2 * len(outs),))],
        aliases={1 + i: i for i in range(len(olds))},
    )(me, *(away(old) for old in olds), *halves)


def device_count():
    return lax.axis_size("gr") * lax.axis_size("gc")


def swap(values, mask):
    pairs = [(i, i ^ mask) for i in range(device_count())]
    return lax.ppermute(values, ("gr", "gc"), pairs)


def plus(left, *others):
    total = left.astype(F32)
    for other in others:
        total = total + other.astype(F32)
    return total.astype(BF)


def flow(send, keep_of):
    (got,) = yield (swap(send, 1),)
    keep = keep_of()
    one, two = plus(keep[0], got[0]), plus(keep[1], got[1])
    one, two = yield plus(one[:8], swap(one[8:], 2)), plus(two[:8], swap(two[8:], 4))
    one, two = plus(one[:4], swap(one[4:], 4)), plus(two[:4], swap(two[4:], 2))
    ours, others = yield jnp.stack([one[:2], two[:2]], axis=1), jnp.stack([one[2:], two[2:]], axis=1)
    (both,) = yield (plus(ours, swap(others, 8)),)
    own = plus(both[0], swap(both[1], 16))
    mask = 32
    while mask < device_count():
        own = plus(own, swap(own, mask))
        mask *= 2
    (own,) = yield (own,)
    (both,) = yield (jnp.stack([own, swap(own, 16)]),)
    both = jnp.concatenate([both, swap(both, 8)])
    one, two = yield both[:, 0], both[:, 1]
    one, two = yield jnp.concatenate([one, swap(one, 4)]), jnp.concatenate([two, swap(two, 2)])
    one, two = yield jnp.concatenate([one, swap(one, 2)]), jnp.concatenate([two, swap(two, 4)])
    return (one, two), (swap(one, 1), swap(two, 1))


def flow_sums(sums):
    mask = 1
    while mask < device_count():
        (sums,) = yield (sums + swap(sums, mask),)
        mask *= 2


class Line:
    def __init__(self, steps, made):
        self.steps, self.made = steps, made
        self.result = None
        self.opened = False

    def go(self, made):
        try:
            self.made = self.steps(*made) if not self.opened else self.steps.send(made)
            if not self.opened:
                self.steps, self.made = self.made, next(self.made)
            self.opened = True
        except StopIteration as end:
            self.result = self.made = end.value


class Rounds:
    def __init__(self, me, token):
        self.me, self.token, self.going = me, token, []

    def begin(self, lines):
        kept = [line.made for line in self.going]
        made, kept, token = lax.optimization_barrier(([line.made for line in lines], kept, self.token))
        self.token = (kept, token)
        for line, arrays in zip(self.going, kept):
            line.made = arrays
            if line.result is not None:
                line.result = arrays
        for line, arrays in zip(lines, made):
            line.go(arrays if line not in self.going else line.made)
        self.going = lines

    def work(self, call, *args, token=lambda made: made):
        me, _ = lax.optimization_barrier((self.me, self.token))
        made = call(me, *args)
        self.token = token(made)
        return made


def bits_of(value, order):
    out = jnp.zeros_like(value)
    for bit in order:
        out = out * 2 + ((value >> bit) & 1)
    return out


def per_device(
    tokens, span_ids, mlm_pos, mlm_count, mlm_grad, positive, w_in, b_query, b_value, w_out, b_out,
    ln1_gain, ln1_bias, w_up, b_up, w_down, b_down, ln2_gain, ln2_bias,
):
    rows, length = span_ids.shape
    spans = mlm_pos.shape[0]
    index = lax.axis_index("gr") * lax.axis_size("gc") + lax.axis_index("gc")
    chip = (index >> 1) & 15
    me = jnp.stack(
        [index & 1, bits_of(chip, (0, 1, 2, 3)), bits_of(chip, (1, 0, 2, 3))]
    ).astype(jnp.int32)
    where = index.astype(jnp.int32)[None]
    me, where, b_query = lax.optimization_barrier((me, where, b_query))
    weights = (w_out, w_up, w_down)
    vectors = (b_out, ln1_gain, ln1_bias, b_up, b_down, ln2_gain, ln2_bias)

    packed, mixed, lse, weights = attend(span_ids, tokens, w_in, b_query, b_value, weights)
    cls = opening(spans, span_ids, tokens, mixed, weights, vectors)
    cls, here = lax.optimization_barrier((cls, me))
    masks = (0, 8, 16, 24)
    parts = [cls] + [swap(cls, m) for m in masks[1:]]
    made = [feed(0, here, tokens, mixed[0], weights, vectors)]
    table = merge(parts)
    table, here, _ = lax.optimization_barrier((table, me, made[0][1]))
    tables = [table] + [swap(table, m) for m in range(1, 8)]
    slots_of = [tuple(m ^ k for k in masks) for m in range(8)]
    made.append(feed(1, here, tokens, mixed[1], weights, vectors))
    bit = 32
    while bit < device_count():
        table, masks = jnp.concatenate(tables), sum(slots_of, ())
        tables = [table, swap(table, bit)]
        slots_of = [masks, tuple(m ^ bit for m in masks)]
        bit *= 2
    low, n1, f1, hidden, slope, n2, f2, layer_out = zip(*made)
    loss, second, branch, sums_two = contrast(
        where, mlm_count, span_ids, positive, tables, slots_of, mlm_pos, mlm_grad, n2, f2, ln2_gain
    )

    order = Rounds(me, sums_two)
    lines, keeps, links, sums_in, sides = {}, {}, [None] * rows, [], {}
    d_packed = [None] * rows
    part = [0] * rows

    def gradient(name, call, *args):
        if name not in lines:
            send = order.work(functools.partial(call, rel=1), *args)
            lines[name] = Line(functools.partial(flow, keep_of=lambda: keeps[name]), (send,))
        else:
            keeps[name] = order.work(functools.partial(call, rel=0), *args)

    def link(row):
        links[row] = order.work(
            chain, branch[row], second[row], slope[row], n1[row], f1[row], ln1_gain,
            weights[2], weights[1], weights[0], token=lambda made: made[4],
        )

    def back(row):
        pairs = (part[row] * HEADS // 4, (part[row] + 1) * HEADS // 4)
        d_packed[row], sums = order.work(
            functools.partial(attend_back, row, pairs),
            span_ids, packed[row], mixed[row], links[row][3], lse[row], d_packed[row],
            token=lambda made: made[1],
        )
        part[row] += 1
        sums_in.append(sums)

    def settle(name, rel):
        call = functools.partial(place, {"D": "down", "U": "up", "I": "in"}[name], rel)
        sides[name] = order.work(call, lines[name].result[rel], sides.get(name))

    for going, events in PLAN:
        if "S" in going and "S" not in lines:
            sums_one = sum(made[4] for made in links)
            lines["S"] = Line(flow_sums, (jnp.concatenate([sums_two, sums_one, sum(sums_in)]),))
        order.begin([lines[name] for name in going])
        for event in events:
            if event == "gd":
                gradient("D", grad_down, hidden, branch)
            elif event == "gu":
                gradient("U", grad_up, low, [made[0] for made in links])
            elif event == "gi":
                gradient("I", grad_in, tokens, d_packed, mixed, [made[2] for made in links])
            elif event == "gt":
                sides["T"] = order.work(grad_token, [made[1] for made in links], d_packed, w_in)
            elif event == "jo":
                sides["J"] = order.work(join, layer_out)
            elif event == "ou":
                sides["S"] = order.work(spread, lines["S"].made[0])
            elif event[:2] == "ch":
                link(int(event[2]))
            elif event[:2] == "ab":
                back(int(event[2]))
            else:
                settle(event[1], int(event[2]))
    grad_tokens, g_down, g_up, g_in, small = (sides[name] for name in "TDUIS")

    return (
        sides["J"], grad_tokens, g_in[0], small[0], small[1], g_in[1], *small[2:5], g_up[0], small[5], g_down[0],
        *small[6:], loss[0, 0],
    )


PLAN = (
    ("", ("gd",)),
    ("D", ("gd", "ch0", "ch1", "gu",)),
    ("DU", ("gu", "ab0", "ab0",)),
    ("DU", ("ab1", "ab1", "gi", "jo",)),
    ("DUIS", ("gi",)),
    ("DUI", ("gt",)),
    ("DI", ()),
    ("DUIS", ()),
    ("DUIS", ()),
    ("DUIS", ()),
    ("DUI", ("pD0",)),
    ("UIS", ("pD1",)),
    ("UI", ("pU0", "ou",)),
    ("I", ("pU1", "pI0",)),
    ("", ("pI1",)),
)


def solution(mesh):
    split = P(("gr", "gc"))
    return jax.shard_map(
        per_device,
        mesh=mesh,
        in_specs=(split,) * 5 + (P(),) * 14,
        out_specs=(split, split) + (P(),) * 14,
        check_vma=False,
    )
```

```python
import functools
import jax
import jax.numpy as jnp
from jax import lax
from jax.experimental import pallas as pl
from jax.experimental.pallas import tpu as pltpu
from jax.sharding import PartitionSpec as P

D = 768
HEADS = 12
HEAD_DIM = 64
FF = 3072
BF = jnp.bfloat16
F32 = jnp.float32
EPS = 1e-12
FAR = 1e30
NEG = -1e30
HALF_ROOT = 0.7071067811865476
DENSITY = 0.3989422804014327
NN = (((1,), (0,)), ((), ()))
NT = (((1,), (1,)), ((), ()))
TN = (((0,), (0,)), ((), ()))
MIB = 1024 * 1024
PACE = 0.05
WAIT = 0.05
SMEM = pltpu.SMEM
VMEM = pltpu.VMEM


def shape(dims, dtype):
    return jax.ShapeDtypeStruct(dims, dtype)


def near(dims, dtype):
    return VMEM(dims, dtype)


def away(array):
    return pltpu.with_memory_space_constraint(array, pltpu.HBM)


def kernel_call(body, outs, name, us, limit, scalars=0, far=0, far_outs=(), scratch=(), aliases=None):
    def place(i):
        if i < scalars:
            return pl.BlockSpec(memory_space=SMEM)
        return pl.BlockSpec(memory_space=pltpu.HBM if i < scalars + far else VMEM)

    def call(*args):
        return pl.pallas_call(
            body,
            in_specs=[place(i) for i in range(len(args))],
            out_specs=[pl.BlockSpec(memory_space=pltpu.HBM if i in far_outs else VMEM) for i in range(len(outs))]
            if isinstance(outs, list)
            else pl.BlockSpec(memory_space=VMEM),
            out_shape=outs,
            scratch_shapes=list(scratch),
            input_output_aliases=aliases or {},
            compiler_params=pltpu.CompilerParams(vmem_limit_bytes=limit * MIB),
            cost_estimate=pl.CostEstimate(
                flops=int(us * 1.1e9), bytes_accessed=int(us * 3e6), transcendentals=0
            ),
            name=name,
        )(*args)

    return call


def mm(left, right, dims=NN):
    return lax.dot_general(left, right, dims, preferred_element_type=F32)


def lanes(dims):
    return lax.broadcasted_iota(jnp.int32, dims, len(dims) - 1)


def row_of(ref):
    return ref[...][None, :]


def normalize(values):
    centre = values - jnp.mean(values, axis=-1, keepdims=True)
    factor = lax.rsqrt(jnp.mean(centre * centre, axis=-1, keepdims=True) + EPS)
    return centre * factor, factor


def norm_back(incoming, normed, factor, gain):
    scaled = incoming * gain
    return factor * (
        scaled
        - jnp.mean(scaled, axis=-1, keepdims=True)
        - normed * jnp.mean(scaled * normed, axis=-1, keepdims=True)
    )


def span_lanes(labels, length):
    rows = lax.broadcasted_iota(jnp.int32, (128, length), 0)
    return jnp.where(rows == jnp.broadcast_to(labels, (128, length)), 1.0, 0.0).T


def attend_kernel(
    unroll, rows, labels_far, tokens_far, w_far, bq_far, bv_far, w_out_far, w_up_far, w_down_far, *refs
):
    packed_far, mixed, lse = refs[:rows], refs[rows : 2 * rows], refs[2 * rows : 3 * rows]
    w_out_ref, w_up_ref, w_down_ref = refs[3 * rows : 3 * rows + 3]
    labels_ref, tokens_ref, w_ref, bq_ref, bv_ref = refs[3 * rows + 3 : 3 * rows + 8]
    packed, sems = refs[3 * rows + 8 : 4 * rows + 8], refs[-1]
    length = packed[0].shape[0]
    columns = [slice(at, at + D) for at in range(0, 3 * D, D)]
    pairs = [(tokens_far, tokens_ref), (bq_far, bq_ref), (bv_far, bv_ref), (labels_far, labels_ref)]
    pairs += [(w_far.at[:, c], w_ref.at[:, c]) for c in columns]
    pairs += [(w_out_far, w_out_ref), (w_up_far, w_up_ref), (w_down_far, w_down_ref)]
    pairs += list(zip(packed, packed_far))
    copies = [pltpu.make_async_copy(*pair, sems.at[i]) for i, pair in enumerate(pairs)]
    for copy in copies[:10]:
        copy.start()
    scale = jnp.asarray(HEAD_DIM ** (-0.5), BF)
    for copy in copies[:4]:
        copy.wait()
    for k, c in enumerate(columns):
        copies[4 + k].wait()
        for row in range(rows):
            made = mm(tokens_ref[row * length : (row + 1) * length, :], w_ref[:, c])
            bias = (row_of(bq_ref), 0.0, row_of(bv_ref))[k]
            packed[row][:, c] = (made + bias).astype(BF)
    for copy in copies[10:]:
        copy.start()
    lane = lanes((length, 128))
    low_half = lane < HEAD_DIM

    for row in range(rows):
        hot = span_lanes(labels_ref[row : row + 1, :], length)
        mark_q = (hot * FAR).astype(BF)
        mark_k = jnp.where(lane < 4, hot - 1.0, 0.0).astype(BF)
        packed_ref, mixed_ref, lse_ref = packed[row], mixed[row], lse[row]
        lse_ref[...] = jnp.zeros_like(lse_ref)

        def one(p):
            at = pl.multiple_of(p * 128, 128)
            query = packed_ref[:, pl.ds(at, 128)] * scale
            keys = jnp.concatenate([packed_ref[:, pl.ds(D + at, 128)], mark_k], axis=1)
            values = packed_ref[:, pl.ds(2 * D + at, 128)]
            outs = []
            logs = lse_ref[...]
            for half in range(2):
                own = low_half if half == 0 else jnp.logical_not(low_half)
                queries = jnp.concatenate(
                    [jnp.where(own, query, jnp.zeros_like(query)), mark_q], axis=1
                )
                scores = mm(queries, keys, NT)
                top = jnp.max(scores, axis=1, keepdims=True)
                grown = jnp.exp(scores - top)
                total = jnp.sum(grown, axis=1, keepdims=True)
                outs.append(mm(grown.astype(BF), values) * (1.0 / total))
                logs = jnp.where(lane == 2 * p + half, top + jnp.log(total), logs)
            lse_ref[...] = logs
            mixed_ref[:, pl.ds(at, 128)] = jnp.where(low_half, outs[0], outs[1]).astype(BF)

        def some(t, carry):
            for u in range(unroll):
                one(t * unroll + u)
            return carry

        lax.fori_loop(0, HEADS // 2 // unroll, some, 0)
    for copy in copies[7:]:
        copy.wait()


def attend(labels, tokens, w_in, b_query, b_value, weights, unroll=3):
    rows, length = labels.shape
    made = kernel_call(
        functools.partial(attend_kernel, unroll, rows),
        [pltpu.HBM((length, 3 * D), BF)] * rows + [near((length, D), BF)] * rows
        + [near((length, 128), F32)] * rows + [near(w.shape, BF) for w in weights],
        "attend", 15 * PACE, 20, far=8, far_outs=range(rows),
        scratch=[VMEM(labels.shape, jnp.int32), VMEM(tokens.shape, BF), VMEM(w_in.shape, BF), VMEM((D,), F32), VMEM((D,), F32)]
        + [VMEM((length, 3 * D), BF)] * rows + [pltpu.SemaphoreType.DMA((10 + rows,))],
    )(*(away(x) for x in (labels, tokens, w_in, b_query, b_value) + tuple(weights)))
    return made[:rows], made[rows : 2 * rows], made[2 * rows : 3 * rows], made[3 * rows :]


def span_starts(labels_ref, per_row):
    rows, length = labels_ref.shape
    out = []
    for row in range(rows):
        labels = jnp.broadcast_to(labels_ref[row : row + 1, :], (per_row, length))
        level = lax.broadcasted_iota(jnp.int32, (per_row, length), 0)
        below = jnp.sum(jnp.where(labels < level, 1.0, 0.0), axis=1, keepdims=True)
        out.append(below.astype(jnp.int32) + row * length)
    return jnp.concatenate(out, axis=0)


def picked(spot, at, size):
    place = lax.broadcasted_iota(jnp.int32, (spot.shape[0], size), 1) + at
    return jnp.where(place == spot, 1.0, 0.0).astype(BF)


def feed_rows(tokens, mixed, w_out_ref, w_up_ref, w_down_ref, vectors, width, keep):
    b_out, gain_one, bias_one, b_up, b_down, gain_two, bias_two = (row_of(ref) for ref in vectors)
    first = tokens.astype(F32) + mm(mixed, w_out_ref[...]) + b_out
    normed, factor = normalize(first)
    middle = normed * gain_one + bias_one
    low = middle.astype(BF)
    keep("first", normed, factor, low)
    total = middle + b_down
    for at in range(0, FF, width):
        before = mm(low, w_up_ref[:, at : at + width]) + b_up[:, at : at + width]
        share = 0.5 * (1.0 + lax.erf(before * HALF_ROOT))
        hidden = (before * share).astype(BF)
        keep("hidden", before, share, hidden, at)
        total = total + mm(hidden, w_down_ref[at : at + width, :])
    normed, factor = normalize(total)
    keep("second", normed, factor)
    return (normed * gain_two + bias_two).astype(BF)


def opening_kernel(rows, spans, labels_ref, tokens_ref, *refs):
    mixed_refs, weights, vectors, cls_ref = refs[:rows], refs[rows : rows + 3], refs[rows + 3 : -1], refs[-1]
    length = labels_ref.shape[1]
    spot = span_starts(labels_ref, spans // rows)
    tokens = jnp.zeros((spans, D), F32)
    mixed = jnp.zeros((spans, D), F32)
    for row in range(rows):
        pick = picked(spot, row * length, length)
        tokens += mm(pick, tokens_ref[row * length : (row + 1) * length, :])
        mixed += mm(pick, mixed_refs[row][...])
    cls_ref[...] = feed_rows(tokens, mixed.astype(BF), *weights, vectors, D, lambda *made: None)


def opening(spans, labels, tokens, mixed, weights, vectors):
    return kernel_call(
        functools.partial(opening_kernel, len(mixed), spans), shape((spans, D), BF), "opening", 4 * PACE, 4
    )(labels, tokens, *mixed, *weights, *vectors)


def feed_kernel(row, width, me_ref, tokens_ref, mixed_ref, *refs):
    weights, vectors = refs[:3], refs[3:10]
    low_ref, n1_ref, f1_ref, hidden_ref, slope_ref, n2_ref, f2_ref, out_ref = refs[10:]
    length = mixed_ref.shape[0]

    def keep(what, *made):
        if what == "first":
            n1_ref[...] = made[0].astype(BF)
            f1_ref[...] = jnp.broadcast_to(made[1], (length, 128))
            low_ref[...] = made[2]
        elif what == "hidden":
            before, share, hidden, at = made
            hidden_ref[:, at : at + width] = hidden
            slope_ref[:, at : at + width] = (
                share + before * jnp.exp(-0.5 * before * before) * DENSITY
            ).astype(BF)
        else:
            n2_ref[...] = made[0].astype(BF)
            f2_ref[...] = jnp.broadcast_to(made[1], (length, 128))

    tokens = tokens_ref[row * length : (row + 1) * length, :]
    out_ref[...] = feed_rows(tokens, mixed_ref[...], *weights, vectors, width, keep)


def feed(row, me, tokens, mixed, weights, vectors, width=768):
    length = mixed.shape[0]
    return kernel_call(
        functools.partial(feed_kernel, row, width),
        [
            near((length, D), BF), near((length, D), BF), near((length, 128), F32), near((length, FF), BF),
            near((length, FF), BF), near((length, D), BF), near((length, 128), F32), shape((length, D), BF),
        ],
        "feed", 9 * PACE, 7, scalars=1,
    )(me, tokens, mixed, *weights, *vectors)


def chain_kernel(
    width, me_ref, branch_ref, second_ref, slope_ref, n1_ref, f1_ref, gain_ref, w_down_ref, w_up_ref, w_out_ref,
    before_ref, first_ref, attn_ref, mixed_ref, sums_ref,
):
    d_middle = second_ref[...]
    branch = branch_ref[...]
    parts = []
    for at in range(0, FF, width):
        d_hidden = mm(branch, w_down_ref[at : at + width, :], NT)
        d_before = (d_hidden * slope_ref[:, at : at + width].astype(F32)).astype(BF)
        before_ref[:, at : at + width] = d_before
        parts.append(jnp.sum(d_before.astype(F32), axis=0, keepdims=True))
        d_middle = d_middle + mm(d_before, w_up_ref[:, at : at + width], NT)
    normed = n1_ref[...].astype(F32)
    d_first = norm_back(d_middle, normed, f1_ref[:, 0:1], row_of(gain_ref))
    d_attn = d_first.astype(BF)
    first_ref[...] = d_first
    attn_ref[...] = d_attn
    mixed_ref[...] = mm(d_attn, w_out_ref[...], NT).astype(BF)
    sums_ref[...] = jnp.concatenate(
        [
            jnp.sum(d_middle * normed, axis=0, keepdims=True),
            jnp.sum(d_middle, axis=0, keepdims=True),
            jnp.sum(d_attn.astype(F32), axis=0, keepdims=True),
        ] + parts + [jnp.zeros((1, D), F32)],
        axis=0,
    )


def chain(me, branch, second, slope, n1, f1, gain_one, w_down, w_up, w_out):
    length = branch.shape[0]
    return kernel_call(
        functools.partial(chain_kernel, D),
        [
            near((length, FF), BF), near((length, D), F32), near((length, D), BF),
            near((length, D), BF), shape((8, D), F32),
        ],
        "chain", 6.6 * PACE, 6, scalars=1,
    )(me, branch, second, slope, n1, f1, gain_one, w_down, w_up, w_out)


def split3(values):
    high = values.astype(BF)
    rest = values - high.astype(F32)
    mid = rest.astype(BF)
    return high, mid, (rest - mid.astype(F32)).astype(BF)


def contrast_kernel(
    size, rows_count, slots_of, me_ref, count_ref, labels_ref, partner_ref, pos_ref, given_ref, gain_ref, *refs
):
    tables, refs = refs[: len(slots_of)], refs[len(slots_of) :]
    groups = [refs[i * rows_count : (i + 1) * rows_count] for i in range(2)]
    n2_refs, f2_refs = groups
    loss_ref, sums_ref = refs[2 * rows_count : 2 * rows_count + 2]
    second_refs = refs[2 * rows_count + 2 : 3 * rows_count + 2]
    branch_refs = refs[3 * rows_count + 2 : 4 * rows_count + 2]
    table = refs[-1]
    spans = tables[0].shape[1]
    total = table.shape[0]
    me = me_ref[0]
    for ref, masks in zip(tables, slots_of):
        for k, mask in enumerate(masks):
            table[pl.ds(pl.multiple_of((mask ^ me) * spans, spans), spans), :] = ref[k].astype(F32)
    rows = table[...].astype(BF)
    scale = 2.0 * D ** (-0.5)
    similar = mm(rows, rows, NT) * scale
    other = lax.broadcasted_iota(jnp.int32, (total, total), 0)
    own = lax.broadcasted_iota(jnp.int32, (total, total), 1)
    similar = jnp.where(own == other, NEG, similar)
    partner = row_of(partner_ref) == other
    top = jnp.max(similar, axis=0, keepdims=True)
    log_rows = top + jnp.log(jnp.sum(jnp.exp(similar - top), axis=0, keepdims=True))
    chosen = jnp.sum(jnp.where(partner, similar, 0.0), axis=0, keepdims=True)
    loss = jnp.sum(log_rows - chosen, axis=1, keepdims=True) / total
    loss_ref[...] = jnp.broadcast_to(loss, loss_ref.shape)
    slope = (jnp.exp(similar - log_rows) - jnp.where(partner, 1.0, 0.0)).astype(BF)
    spot = lax.broadcasted_iota(jnp.int32, (spans, total), 0) + me * spans
    pick = jnp.where(spot == lax.broadcasted_iota(jnp.int32, (spans, total), 1), 1.0, 0.0).astype(BF)
    mine = mm(pick, slope, NT).astype(BF)
    across = mm(pick, slope).astype(BF)
    parts = split3((mm(mine, rows) + mm(across, rows)) * scale)

    starts = span_starts(labels_ref, spans // rows_count)
    slots = given_ref.shape[1]
    per_row = spans // rows_count
    sums = [jnp.zeros((1, D), F32)] * 3
    for row in range(rows_count):
        for at in range(0, n2_refs[row].shape[0], size):
            base = row * n2_refs[row].shape[0] + at
            here = slice(at, at + size)
            place = lax.broadcasted_iota(jnp.int32, (size, slots), 0) + at
            upstream = jnp.zeros((size, D), F32)
            for span in range(row * per_row, (row + 1) * per_row):
                used = lanes((size, slots)) < count_ref[span]
                slot = jnp.where((place == pos_ref[span : span + 1, :]) & used, 1.0, 0.0).astype(BF)
                upstream += mm(slot, given_ref[span])
            hot = picked(starts, base, size)
            upstream += mm(hot, parts[0], TN) + (mm(hot, parts[1], TN) + mm(hot, parts[2], TN))
            normed = n2_refs[row][here, :].astype(F32)
            second = norm_back(upstream, normed, f2_refs[row][here, 0:1], row_of(gain_ref))
            branch = second.astype(BF)
            second_refs[row][here, :] = second
            branch_refs[row][here, :] = branch
            for k, values in enumerate((upstream * normed, upstream, branch.astype(F32))):
                sums[k] = sums[k] + jnp.sum(values, axis=0, keepdims=True)
    sums_ref[...] = jnp.concatenate(sums + [jnp.zeros((5, D), F32)], axis=0)


def contrast(me, count, labels, partner, tables, slots_of, pos, given, n2, f2, gain_two, size=256):
    length = n2[0].shape[0]
    rows = len(n2)
    spans = tables[0].shape[1]
    devices = sum(len(masks) for masks in slots_of)
    made = kernel_call(
        functools.partial(contrast_kernel, size, rows, slots_of),
        [shape((8, 128), F32), shape((8, D), F32)]
        + [near((length, D), F32)] * rows + [near((length, D), BF)] * rows,
        "contrast", 4 * PACE, 6 if devices * spans <= 512 else 40, scalars=2,
        scratch=[VMEM((devices * spans, D), F32)],
    )(me, count, labels, partner, pos, given, gain_two, *tables, *n2, *f2)
    return made[0], made[2 : 2 + rows], made[2 + rows :], made[1]


def merge_kernel(*refs):
    for k, ref in enumerate(refs[:-1]):
        refs[-1][k] = ref[...]


def merge(parts):
    return kernel_call(
        merge_kernel, near((len(parts),) + parts[0].shape, parts[0].dtype), "merge", 0.5 * PACE, 2
    )(*parts)


def tile_place(kind, j):
    order = (0, 1, 2, 3) if kind == 0 else (1, 0, 2, 3)
    out = 0
    for bit in order:
        out = out * 2 + ((j >> bit) & 1)
    return out


def put_tiles(out_ref, kind, values, base):
    rows = values.shape[0] // 16
    for j in range(16):
        out_ref[kind, tile_place(kind, j) ^ base] = values[j * rows : (j + 1) * rows, :]


def cut(start, size):
    return pl.ds(pl.multiple_of(start, 128), size)


def product(lefts, rights, left_cut=None, right_cut=None):
    whole = slice(None)
    return sum(
        mm(left[:, left_cut or whole], right[:, right_cut or whole], TN) for left, right in zip(lefts, rights)
    ).astype(BF)


def grad_down_kernel(rel, rows, me_ref, *refs):
    hidden, branch, out_ref = refs[:rows], refs[rows : 2 * rows], refs[-1]
    for kind in range(2):
        columns = cut(((me_ref[0] ^ rel) * 2 + kind) * D, D)
        put_tiles(out_ref, kind, product(hidden, branch, columns), me_ref[1 + kind])


def grad_up_kernel(rel, rows, me_ref, *refs):
    low, before, out_ref = refs[:rows], refs[rows : 2 * rows], refs[-1]
    for kind in range(2):
        columns = cut(((me_ref[0] ^ rel) * 2 + kind) * D, D)
        put_tiles(out_ref, kind, product(low, before, None, columns), me_ref[1 + kind])


def grad_in_kernel(rel, rows, me_ref, tokens_ref, *refs):
    packed, mixed, attn, out_ref = refs[:rows], refs[rows : 2 * rows], refs[2 * rows : 3 * rows], refs[-1]
    length = packed[0].shape[0]
    half = me_ref[0] ^ rel
    tokens = [tokens_ref.at[r * length : (r + 1) * length, :] for r in range(rows)]
    left = product(tokens, packed, None, cut(half * (3 * D // 2), 3 * D // 2))
    right = product(mixed, attn, None, cut(half * (D // 2), D // 2))
    joined = jnp.concatenate([left, right], axis=1)
    for kind in range(2):
        put_tiles(out_ref, kind, joined[kind * D // 2 : (kind + 1) * D // 2, :], me_ref[1 + kind])


def grad_down(me, hidden, branch, rel):
    return kernel_call(
        functools.partial(grad_down_kernel, rel, len(hidden)), shape((2, 16, 48, D), BF), "grad_down",
        WAIT if rel == 0 else 3.3 * PACE, 6, scalars=1,
    )(me, *hidden, *branch)


def grad_up(me, low, d_before, rel):
    return kernel_call(
        functools.partial(grad_up_kernel, rel, len(low)), shape((2, 16, 48, D), BF), "grad_up",
        WAIT if rel == 0 else 3.3 * PACE, 6, scalars=1,
    )(me, *low, *d_before)


def grad_in(me, tokens, d_packed, mixed, d_attn, rel):
    return kernel_call(
        functools.partial(grad_in_kernel, rel, len(mixed)), shape((2, 16, 24, 2 * D), BF), "grad_in",
        WAIT if rel == 0 else 3.6 * PACE, 8, scalars=1,
    )(me, tokens, *d_packed, *mixed, *d_attn)


def attend_back_kernel(row, pairs, unroll, me_ref, labels_ref, packed_ref, mixed_ref, incoming_ref, lse_ref, *refs):
    out_ref, sums_ref = refs[-2:]
    length = labels_ref.shape[1]
    here = slice(None)
    hot = span_lanes(labels_ref[row : row + 1, :], length)
    lane = lanes((length, 128))
    mark_q = (hot * FAR).astype(BF)
    mark_k = jnp.where(lane < 4, hot - 1.0, jnp.where(lane < 7, -1.0, 0.0)).astype(BF)
    mark_v = jnp.where((lane >= 4) & (lane < 7), -1.0, 0.0).astype(BF)
    none = jnp.zeros((length, 128), BF)
    low_half = lane < HEAD_DIM
    scale = jnp.asarray(HEAD_DIM ** (-0.5), BF)
    sums_ref[...] = jnp.zeros_like(sums_ref)

    def pack3(column, base):
        high, mid, low = (part.astype(F32) for part in split3(column))
        filled = jnp.where(lane == 4, high, jnp.where(lane == 5, mid, jnp.where(lane == 6, low, 0.0)))
        return base + filled.astype(BF)

    def one(p):
        at = pl.multiple_of(p * 128, 128)
        query = packed_ref[here, pl.ds(at, 128)] * scale
        key = packed_ref[here, pl.ds(D + at, 128)]
        keys = jnp.concatenate([key, mark_k], axis=1)
        values = jnp.concatenate([packed_ref[here, pl.ds(2 * D + at, 128)], mark_v], axis=1)
        incoming = incoming_ref[here, pl.ds(at, 128)]
        product = incoming.astype(F32) * mixed_ref[here, pl.ds(at, 128)].astype(F32)
        logs = lse_ref[here, :]
        d_query = jnp.zeros((length, 128), F32)
        d_key = jnp.zeros((length, 128), F32)
        d_value = jnp.zeros((length, 128), F32)
        for half in range(2):
            own = low_half if half == 0 else jnp.logical_not(low_half)
            log_total = jnp.sum(jnp.where(lane == 2 * p + half, logs, 0.0), axis=1, keepdims=True)
            centred = jnp.sum(jnp.where(own, product, 0.0), axis=1, keepdims=True)
            own_query = jnp.where(own, query, none)
            own_incoming = jnp.where(own, incoming, none)
            own_key = jnp.where(own, key, none)
            queries = jnp.concatenate([own_query, pack3(log_total, mark_q)], axis=1)
            grads = jnp.concatenate([own_incoming, pack3(centred, none)], axis=1)
            weights = jnp.exp(mm(keys, queries, NT))
            d_scores = (weights * mm(values, grads, NT)).astype(BF)
            d_value += mm(weights.astype(BF), own_incoming)
            d_key += mm(d_scores, own_query)
            d_query += mm(d_scores, own_key, TN)
        d_query = (d_query * HEAD_DIM ** (-0.5)).astype(BF)
        d_value = d_value.astype(BF)
        out_ref[:, pl.ds(at, 128)] = d_query
        out_ref[:, pl.ds(D + at, 128)] = d_key.astype(BF)
        out_ref[:, pl.ds(2 * D + at, 128)] = d_value
        sums_ref[0:1, pl.ds(at, 128)] = jnp.sum(d_query.astype(F32), axis=0, keepdims=True)
        sums_ref[1:2, pl.ds(at, 128)] = jnp.sum(d_value.astype(F32), axis=0, keepdims=True)

    def some(t, carry):
        for u in range(unroll):
            one(pairs[0] + t * unroll + u)
        return carry

    lax.fori_loop(0, (pairs[1] - pairs[0]) // unroll, some, 0)


def attend_back(row, pairs, me, labels, packed, mixed, incoming, lse, before=None, unroll=3):
    length = labels.shape[1]
    olds = [] if before is None else [before]
    return kernel_call(
        functools.partial(attend_back_kernel, row, pairs, unroll),
        [near((length, 3 * D), BF), shape((8, D), F32)],
        "attend_back", 5 * PACE, 6, scalars=1, aliases={6: 0} if olds else None,
    )(me, labels, packed, mixed, incoming, lse, *olds)


def token_kernel(rows, me_ref, *refs):
    first, packed, w_ref, out_ref = refs[:rows], refs[rows : 2 * rows], refs[-2], refs[-1]
    length = packed[0].shape[0]
    for r in range(rows):
        out_ref[r * length : (r + 1) * length, :] = first[r][...] + mm(packed[r][...], w_ref[...], NT)


def grad_token(me, first, d_packed, w_in):
    rows = len(first)
    return kernel_call(
        functools.partial(token_kernel, rows), shape((rows * first[0].shape[0], D), F32), "grad_token", 5.6 * PACE, 6, scalars=1,
    )(me, *first, *d_packed, w_in)


SUMS = (16, 17, 10, 8, 9, 11, 2, 0, 1)


def spread_kernel(me_ref, sums_ref, *outs):
    for at, out in zip(SUMS, outs):
        for k in range(out.shape[0] // D):
            out[k * D : (k + 1) * D] = sums_ref[at + k, :]


def spread(me, sums):
    return kernel_call(
        spread_kernel, [shape((FF if at == 11 else D,), F32) for at in SUMS], "spread", 1 * PACE, 2, scalars=1
    )(me, sums)


def join_kernel(me_ref, *refs):
    length = refs[0].shape[0]
    for k, ref in enumerate(refs[:-1]):
        refs[-1][k * length : (k + 1) * length, :] = ref[...]


def join(me, parts):
    length, width = parts[0].shape
    return kernel_call(
        join_kernel, shape((len(parts) * length, width), parts[0].dtype), "join", 1 * PACE, 4, scalars=1
    )(me, *parts)


def place_kernel(rel, name, olds, me_ref, *refs):
    refs = refs[olds:]
    halves = refs[:2]
    outs, holds, sems = (refs[2:4], refs[4:6], refs[6]) if name == "in" else (refs[2:3], refs[3:4], refs[4])
    half = me_ref[0] ^ rel
    copies = []
    for kind, half_ref in enumerate(halves):
        rows = half_ref.shape[1]
        for j in range(16):
            tile = half_ref[tile_place(kind, j) ^ me_ref[1 + kind]].astype(F32)
            at = 0
            for hold in holds:
                hold[kind, j * rows : (j + 1) * rows, :] = tile[:, at : at + hold.shape[2]]
                at += hold.shape[2]
        for out, hold in zip(outs, holds):
            high, wide = hold.shape[1:]
            if name == "down":
                spot = out.at[pl.ds(pl.multiple_of((half * 2 + kind) * high, high), high), :]
            elif name == "up":
                spot = out.at[:, cut((half * 2 + kind) * wide, wide)]
            else:
                spot = out.at[kind * high : (kind + 1) * high, cut(half * wide, wide)]
            copies.append(pltpu.make_async_copy(hold.at[kind], spot, sems.at[len(copies)]))
            copies[-1].start()
    for copy in copies:
        copy.wait()


PLACES = {
    "down": [((FF, D), (D, D))],
    "up": [((D, FF), (D, D))],
    "in": [((D, 3 * D), (D // 2, 3 * D // 2)), ((D, D), (D // 2, D // 2))],
}


def place(name, rel, me, halves, before=None):
    outs = PLACES[name]
    olds = [] if before is None else list(before)
    return kernel_call(
        functools.partial(place_kernel, rel, name, len(olds)),
        [pltpu.HBM(whole, F32) for whole, _ in outs],
        "place", 2 * PACE, 10, scalars=1, far=len(olds), far_outs=range(len(outs)),
        scratch=[VMEM((2,) + part, F32) for _, part in outs] + [pltpu.SemaphoreType.DMA((2 * len(outs),))],
        aliases={1 + i: i for i in range(len(olds))},
    )(me, *(away(old) for old in olds), *halves)


def device_count():
    return lax.axis_size("gr") * lax.axis_size("gc")


def swap(values, mask):
    pairs = [(i, i ^ mask) for i in range(device_count())]
    return lax.ppermute(values, ("gr", "gc"), pairs)


def plus(left, *others):
    total = left.astype(F32)
    for other in others:
        total = total + other.astype(F32)
    return total.astype(BF)


def packed_slot(extra):
    high = lax.reduce_precision(extra, exponent_bits=8, mantissa_bits=7)
    return jnp.concatenate([high, extra - high]).astype(BF)[None]


def swap_with(tiles, extra, mask):
    if extra is None:
        return swap(tiles, mask), None
    got = swap(jnp.concatenate([tiles, packed_slot(extra)]), mask)
    wide = got[-1].astype(F32)
    cut_at = extra.shape[0]
    return got[:-1], extra + (wide[:cut_at] + wide[cut_at:])


def flow(send, keep_of, extra_of=None):
    (got,) = yield (swap(send, 1),)
    keep = keep_of()
    one, two = plus(keep[0], got[0]), plus(keep[1], got[1])
    one, two = yield plus(one[:8], swap(one[8:], 2)), plus(two[:8], swap(two[8:], 4))
    one, two = plus(one[:4], swap(one[4:], 4)), plus(two[:4], swap(two[4:], 2))
    ours, others = yield jnp.stack([one[:2], two[:2]], axis=1), jnp.stack([one[2:], two[2:]], axis=1)
    (both,) = yield (plus(ours, swap(others, 8)),)
    own = plus(both[0], swap(both[1], 16))
    mask = 32
    while mask < device_count():
        own = plus(own, swap(own, mask))
        mask *= 2
    (own,) = yield (own,)
    extra = None if extra_of is None else extra_of()
    mask = 32
    while extra is not None and mask < device_count():
        extra = extra + swap(extra, mask)
        mask *= 2
    got, extra = swap_with(own, extra, 16)
    both, extra = yield jnp.concatenate([own, got]), extra
    got, extra = swap_with(both, extra, 8)
    both = jnp.concatenate([both, got])
    one, two, extra = yield both[::2], both[1::2], extra
    got, extra = swap_with(one, extra, 4)
    one, two, extra = yield jnp.concatenate([one, got]), jnp.concatenate([two, swap(two, 2)]), extra
    got, extra = swap_with(one, extra, 2)
    one, two, extra = yield jnp.concatenate([one, got]), jnp.concatenate([two, swap(two, 4)]), extra
    return (one, two), (swap(one, 1), swap(two, 1)), extra


def flow_near(sums):
    yield (sums + swap(sums, 1),)


class Line:
    def __init__(self, steps, made):
        self.steps, self.made = steps, made
        self.result = None
        self.opened = False

    def go(self, made):
        try:
            self.made = self.steps(*made) if not self.opened else self.steps.send(made)
            if not self.opened:
                self.steps, self.made = self.made, next(self.made)
            self.opened = True
        except StopIteration as end:
            self.result = self.made = end.value


class Rounds:
    def __init__(self, me, token):
        self.me, self.token, self.going = me, token, []

    def begin(self, lines):
        kept = [line.made for line in self.going]
        made, kept, token = lax.optimization_barrier(([line.made for line in lines], kept, self.token))
        self.token = (kept, token)
        for line, arrays in zip(self.going, kept):
            line.made = arrays
            if line.result is not None:
                line.result = arrays
        for line, arrays in zip(lines, made):
            line.go(arrays if line not in self.going else line.made)
        self.going = lines

    def work(self, call, *args, token=lambda made: made):
        me, _ = lax.optimization_barrier((self.me, self.token))
        made = call(me, *args)
        self.token = token(made)
        return made


def bits_of(value, order):
    out = jnp.zeros_like(value)
    for bit in order:
        out = out * 2 + ((value >> bit) & 1)
    return out


def per_device(
    tokens, span_ids, mlm_pos, mlm_count, mlm_grad, positive, w_in, b_query, b_value, w_out, b_out,
    ln1_gain, ln1_bias, w_up, b_up, w_down, b_down, ln2_gain, ln2_bias,
):
    rows, length = span_ids.shape
    spans = mlm_pos.shape[0]
    index = lax.axis_index("gr") * lax.axis_size("gc") + lax.axis_index("gc")
    chip = (index >> 1) & 15
    me = jnp.stack(
        [index & 1, bits_of(chip, (0, 1, 2, 3)), bits_of(chip, (1, 0, 2, 3))]
    ).astype(jnp.int32)
    where = index.astype(jnp.int32)[None]
    me, where, b_query = lax.optimization_barrier((me, where, b_query))
    weights = (w_out, w_up, w_down)
    vectors = (b_out, ln1_gain, ln1_bias, b_up, b_down, ln2_gain, ln2_bias)

    packed, mixed, lse, weights = attend(span_ids, tokens, w_in, b_query, b_value, weights)
    cls = opening(spans, span_ids, tokens, mixed, weights, vectors)
    cls, here = lax.optimization_barrier((cls, me))
    masks = (0, 8, 16, 24)
    parts = [cls] + [swap(cls, m) for m in masks[1:]]
    made = [feed(0, here, tokens, mixed[0], weights, vectors)]
    table = merge(parts)
    table, here, _ = lax.optimization_barrier((table, me, made[0][1]))
    tables = [table] + [swap(table, m) for m in range(1, 8)]
    slots_of = [tuple(m ^ k for k in masks) for m in range(8)]
    made.append(feed(1, here, tokens, mixed[1], weights, vectors))
    bit = 32
    while bit < device_count():
        table, masks = jnp.concatenate(tables), sum(slots_of, ())
        tables = [table, swap(table, bit)]
        slots_of = [masks, tuple(m ^ bit for m in masks)]
        bit *= 2
    low, n1, f1, hidden, slope, n2, f2, layer_out = zip(*made)
    loss, second, branch, sums_two = contrast(
        where, mlm_count, span_ids, positive, tables, slots_of, mlm_pos, mlm_grad, n2, f2, ln2_gain
    )

    order = Rounds(me, sums_two)
    lines, keeps, links, sums_in, sides = {}, {}, [None] * rows, [], {}
    d_packed = [None] * rows
    part = [0] * rows

    def gradient(name, call, *args):
        if name not in lines:
            send = order.work(functools.partial(call, rel=1), *args)
            extra_of = (lambda: lines["S"].made[0]) if name == "D" else None
            lines[name] = Line(functools.partial(flow, keep_of=lambda: keeps[name], extra_of=extra_of), (send,))
        else:
            keeps[name] = order.work(functools.partial(call, rel=0), *args)

    def link(row):
        links[row] = order.work(
            chain, branch[row], second[row], slope[row], n1[row], f1[row], ln1_gain,
            weights[2], weights[1], weights[0], token=lambda made: made[4],
        )

    def back(row):
        pairs = (part[row] * HEADS // 4, (part[row] + 1) * HEADS // 4)
        d_packed[row], sums = order.work(
            functools.partial(attend_back, row, pairs),
            span_ids, packed[row], mixed[row], links[row][3], lse[row], d_packed[row],
            token=lambda made: made[1],
        )
        part[row] += 1
        sums_in.append(sums)

    def settle(name, rel):
        call = functools.partial(place, {"D": "down", "U": "up", "I": "in"}[name], rel)
        sides[name] = order.work(call, lines[name].result[rel], sides.get(name))

    for going, events in PLAN:
        if "S" in going:
            sums_one = sum(made[4] for made in links)
            lines["S"] = Line(flow_near, (jnp.concatenate([sums_two, sums_one, sum(sums_in)]),))
        order.begin([lines[name] for name in going])
        for event in events:
            if event == "gd":
                gradient("D", grad_down, hidden, branch)
            elif event == "gu":
                gradient("U", grad_up, low, [made[0] for made in links])
            elif event == "gi":
                gradient("I", grad_in, tokens, d_packed, mixed, [made[2] for made in links])
            elif event == "gt":
                sides["T"] = order.work(grad_token, [made[1] for made in links], d_packed, w_in)
            elif event == "jo":
                sides["J"] = order.work(join, layer_out)
            elif event == "ou":
                sides["S"] = order.work(spread, lines["D"].result[2])
            elif event[:2] == "ch":
                link(int(event[2]))
            elif event[:2] == "ab":
                back(int(event[2]))
            else:
                settle(event[1], int(event[2]))
    grad_tokens, g_down, g_up, g_in, small = (sides[name] for name in "TDUIS")

    return (
        sides["J"], grad_tokens, g_in[0], small[0], small[1], g_in[1], *small[2:5], g_up[0], small[5], g_down[0],
        *small[6:], loss[0, 0],
    )


PLAN = (
    ("", ("gd",)),
    ("D", ("gd",)),
    ("D", ("ch0", "ch1", "gu",)),
    ("DU", ("gu", "ab0", "ab0",)),
    ("DU", ("ab1", "ab1", "gi",)),
    ("DUIS", ("gi",)),
    ("DUI", ("gt",)),
    ("DI", ()),
    ("DUI", ()),
    ("DUI", ()),
    ("DUI", ("pD0",)),
    ("UI", ("pD1",)),
    ("UI", ()),
    ("UI", ("pU0", "ou", "jo",)),
    ("I", ("pU1", "pI0",)),
    ("", ("pI1",)),
)


def solution(mesh):
    split = P(("gr", "gc"))
    return jax.shard_map(
        per_device,
        mesh=mesh,
        in_specs=(split,) * 5 + (P(),) * 14,
        out_specs=(split, split) + (P(),) * 14,
        check_vma=False,
    )
```

```python
import functools
import jax
import jax.numpy as jnp
from jax import lax
from jax.experimental import pallas as pl
from jax.experimental.pallas import tpu as pltpu
from jax.sharding import PartitionSpec as P

D = 768
HEADS = 12
HEAD_DIM = 64
FF = 3072
BF = jnp.bfloat16
F32 = jnp.float32
EPS = 1e-12
FAR = 1e30
NEG = -1e30
HALF_ROOT = 0.7071067811865476
DENSITY = 0.3989422804014327
NN = (((1,), (0,)), ((), ()))
NT = (((1,), (1,)), ((), ()))
TN = (((0,), (0,)), ((), ()))
MIB = 1024 * 1024
PACE = 0.05
WAIT = 0.05
SMEM = pltpu.SMEM
VMEM = pltpu.VMEM


def shape(dims, dtype):
    return jax.ShapeDtypeStruct(dims, dtype)


def near(dims, dtype):
    return VMEM(dims, dtype)


def away(array):
    return pltpu.with_memory_space_constraint(array, pltpu.HBM)


def kernel_call(body, outs, name, us, limit, scalars=0, far=0, far_outs=(), scratch=(), aliases=None):
    def place(i):
        if i < scalars:
            return pl.BlockSpec(memory_space=SMEM)
        return pl.BlockSpec(memory_space=pltpu.HBM if i < scalars + far else VMEM)

    def call(*args):
        return pl.pallas_call(
            body,
            in_specs=[place(i) for i in range(len(args))],
            out_specs=[pl.BlockSpec(memory_space=pltpu.HBM if i in far_outs else VMEM) for i in range(len(outs))]
            if isinstance(outs, list)
            else pl.BlockSpec(memory_space=VMEM),
            out_shape=outs,
            scratch_shapes=list(scratch),
            input_output_aliases=aliases or {},
            compiler_params=pltpu.CompilerParams(vmem_limit_bytes=limit * MIB),
            cost_estimate=pl.CostEstimate(
                flops=int(us * 1.1e9), bytes_accessed=int(us * 3e6), transcendentals=0
            ),
            name=name,
        )(*args)

    return call


def mm(left, right, dims=NN):
    return lax.dot_general(left, right, dims, preferred_element_type=F32)


def lanes(dims):
    return lax.broadcasted_iota(jnp.int32, dims, len(dims) - 1)


def row_of(ref):
    return ref[...][None, :]


def normalize(values):
    centre = values - jnp.mean(values, axis=-1, keepdims=True)
    factor = lax.rsqrt(jnp.mean(centre * centre, axis=-1, keepdims=True) + EPS)
    return centre * factor, factor


def norm_back(incoming, normed, factor, gain):
    scaled = incoming * gain
    return factor * (
        scaled
        - jnp.mean(scaled, axis=-1, keepdims=True)
        - normed * jnp.mean(scaled * normed, axis=-1, keepdims=True)
    )


def span_lanes(labels, length):
    rows = lax.broadcasted_iota(jnp.int32, (128, length), 0)
    return jnp.where(rows == jnp.broadcast_to(labels, (128, length)), 1.0, 0.0).T


def attend_kernel(
    unroll, rows, labels_far, tokens_far, w_far, bq_far, bv_far, w_out_far, w_up_far, w_down_far, *refs
):
    packed_far, mixed, lse = refs[:rows], refs[rows : 2 * rows], refs[2 * rows : 3 * rows]
    w_out_ref, w_up_ref, w_down_ref = refs[3 * rows : 3 * rows + 3]
    labels_ref, tokens_ref, w_ref, bq_ref, bv_ref = refs[3 * rows + 3 : 3 * rows + 8]
    packed, sems = refs[3 * rows + 8 : 4 * rows + 8], refs[-1]
    length = packed[0].shape[0]
    columns = [slice(at, at + D) for at in range(0, 3 * D, D)]
    pairs = [(tokens_far, tokens_ref), (bq_far, bq_ref), (bv_far, bv_ref), (labels_far, labels_ref)]
    pairs += [(w_far.at[:, c], w_ref.at[:, c]) for c in columns]
    pairs += [(w_out_far, w_out_ref), (w_up_far, w_up_ref), (w_down_far, w_down_ref)]
    pairs += list(zip(packed, packed_far))
    copies = [pltpu.make_async_copy(*pair, sems.at[i]) for i, pair in enumerate(pairs)]
    for copy in copies[:10]:
        copy.start()
    scale = jnp.asarray(HEAD_DIM ** (-0.5), BF)
    for copy in copies[:4]:
        copy.wait()
    for k, c in enumerate(columns):
        copies[4 + k].wait()
        for row in range(rows):
            made = mm(tokens_ref[row * length : (row + 1) * length, :], w_ref[:, c])
            bias = (row_of(bq_ref), 0.0, row_of(bv_ref))[k]
            packed[row][:, c] = (made + bias).astype(BF)
    for copy in copies[10:]:
        copy.start()
    lane = lanes((length, 128))
    low_half = lane < HEAD_DIM

    for row in range(rows):
        hot = span_lanes(labels_ref[row : row + 1, :], length)
        mark_q = (hot * FAR).astype(BF)
        mark_k = jnp.where(lane < 4, hot - 1.0, 0.0).astype(BF)
        packed_ref, mixed_ref, lse_ref = packed[row], mixed[row], lse[row]
        lse_ref[...] = jnp.zeros_like(lse_ref)

        def one(p):
            at = pl.multiple_of(p * 128, 128)
            query = packed_ref[:, pl.ds(at, 128)] * scale
            keys = jnp.concatenate([packed_ref[:, pl.ds(D + at, 128)], mark_k], axis=1)
            values = packed_ref[:, pl.ds(2 * D + at, 128)]
            outs = []
            logs = lse_ref[...]
            for half in range(2):
                own = low_half if half == 0 else jnp.logical_not(low_half)
                queries = jnp.concatenate(
                    [jnp.where(own, query, jnp.zeros_like(query)), mark_q], axis=1
                )
                scores = mm(queries, keys, NT)
                top = jnp.max(scores, axis=1, keepdims=True)
                grown = jnp.exp(scores - top)
                total = jnp.sum(grown, axis=1, keepdims=True)
                outs.append(mm(grown.astype(BF), values) * (1.0 / total))
                logs = jnp.where(lane == 2 * p + half, top + jnp.log(total), logs)
            lse_ref[...] = logs
            mixed_ref[:, pl.ds(at, 128)] = jnp.where(low_half, outs[0], outs[1]).astype(BF)

        def some(t, carry):
            for u in range(unroll):
                one(t * unroll + u)
            return carry

        lax.fori_loop(0, HEADS // 2 // unroll, some, 0)
    for copy in copies[7:]:
        copy.wait()


def attend(labels, tokens, w_in, b_query, b_value, weights, unroll=3):
    rows, length = labels.shape
    made = kernel_call(
        functools.partial(attend_kernel, unroll, rows),
        [pltpu.HBM((length, 3 * D), BF)] * rows + [near((length, D), BF)] * rows
        + [near((length, 128), F32)] * rows + [near(w.shape, BF) for w in weights],
        "attend", 15 * PACE, 20, far=8, far_outs=range(rows),
        scratch=[VMEM(labels.shape, jnp.int32), VMEM(tokens.shape, BF), VMEM(w_in.shape, BF), VMEM((D,), F32), VMEM((D,), F32)]
        + [VMEM((length, 3 * D), BF)] * rows + [pltpu.SemaphoreType.DMA((10 + rows,))],
    )(*(away(x) for x in (labels, tokens, w_in, b_query, b_value) + tuple(weights)))
    return made[:rows], made[rows : 2 * rows], made[2 * rows : 3 * rows], made[3 * rows :]


def span_starts(labels_ref, per_row):
    rows, length = labels_ref.shape
    out = []
    for row in range(rows):
        labels = jnp.broadcast_to(labels_ref[row : row + 1, :], (per_row, length))
        level = lax.broadcasted_iota(jnp.int32, (per_row, length), 0)
        below = jnp.sum(jnp.where(labels < level, 1.0, 0.0), axis=1, keepdims=True)
        out.append(below.astype(jnp.int32) + row * length)
    return jnp.concatenate(out, axis=0)


def picked(spot, at, size):
    place = lax.broadcasted_iota(jnp.int32, (spot.shape[0], size), 1) + at
    return jnp.where(place == spot, 1.0, 0.0).astype(BF)


def feed_rows(tokens, mixed, w_out_ref, w_up_ref, w_down_ref, vectors, width, keep):
    b_out, gain_one, bias_one, b_up, b_down, gain_two, bias_two = (row_of(ref) for ref in vectors)
    first = tokens.astype(F32) + mm(mixed, w_out_ref[...]) + b_out
    normed, factor = normalize(first)
    middle = normed * gain_one + bias_one
    low = middle.astype(BF)
    keep("first", normed, factor, low)
    total = middle + b_down
    for at in range(0, FF, width):
        before = mm(low, w_up_ref[:, at : at + width]) + b_up[:, at : at + width]
        share = 0.5 * (1.0 + lax.erf(before * HALF_ROOT))
        hidden = (before * share).astype(BF)
        keep("hidden", before, share, hidden, at)
        total = total + mm(hidden, w_down_ref[at : at + width, :])
    normed, factor = normalize(total)
    keep("second", normed, factor)
    return (normed * gain_two + bias_two).astype(BF)


def opening_kernel(rows, spans, labels_ref, tokens_ref, *refs):
    mixed_refs, weights, vectors, cls_ref = refs[:rows], refs[rows : rows + 3], refs[rows + 3 : -1], refs[-1]
    length = labels_ref.shape[1]
    spot = span_starts(labels_ref, spans // rows)
    tokens = jnp.zeros((spans, D), F32)
    mixed = jnp.zeros((spans, D), F32)
    for row in range(rows):
        pick = picked(spot, row * length, length)
        tokens += mm(pick, tokens_ref[row * length : (row + 1) * length, :])
        mixed += mm(pick, mixed_refs[row][...])
    cls_ref[...] = feed_rows(tokens, mixed.astype(BF), *weights, vectors, D, lambda *made: None)


def opening(spans, labels, tokens, mixed, weights, vectors):
    return kernel_call(
        functools.partial(opening_kernel, len(mixed), spans), shape((spans, D), BF), "opening", 4 * PACE, 4
    )(labels, tokens, *mixed, *weights, *vectors)


def feed_kernel(row, width, me_ref, tokens_ref, mixed_ref, *refs):
    weights, vectors = refs[:3], refs[3:10]
    low_ref, n1_ref, f1_ref, hidden_ref, slope_ref, n2_ref, f2_ref, out_ref = refs[10:]
    length = mixed_ref.shape[0]

    def keep(what, *made):
        if what == "first":
            n1_ref[...] = made[0].astype(BF)
            f1_ref[...] = jnp.broadcast_to(made[1], (length, 128))
            low_ref[...] = made[2]
        elif what == "hidden":
            before, share, hidden, at = made
            hidden_ref[:, at : at + width] = hidden
            slope_ref[:, at : at + width] = (
                share + before * jnp.exp(-0.5 * before * before) * DENSITY
            ).astype(BF)
        else:
            n2_ref[...] = made[0].astype(BF)
            f2_ref[...] = jnp.broadcast_to(made[1], (length, 128))

    tokens = tokens_ref[row * length : (row + 1) * length, :]
    out_ref[...] = feed_rows(tokens, mixed_ref[...], *weights, vectors, width, keep)


def feed(row, me, tokens, mixed, weights, vectors, width=768):
    length = mixed.shape[0]
    return kernel_call(
        functools.partial(feed_kernel, row, width),
        [
            near((length, D), BF), near((length, D), BF), near((length, 128), F32), near((length, FF), BF),
            near((length, FF), BF), near((length, D), BF), near((length, 128), F32), shape((length, D), BF),
        ],
        "feed", 9 * PACE, 7, scalars=1,
    )(me, tokens, mixed, *weights, *vectors)


def chain_kernel(
    width, me_ref, branch_ref, second_ref, slope_ref, n1_ref, f1_ref, gain_ref, w_down_ref, w_up_ref, w_out_ref,
    before_ref, first_ref, attn_ref, mixed_ref, sums_ref,
):
    d_middle = second_ref[...]
    branch = branch_ref[...]
    parts = []
    for at in range(0, FF, width):
        d_hidden = mm(branch, w_down_ref[at : at + width, :], NT)
        d_before = (d_hidden * slope_ref[:, at : at + width].astype(F32)).astype(BF)
        before_ref[:, at : at + width] = d_before
        parts.append(jnp.sum(d_before.astype(F32), axis=0, keepdims=True))
        d_middle = d_middle + mm(d_before, w_up_ref[:, at : at + width], NT)
    normed = n1_ref[...].astype(F32)
    d_first = norm_back(d_middle, normed, f1_ref[:, 0:1], row_of(gain_ref))
    d_attn = d_first.astype(BF)
    first_ref[...] = d_first
    attn_ref[...] = d_attn
    mixed_ref[...] = mm(d_attn, w_out_ref[...], NT).astype(BF)
    sums_ref[...] = jnp.concatenate(
        [
            jnp.sum(d_middle * normed, axis=0, keepdims=True),
            jnp.sum(d_middle, axis=0, keepdims=True),
            jnp.sum(d_attn.astype(F32), axis=0, keepdims=True),
        ] + parts + [jnp.zeros((1, D), F32)],
        axis=0,
    )


def chain(me, branch, second, slope, n1, f1, gain_one, w_down, w_up, w_out):
    length = branch.shape[0]
    return kernel_call(
        functools.partial(chain_kernel, D),
        [
            near((length, FF), BF), near((length, D), F32), near((length, D), BF),
            near((length, D), BF), shape((8, D), F32),
        ],
        "chain", 6.6 * PACE, 6, scalars=1,
    )(me, branch, second, slope, n1, f1, gain_one, w_down, w_up, w_out)


def split3(values):
    high = values.astype(BF)
    rest = values - high.astype(F32)
    mid = rest.astype(BF)
    return high, mid, (rest - mid.astype(F32)).astype(BF)


def contrast_kernel(
    size, rows_count, slots_of, me_ref, count_ref, labels_ref, partner_ref, pos_ref, given_ref, gain_ref, *refs
):
    tables, refs = refs[: len(slots_of)], refs[len(slots_of) :]
    groups = [refs[i * rows_count : (i + 1) * rows_count] for i in range(2)]
    n2_refs, f2_refs = groups
    loss_ref, sums_ref = refs[2 * rows_count : 2 * rows_count + 2]
    second_refs = refs[2 * rows_count + 2 : 3 * rows_count + 2]
    branch_refs = refs[3 * rows_count + 2 : 4 * rows_count + 2]
    table = refs[-1]
    spans = tables[0].shape[1]
    total = table.shape[0]
    me = me_ref[0]
    for ref, masks in zip(tables, slots_of):
        for k, mask in enumerate(masks):
            table[pl.ds(pl.multiple_of((mask ^ me) * spans, spans), spans), :] = ref[k].astype(F32)
    rows = table[...].astype(BF)
    scale = 2.0 * D ** (-0.5)
    similar = mm(rows, rows, NT) * scale
    other = lax.broadcasted_iota(jnp.int32, (total, total), 0)
    own = lax.broadcasted_iota(jnp.int32, (total, total), 1)
    similar = jnp.where(own == other, NEG, similar)
    partner = row_of(partner_ref) == other
    top = jnp.max(similar, axis=0, keepdims=True)
    log_rows = top + jnp.log(jnp.sum(jnp.exp(similar - top), axis=0, keepdims=True))
    chosen = jnp.sum(jnp.where(partner, similar, 0.0), axis=0, keepdims=True)
    loss = jnp.sum(log_rows - chosen, axis=1, keepdims=True) / total
    loss_ref[...] = jnp.broadcast_to(loss, loss_ref.shape)
    slope = (jnp.exp(similar - log_rows) - jnp.where(partner, 1.0, 0.0)).astype(BF)
    spot = lax.broadcasted_iota(jnp.int32, (spans, total), 0) + me * spans
    pick = jnp.where(spot == lax.broadcasted_iota(jnp.int32, (spans, total), 1), 1.0, 0.0).astype(BF)
    mine = mm(pick, slope, NT).astype(BF)
    across = mm(pick, slope).astype(BF)
    parts = split3((mm(mine, rows) + mm(across, rows)) * scale)

    starts = span_starts(labels_ref, spans // rows_count)
    slots = given_ref.shape[1]
    per_row = spans // rows_count
    sums = [jnp.zeros((1, D), F32)] * 3
    for row in range(rows_count):
        for at in range(0, n2_refs[row].shape[0], size):
            base = row * n2_refs[row].shape[0] + at
            here = slice(at, at + size)
            place = lax.broadcasted_iota(jnp.int32, (size, slots), 0) + at
            upstream = jnp.zeros((size, D), F32)
            for span in range(row * per_row, (row + 1) * per_row):
                used = lanes((size, slots)) < count_ref[span]
                slot = jnp.where((place == pos_ref[span : span + 1, :]) & used, 1.0, 0.0).astype(BF)
                upstream += mm(slot, given_ref[span])
            hot = picked(starts, base, size)
            upstream += mm(hot, parts[0], TN) + (mm(hot, parts[1], TN) + mm(hot, parts[2], TN))
            normed = n2_refs[row][here, :].astype(F32)
            second = norm_back(upstream, normed, f2_refs[row][here, 0:1], row_of(gain_ref))
            branch = second.astype(BF)
            second_refs[row][here, :] = second
            branch_refs[row][here, :] = branch
            for k, values in enumerate((upstream * normed, upstream, branch.astype(F32))):
                sums[k] = sums[k] + jnp.sum(values, axis=0, keepdims=True)
    sums_ref[...] = jnp.concatenate(sums + [jnp.zeros((5, D), F32)], axis=0)


def contrast(me, count, labels, partner, tables, slots_of, pos, given, n2, f2, gain_two, size=256):
    length = n2[0].shape[0]
    rows = len(n2)
    spans = tables[0].shape[1]
    devices = sum(len(masks) for masks in slots_of)
    made = kernel_call(
        functools.partial(contrast_kernel, size, rows, slots_of),
        [shape((8, 128), F32), shape((8, D), F32)]
        + [near((length, D), F32)] * rows + [near((length, D), BF)] * rows,
        "contrast", 4 * PACE, 6 if devices * spans <= 512 else 40, scalars=2,
        scratch=[VMEM((devices * spans, D), F32)],
    )(me, count, labels, partner, pos, given, gain_two, *tables, *n2, *f2)
    return made[0], made[2 : 2 + rows], made[2 + rows :], made[1]


def merge_kernel(*refs):
    for k, ref in enumerate(refs[:-1]):
        refs[-1][k] = ref[...]


def merge(parts):
    return kernel_call(
        merge_kernel, near((len(parts),) + parts[0].shape, parts[0].dtype), "merge", 0.5 * PACE, 2
    )(*parts)


def tile_place(kind, j):
    order = (0, 1, 2, 3) if kind == 0 else (1, 0, 2, 3)
    out = 0
    for bit in order:
        out = out * 2 + ((j >> bit) & 1)
    return out


def put_tiles(out_ref, kind, values, base):
    rows = values.shape[0] // 16
    for j in range(16):
        out_ref[kind, tile_place(kind, j) ^ base] = values[j * rows : (j + 1) * rows, :]


def cut(start, size):
    return pl.ds(pl.multiple_of(start, 128), size)


def product(lefts, rights, left_cut=None, right_cut=None):
    whole = slice(None)
    return sum(
        mm(left[:, left_cut or whole], right[:, right_cut or whole], TN) for left, right in zip(lefts, rights)
    ).astype(BF)


def grad_down_kernel(rel, rows, me_ref, *refs):
    hidden, branch, out_ref = refs[:rows], refs[rows : 2 * rows], refs[-1]
    for kind in range(2):
        columns = cut(((me_ref[0] ^ rel) * 2 + kind) * D, D)
        put_tiles(out_ref, kind, product(hidden, branch, columns), me_ref[1 + kind])


def grad_up_kernel(rel, rows, me_ref, *refs):
    low, before, out_ref = refs[:rows], refs[rows : 2 * rows], refs[-1]
    for kind in range(2):
        columns = cut(((me_ref[0] ^ rel) * 2 + kind) * D, D)
        put_tiles(out_ref, kind, product(low, before, None, columns), me_ref[1 + kind])


def grad_in_kernel(rel, rows, me_ref, tokens_ref, *refs):
    packed, mixed, attn, out_ref = refs[:rows], refs[rows : 2 * rows], refs[2 * rows : 3 * rows], refs[-1]
    length = packed[0].shape[0]
    half = me_ref[0] ^ rel
    tokens = [tokens_ref.at[r * length : (r + 1) * length, :] for r in range(rows)]
    left = product(tokens, packed, None, cut(half * (3 * D // 2), 3 * D // 2))
    right = product(mixed, attn, None, cut(half * (D // 2), D // 2))
    joined = jnp.concatenate([left, right], axis=1)
    for kind in range(2):
        put_tiles(out_ref, kind, joined[kind * D // 2 : (kind + 1) * D // 2, :], me_ref[1 + kind])


def grad_down(me, hidden, branch, rel):
    return kernel_call(
        functools.partial(grad_down_kernel, rel, len(hidden)), shape((2, 16, 48, D), BF), "grad_down",
        WAIT if rel == 0 else 3.3 * PACE, 6, scalars=1,
    )(me, *hidden, *branch)


def grad_up(me, low, d_before, rel):
    return kernel_call(
        functools.partial(grad_up_kernel, rel, len(low)), shape((2, 16, 48, D), BF), "grad_up",
        WAIT if rel == 0 else 3.3 * PACE, 6, scalars=1,
    )(me, *low, *d_before)


def grad_in(me, tokens, d_packed, mixed, d_attn, rel):
    return kernel_call(
        functools.partial(grad_in_kernel, rel, len(mixed)), shape((2, 16, 24, 2 * D), BF), "grad_in",
        WAIT if rel == 0 else 3.6 * PACE, 8, scalars=1,
    )(me, tokens, *d_packed, *mixed, *d_attn)


def attend_back_kernel(row, pairs, unroll, me_ref, labels_ref, packed_ref, mixed_ref, incoming_ref, lse_ref, *refs):
    out_ref, sums_ref = refs[-2:]
    length = labels_ref.shape[1]
    here = slice(None)
    hot = span_lanes(labels_ref[row : row + 1, :], length)
    lane = lanes((length, 128))
    mark_q = (hot * FAR).astype(BF)
    mark_k = jnp.where(lane < 4, hot - 1.0, jnp.where(lane < 7, -1.0, 0.0)).astype(BF)
    mark_v = jnp.where((lane >= 4) & (lane < 7), -1.0, 0.0).astype(BF)
    none = jnp.zeros((length, 128), BF)
    low_half = lane < HEAD_DIM
    scale = jnp.asarray(HEAD_DIM ** (-0.5), BF)
    sums_ref[...] = jnp.zeros_like(sums_ref)

    def pack3(column, base):
        high, mid, low = (part.astype(F32) for part in split3(column))
        filled = jnp.where(lane == 4, high, jnp.where(lane == 5, mid, jnp.where(lane == 6, low, 0.0)))
        return base + filled.astype(BF)

    def one(p):
        at = pl.multiple_of(p * 128, 128)
        query = packed_ref[here, pl.ds(at, 128)] * scale
        key = packed_ref[here, pl.ds(D + at, 128)]
        keys = jnp.concatenate([key, mark_k], axis=1)
        values = jnp.concatenate([packed_ref[here, pl.ds(2 * D + at, 128)], mark_v], axis=1)
        incoming = incoming_ref[here, pl.ds(at, 128)]
        product = incoming.astype(F32) * mixed_ref[here, pl.ds(at, 128)].astype(F32)
        logs = lse_ref[here, :]
        d_query = jnp.zeros((length, 128), F32)
        d_key = jnp.zeros((length, 128), F32)
        d_value = jnp.zeros((length, 128), F32)
        for half in range(2):
            own = low_half if half == 0 else jnp.logical_not(low_half)
            log_total = jnp.sum(jnp.where(lane == 2 * p + half, logs, 0.0), axis=1, keepdims=True)
            centred = jnp.sum(jnp.where(own, product, 0.0), axis=1, keepdims=True)
            own_query = jnp.where(own, query, none)
            own_incoming = jnp.where(own, incoming, none)
            own_key = jnp.where(own, key, none)
            queries = jnp.concatenate([own_query, pack3(log_total, mark_q)], axis=1)
            grads = jnp.concatenate([own_incoming, pack3(centred, none)], axis=1)
            weights = jnp.exp(mm(keys, queries, NT))
            d_scores = (weights * mm(values, grads, NT)).astype(BF)
            d_value += mm(weights.astype(BF), own_incoming)
            d_key += mm(d_scores, own_query)
            d_query += mm(d_scores, own_key, TN)
        d_query = (d_query * HEAD_DIM ** (-0.5)).astype(BF)
        d_value = d_value.astype(BF)
        out_ref[:, pl.ds(at, 128)] = d_query
        out_ref[:, pl.ds(D + at, 128)] = d_key.astype(BF)
        out_ref[:, pl.ds(2 * D + at, 128)] = d_value
        sums_ref[0:1, pl.ds(at, 128)] = jnp.sum(d_query.astype(F32), axis=0, keepdims=True)
        sums_ref[1:2, pl.ds(at, 128)] = jnp.sum(d_value.astype(F32), axis=0, keepdims=True)

    def some(t, carry):
        for u in range(unroll):
            one(pairs[0] + t * unroll + u)
        return carry

    lax.fori_loop(0, (pairs[1] - pairs[0]) // unroll, some, 0)


def attend_back(row, pairs, me, labels, packed, mixed, incoming, lse, before=None, unroll=3):
    length = labels.shape[1]
    olds = [] if before is None else [before]
    return kernel_call(
        functools.partial(attend_back_kernel, row, pairs, unroll),
        [near((length, 3 * D), BF), shape((8, D), F32)],
        "attend_back", 5 * PACE, 6, scalars=1, aliases={6: 0} if olds else None,
    )(me, labels, packed, mixed, incoming, lse, *olds)


def token_kernel(rows, me_ref, *refs):
    first, packed, w_ref, out_ref = refs[:rows], refs[rows : 2 * rows], refs[-2], refs[-1]
    length = packed[0].shape[0]
    for r in range(rows):
        out_ref[r * length : (r + 1) * length, :] = first[r][...] + mm(packed[r][...], w_ref[...], NT)


def grad_token(me, first, d_packed, w_in):
    rows = len(first)
    return kernel_call(
        functools.partial(token_kernel, rows), shape((rows * first[0].shape[0], D), F32), "grad_token", 5.6 * PACE, 6, scalars=1,
    )(me, *first, *d_packed, w_in)


def halve_kernel(keep_ref, got_ref, *outs):
    for kind in range(2):
        for j in range(16):
            total = keep_ref[kind, j].astype(F32) + got_ref[kind, j].astype(F32)
            outs[2 * kind + j // 8][j % 8] = total.astype(BF)


def halve(keep, got):
    part = (8,) + keep.shape[2:]
    return kernel_call(halve_kernel, [shape(part, BF)] * 4, "halve", 1 * PACE, 4)(keep, got)


SUMS = (16, 17, 10, 8, 9, 11, 2, 0, 1)


def spread_kernel(me_ref, sums_ref, *outs):
    for at, out in zip(SUMS, outs):
        for k in range(out.shape[0] // D):
            out[k * D : (k + 1) * D] = sums_ref[at + k, :]


def spread(me, sums):
    return kernel_call(
        spread_kernel, [shape((FF if at == 11 else D,), F32) for at in SUMS], "spread", 1 * PACE, 2, scalars=1
    )(me, sums)


def join_kernel(me_ref, *refs):
    length = refs[0].shape[0]
    for k, ref in enumerate(refs[:-1]):
        refs[-1][k * length : (k + 1) * length, :] = ref[...]


def join(me, parts):
    length, width = parts[0].shape
    return kernel_call(
        join_kernel, shape((len(parts) * length, width), parts[0].dtype), "join", 1 * PACE, 4, scalars=1
    )(me, *parts)


def place_kernel(rel, name, olds, me_ref, *refs):
    refs = refs[olds:]
    halves = refs[:2]
    outs, holds, sems = (refs[2:4], refs[4:6], refs[6]) if name == "in" else (refs[2:3], refs[3:4], refs[4])
    half = me_ref[0] ^ rel
    copies = []
    for kind, half_ref in enumerate(halves):
        rows = half_ref.shape[1]
        for j in range(16):
            tile = half_ref[tile_place(kind, j) ^ me_ref[1 + kind]].astype(F32)
            at = 0
            for hold in holds:
                hold[kind, j * rows : (j + 1) * rows, :] = tile[:, at : at + hold.shape[2]]
                at += hold.shape[2]
            if j % 8 != 7:
                continue
            size = 8 * rows
            for out, hold in zip(outs, holds):
                high, wide = hold.shape[1:]
                first = (j // 8) * size
                if name == "down":
                    spot = out.at[pl.ds(pl.multiple_of((half * 2 + kind) * high + first, size), size), :]
                elif name == "up":
                    spot = out.at[first : first + size, cut((half * 2 + kind) * wide, wide)]
                else:
                    spot = out.at[kind * high + first : kind * high + first + size, cut(half * wide, wide)]
                near_part = hold.at[kind, first : first + size, :]
                copies.append(pltpu.make_async_copy(near_part, spot, sems.at[len(copies)]))
                copies[-1].start()
    for copy in copies:
        copy.wait()


PLACES = {
    "down": [((FF, D), (D, D))],
    "up": [((D, FF), (D, D))],
    "in": [((D, 3 * D), (D // 2, 3 * D // 2)), ((D, D), (D // 2, D // 2))],
}


def place(name, rel, me, halves, before=None):
    outs = PLACES[name]
    olds = [] if before is None else list(before)
    return kernel_call(
        functools.partial(place_kernel, rel, name, len(olds)),
        [pltpu.HBM(whole, F32) for whole, _ in outs],
        "place", 2 * PACE, 10, scalars=1, far=len(olds), far_outs=range(len(outs)),
        scratch=[VMEM((2,) + part, F32) for _, part in outs] + [pltpu.SemaphoreType.DMA((4 * len(outs),))],
        aliases={1 + i: i for i in range(len(olds))},
    )(me, *(away(old) for old in olds), *halves)


def device_count():
    return lax.axis_size("gr") * lax.axis_size("gc")


def swap(values, mask):
    pairs = [(i, i ^ mask) for i in range(device_count())]
    return lax.ppermute(values, ("gr", "gc"), pairs)


def plus(left, *others):
    total = left.astype(F32)
    for other in others:
        total = total + other.astype(F32)
    return total.astype(BF)


def packed_slot(extra):
    high = lax.reduce_precision(extra, exponent_bits=8, mantissa_bits=7)
    return jnp.concatenate([high, extra - high]).astype(BF)[None]


def swap_with(tiles, extra, mask):
    if extra is None:
        return swap(tiles, mask), None
    got = swap(jnp.concatenate([tiles, packed_slot(extra)]), mask)
    wide = got[-1].astype(F32)
    cut_at = extra.shape[0]
    return got[:-1], extra + (wide[:cut_at] + wide[cut_at:])


def flow(send, keep_of, extra_of=None):
    (got,) = yield (swap(send, 1),)
    one, one_far, two, two_far = halve(keep_of(), got)
    one, two = yield plus(one, swap(one_far, 2)), plus(two, swap(two_far, 4))
    one, two = plus(one[:4], swap(one[4:], 4)), plus(two[:4], swap(two[4:], 2))
    ours, others = yield jnp.stack([one[:2], two[:2]], axis=1), jnp.stack([one[2:], two[2:]], axis=1)
    (both,) = yield (plus(ours, swap(others, 8)),)
    own = plus(both[0], swap(both[1], 16))
    mask = 32
    while mask < device_count():
        own = plus(own, swap(own, mask))
        mask *= 2
    (own,) = yield (own,)
    extra = None if extra_of is None else extra_of()
    mask = 32
    while extra is not None and mask < device_count():
        extra = extra + swap(extra, mask)
        mask *= 2
    got, extra = swap_with(own, extra, 16)
    both, extra = yield jnp.concatenate([own, got]), extra
    got, extra = swap_with(both, extra, 8)
    both = jnp.concatenate([both, got])
    one, two, extra = yield both[::2], both[1::2], extra
    got, extra = swap_with(one, extra, 4)
    one, two, extra = yield jnp.concatenate([one, got]), jnp.concatenate([two, swap(two, 2)]), extra
    got, extra = swap_with(one, extra, 2)
    one, two, extra = yield jnp.concatenate([one, got]), jnp.concatenate([two, swap(two, 4)]), extra
    return (one, two), (swap(one, 1), swap(two, 1)), extra


def flow_near(sums):
    yield (sums + swap(sums, 1),)


class Line:
    def __init__(self, steps, made):
        self.steps, self.made = steps, made
        self.result = None
        self.opened = False

    def go(self, made):
        try:
            self.made = self.steps(*made) if not self.opened else self.steps.send(made)
            if not self.opened:
                self.steps, self.made = self.made, next(self.made)
            self.opened = True
        except StopIteration as end:
            self.result = self.made = end.value


class Rounds:
    def __init__(self, me, token):
        self.me, self.token, self.going = me, token, []

    def begin(self, lines):
        kept = [line.made for line in self.going]
        made, kept, token = lax.optimization_barrier(([line.made for line in lines], kept, self.token))
        self.token = (kept, token)
        for line, arrays in zip(self.going, kept):
            line.made = arrays
            if line.result is not None:
                line.result = arrays
        for line, arrays in zip(lines, made):
            line.go(arrays if line not in self.going else line.made)
        self.going = lines

    def work(self, call, *args, token=lambda made: made):
        me, _ = lax.optimization_barrier((self.me, self.token))
        made = call(me, *args)
        self.token = token(made)
        return made


def bits_of(value, order):
    out = jnp.zeros_like(value)
    for bit in order:
        out = out * 2 + ((value >> bit) & 1)
    return out


def per_device(
    tokens, span_ids, mlm_pos, mlm_count, mlm_grad, positive, w_in, b_query, b_value, w_out, b_out,
    ln1_gain, ln1_bias, w_up, b_up, w_down, b_down, ln2_gain, ln2_bias,
):
    rows, length = span_ids.shape
    spans = mlm_pos.shape[0]
    index = lax.axis_index("gr") * lax.axis_size("gc") + lax.axis_index("gc")
    chip = (index >> 1) & 15
    me = jnp.stack(
        [index & 1, bits_of(chip, (0, 1, 2, 3)), bits_of(chip, (1, 0, 2, 3))]
    ).astype(jnp.int32)
    where = index.astype(jnp.int32)[None]
    me, where, b_query = lax.optimization_barrier((me, where, b_query))
    weights = (w_out, w_up, w_down)
    vectors = (b_out, ln1_gain, ln1_bias, b_up, b_down, ln2_gain, ln2_bias)

    packed, mixed, lse, weights = attend(span_ids, tokens, w_in, b_query, b_value, weights)
    cls = opening(spans, span_ids, tokens, mixed, weights, vectors)
    cls, here = lax.optimization_barrier((cls, me))
    masks = (0, 8, 16, 24)
    parts = [cls] + [swap(cls, m) for m in masks[1:]]
    made = [feed(0, here, tokens, mixed[0], weights, vectors)]
    table = merge(parts)
    table, here, _ = lax.optimization_barrier((table, me, made[0][1]))
    tables = [table] + [swap(table, m) for m in range(1, 8)]
    slots_of = [tuple(m ^ k for k in masks) for m in range(8)]
    made.append(feed(1, here, tokens, mixed[1], weights, vectors))
    bit = 32
    while bit < device_count():
        table, masks = jnp.concatenate(tables), sum(slots_of, ())
        tables = [table, swap(table, bit)]
        slots_of = [masks, tuple(m ^ bit for m in masks)]
        bit *= 2
    low, n1, f1, hidden, slope, n2, f2, layer_out = zip(*made)
    loss, second, branch, sums_two = contrast(
        where, mlm_count, span_ids, positive, tables, slots_of, mlm_pos, mlm_grad, n2, f2, ln2_gain
    )

    order = Rounds(me, sums_two)
    lines, keeps, links, sums_in, sides = {}, {}, [None] * rows, [], {}
    d_packed = [None] * rows
    part = [0] * rows

    def gradient(name, call, *args):
        if name not in lines:
            send = order.work(functools.partial(call, rel=1), *args)
            extra_of = (lambda: lines["S"].made[0]) if name == "D" else None
            lines[name] = Line(functools.partial(flow, keep_of=lambda: keeps[name], extra_of=extra_of), (send,))
        else:
            keeps[name] = order.work(functools.partial(call, rel=0), *args)

    def link(row):
        links[row] = order.work(
            chain, branch[row], second[row], slope[row], n1[row], f1[row], ln1_gain,
            weights[2], weights[1], weights[0], token=lambda made: made[4],
        )

    def back(row):
        pairs = (part[row] * HEADS // 4, (part[row] + 1) * HEADS // 4)
        d_packed[row], sums = order.work(
            functools.partial(attend_back, row, pairs),
            span_ids, packed[row], mixed[row], links[row][3], lse[row], d_packed[row],
            token=lambda made: made[1],
        )
        part[row] += 1
        sums_in.append(sums)

    def settle(name, rel):
        call = functools.partial(place, {"D": "down", "U": "up", "I": "in"}[name], rel)
        sides[name] = order.work(call, lines[name].result[rel], sides.get(name))

    for going, events in PLAN:
        if "S" in going:
            sums_one = sum(made[4] for made in links)
            lines["S"] = Line(flow_near, (jnp.concatenate([sums_two, sums_one, sum(sums_in)]),))
        order.begin([lines[name] for name in going])
        for event in events:
            if event == "gd":
                gradient("D", grad_down, hidden, branch)
            elif event == "gu":
                gradient("U", grad_up, low, [made[0] for made in links])
            elif event == "gi":
                gradient("I", grad_in, tokens, d_packed, mixed, [made[2] for made in links])
            elif event == "gt":
                sides["T"] = order.work(grad_token, [made[1] for made in links], d_packed, w_in)
            elif event == "jo":
                sides["J"] = order.work(join, layer_out)
            elif event == "ou":
                sides["S"] = order.work(spread, lines["D"].result[2])
            elif event[:2] == "ch":
                link(int(event[2]))
            elif event[:2] == "ab":
                back(int(event[2]))
            else:
                settle(event[1], int(event[2]))
    grad_tokens, g_down, g_up, g_in, small = (sides[name] for name in "TDUIS")

    return (
        sides["J"], grad_tokens, g_in[0], small[0], small[1], g_in[1], *small[2:5], g_up[0], small[5], g_down[0],
        *small[6:], loss[0, 0],
    )


PLAN = (
    ("", ("gd",)),
    ("D", ("gd",)),
    ("D", ("ch0", "ch1", "gu",)),
    ("DU", ("gu", "ab0", "ab0",)),
    ("DU", ("ab1", "ab1", "gi",)),
    ("DUIS", ("gi",)),
    ("DUI", ("gt",)),
    ("DUI", ()),
    ("DUI", ()),
    ("DUI", ()),
    ("DUI", ()),
    ("UI", ("pD0",)),
    ("UI", ("pD1",)),
    ("I", ("pU0", "pU1", "ou", "jo",)),
    ("I", ("pI0",)),
    ("", ("pI1",)),
)


def solution(mesh):
    split = P(("gr", "gc"))
    return jax.shard_map(
        per_device,
        mesh=mesh,
        in_specs=(split,) * 5 + (P(),) * 14,
        out_specs=(split, split) + (P(),) * 14,
        check_vma=False,
    )
```

```python
import functools
import jax
import jax.numpy as jnp
from jax import lax
from jax.experimental import pallas as pl
from jax.experimental.pallas import tpu as pltpu
from jax.sharding import PartitionSpec as P

D = 768
HEADS = 12
HEAD_DIM = 64
FF = 3072
BF = jnp.bfloat16
F32 = jnp.float32
EPS = 1e-12
FAR = 1e30
NEG = -1e30
HALF_ROOT = 0.7071067811865476
DENSITY = 0.3989422804014327
NN = (((1,), (0,)), ((), ()))
NT = (((1,), (1,)), ((), ()))
TN = (((0,), (0,)), ((), ()))
MIB = 1024 * 1024
PACE = 0.05
WAIT = 0.05
SMEM = pltpu.SMEM
VMEM = pltpu.VMEM


def shape(dims, dtype):
    return jax.ShapeDtypeStruct(dims, dtype)


def near(dims, dtype):
    return VMEM(dims, dtype)


def away(array):
    return pltpu.with_memory_space_constraint(array, pltpu.HBM)


def kernel_call(body, outs, name, us, limit, scalars=0, far=0, far_outs=(), scratch=(), aliases=None):
    def place(i):
        if i < scalars:
            return pl.BlockSpec(memory_space=SMEM)
        return pl.BlockSpec(memory_space=pltpu.HBM if i < scalars + far else VMEM)

    def call(*args):
        return pl.pallas_call(
            body,
            in_specs=[place(i) for i in range(len(args))],
            out_specs=[pl.BlockSpec(memory_space=pltpu.HBM if i in far_outs else VMEM) for i in range(len(outs))]
            if isinstance(outs, list)
            else pl.BlockSpec(memory_space=VMEM),
            out_shape=outs,
            scratch_shapes=list(scratch),
            input_output_aliases=aliases or {},
            compiler_params=pltpu.CompilerParams(vmem_limit_bytes=limit * MIB),
            cost_estimate=pl.CostEstimate(
                flops=int(us * 1.1e9), bytes_accessed=int(us * 3e6), transcendentals=0
            ),
            name=name,
        )(*args)

    return call


def mm(left, right, dims=NN):
    return lax.dot_general(left, right, dims, preferred_element_type=F32)


def lanes(dims):
    return lax.broadcasted_iota(jnp.int32, dims, len(dims) - 1)


def row_of(ref):
    return ref[...][None, :]


def normalize(values):
    centre = values - jnp.mean(values, axis=-1, keepdims=True)
    factor = lax.rsqrt(jnp.mean(centre * centre, axis=-1, keepdims=True) + EPS)
    return centre * factor, factor


def norm_back(incoming, normed, factor, gain):
    scaled = incoming * gain
    return factor * (
        scaled
        - jnp.mean(scaled, axis=-1, keepdims=True)
        - normed * jnp.mean(scaled * normed, axis=-1, keepdims=True)
    )


def span_lanes(labels, length):
    rows = lax.broadcasted_iota(jnp.int32, (128, length), 0)
    return jnp.where(rows == jnp.broadcast_to(labels, (128, length)), 1.0, 0.0).T


def attend_kernel(
    unroll, rows, labels_far, tokens_far, w_far, bq_far, bv_far, w_out_far, w_up_far, w_down_far, *refs
):
    packed_far, mixed, lse = refs[:rows], refs[rows : 2 * rows], refs[2 * rows : 3 * rows]
    w_out_ref, w_up_ref, w_down_ref = refs[3 * rows : 3 * rows + 3]
    labels_ref, tokens_ref, w_ref, bq_ref, bv_ref = refs[3 * rows + 3 : 3 * rows + 8]
    packed, sems = refs[3 * rows + 8 : 4 * rows + 8], refs[-1]
    length = packed[0].shape[0]
    columns = [slice(at, at + D) for at in range(0, 3 * D, D)]
    pairs = [(tokens_far, tokens_ref), (bq_far, bq_ref), (bv_far, bv_ref), (labels_far, labels_ref)]
    pairs += [(w_far.at[:, c], w_ref.at[:, c]) for c in columns]
    pairs += [(w_out_far, w_out_ref), (w_up_far, w_up_ref), (w_down_far, w_down_ref)]
    pairs += list(zip(packed, packed_far))
    copies = [pltpu.make_async_copy(*pair, sems.at[i]) for i, pair in enumerate(pairs)]
    for copy in copies[:10]:
        copy.start()
    scale = jnp.asarray(HEAD_DIM ** (-0.5), BF)
    for copy in copies[:4]:
        copy.wait()
    for k, c in enumerate(columns):
        copies[4 + k].wait()
        for row in range(rows):
            made = mm(tokens_ref[row * length : (row + 1) * length, :], w_ref[:, c])
            bias = (row_of(bq_ref), 0.0, row_of(bv_ref))[k]
            packed[row][:, c] = (made + bias).astype(BF)
    for copy in copies[10:]:
        copy.start()
    lane = lanes((length, 128))
    low_half = lane < HEAD_DIM

    for row in range(rows):
        hot = span_lanes(labels_ref[row : row + 1, :], length)
        mark_q = (hot * FAR).astype(BF)
        mark_k = jnp.where(lane < 4, hot - 1.0, 0.0).astype(BF)
        packed_ref, mixed_ref, lse_ref = packed[row], mixed[row], lse[row]
        lse_ref[...] = jnp.zeros_like(lse_ref)

        def one(p):
            at = pl.multiple_of(p * 128, 128)
            query = packed_ref[:, pl.ds(at, 128)] * scale
            keys = jnp.concatenate([packed_ref[:, pl.ds(D + at, 128)], mark_k], axis=1)
            values = packed_ref[:, pl.ds(2 * D + at, 128)]
            outs = []
            logs = lse_ref[...]
            for half in range(2):
                own = low_half if half == 0 else jnp.logical_not(low_half)
                queries = jnp.concatenate(
                    [jnp.where(own, query, jnp.zeros_like(query)), mark_q], axis=1
                )
                scores = mm(queries, keys, NT)
                top = jnp.max(scores, axis=1, keepdims=True)
                grown = jnp.exp(scores - top)
                total = jnp.sum(grown, axis=1, keepdims=True)
                outs.append(mm(grown.astype(BF), values) * (1.0 / total))
                logs = jnp.where(lane == 2 * p + half, top + jnp.log(total), logs)
            lse_ref[...] = logs
            mixed_ref[:, pl.ds(at, 128)] = jnp.where(low_half, outs[0], outs[1]).astype(BF)

        def some(t, carry):
            for u in range(unroll):
                one(t * unroll + u)
            return carry

        lax.fori_loop(0, HEADS // 2 // unroll, some, 0)
    for copy in copies[7:]:
        copy.wait()


def attend(labels, tokens, w_in, b_query, b_value, weights, unroll=3):
    rows, length = labels.shape
    made = kernel_call(
        functools.partial(attend_kernel, unroll, rows),
        [pltpu.HBM((length, 3 * D), BF)] * rows + [near((length, D), BF)] * rows
        + [near((length, 128), F32)] * rows + [near(w.shape, BF) for w in weights],
        "attend", 15 * PACE, 20, far=8, far_outs=range(rows),
        scratch=[VMEM(labels.shape, jnp.int32), VMEM(tokens.shape, BF), VMEM(w_in.shape, BF), VMEM((D,), F32), VMEM((D,), F32)]
        + [VMEM((length, 3 * D), BF)] * rows + [pltpu.SemaphoreType.DMA((10 + rows,))],
    )(*(away(x) for x in (labels, tokens, w_in, b_query, b_value) + tuple(weights)))
    return made[:rows], made[rows : 2 * rows], made[2 * rows : 3 * rows], made[3 * rows :]


def span_starts(labels_ref, per_row):
    rows, length = labels_ref.shape
    out = []
    for row in range(rows):
        labels = jnp.broadcast_to(labels_ref[row : row + 1, :], (per_row, length))
        level = lax.broadcasted_iota(jnp.int32, (per_row, length), 0)
        below = jnp.sum(jnp.where(labels < level, 1.0, 0.0), axis=1, keepdims=True)
        out.append(below.astype(jnp.int32) + row * length)
    return jnp.concatenate(out, axis=0)


def picked(spot, at, size):
    place = lax.broadcasted_iota(jnp.int32, (spot.shape[0], size), 1) + at
    return jnp.where(place == spot, 1.0, 0.0).astype(BF)


def feed_rows(tokens, mixed, w_out_ref, w_up_ref, w_down_ref, vectors, width, keep):
    b_out, gain_one, bias_one, b_up, b_down, gain_two, bias_two = (row_of(ref) for ref in vectors)
    first = tokens.astype(F32) + mm(mixed, w_out_ref[...]) + b_out
    normed, factor = normalize(first)
    middle = normed * gain_one + bias_one
    low = middle.astype(BF)
    keep("first", normed, factor, low)
    total = middle + b_down
    for at in range(0, FF, width):
        before = mm(low, w_up_ref[:, at : at + width]) + b_up[:, at : at + width]
        share = 0.5 * (1.0 + lax.erf(before * HALF_ROOT))
        hidden = (before * share).astype(BF)
        keep("hidden", before, share, hidden, at)
        total = total + mm(hidden, w_down_ref[at : at + width, :])
    normed, factor = normalize(total)
    keep("second", normed, factor)
    return (normed * gain_two + bias_two).astype(BF)


def opening_kernel(rows, spans, labels_ref, tokens_ref, *refs):
    mixed_refs, weights, vectors, cls_ref = refs[:rows], refs[rows : rows + 3], refs[rows + 3 : -1], refs[-1]
    length = labels_ref.shape[1]
    spot = span_starts(labels_ref, spans // rows)
    tokens = jnp.zeros((spans, D), F32)
    mixed = jnp.zeros((spans, D), F32)
    for row in range(rows):
        pick = picked(spot, row * length, length)
        tokens += mm(pick, tokens_ref[row * length : (row + 1) * length, :])
        mixed += mm(pick, mixed_refs[row][...])
    cls_ref[...] = feed_rows(tokens, mixed.astype(BF), *weights, vectors, D, lambda *made: None)


def opening(spans, labels, tokens, mixed, weights, vectors):
    return kernel_call(
        functools.partial(opening_kernel, len(mixed), spans), shape((spans, D), BF), "opening", 4 * PACE, 4
    )(labels, tokens, *mixed, *weights, *vectors)


def feed_kernel(row, width, me_ref, tokens_ref, mixed_ref, *refs):
    weights, vectors = refs[:3], refs[3:10]
    low_ref, n1_ref, f1_ref, hidden_ref, slope_ref, n2_ref, f2_ref, out_ref = refs[10:]
    length = mixed_ref.shape[0]

    def keep(what, *made):
        if what == "first":
            n1_ref[...] = made[0].astype(BF)
            f1_ref[...] = jnp.broadcast_to(made[1], (length, 128))
            low_ref[...] = made[2]
        elif what == "hidden":
            before, share, hidden, at = made
            hidden_ref[:, at : at + width] = hidden
            slope_ref[:, at : at + width] = (
                share + before * jnp.exp(-0.5 * before * before) * DENSITY
            ).astype(BF)
        else:
            n2_ref[...] = made[0].astype(BF)
            f2_ref[...] = jnp.broadcast_to(made[1], (length, 128))

    tokens = tokens_ref[row * length : (row + 1) * length, :]
    out_ref[...] = feed_rows(tokens, mixed_ref[...], *weights, vectors, width, keep)


def feed(row, me, tokens, mixed, weights, vectors, width=768):
    length = mixed.shape[0]
    return kernel_call(
        functools.partial(feed_kernel, row, width),
        [
            near((length, D), BF), near((length, D), BF), near((length, 128), F32), near((length, FF), BF),
            near((length, FF), BF), near((length, D), BF), near((length, 128), F32), shape((length, D), BF),
        ],
        "feed", 9 * PACE, 7, scalars=1,
    )(me, tokens, mixed, *weights, *vectors)


def chain_kernel(
    width, me_ref, branch_ref, second_ref, slope_ref, n1_ref, f1_ref, gain_ref, w_down_ref, w_up_ref, w_out_ref,
    before_ref, first_ref, attn_ref, mixed_ref, sums_ref,
):
    d_middle = second_ref[...]
    branch = branch_ref[...]
    parts = []
    for at in range(0, FF, width):
        d_hidden = mm(branch, w_down_ref[at : at + width, :], NT)
        d_before = (d_hidden * slope_ref[:, at : at + width].astype(F32)).astype(BF)
        before_ref[:, at : at + width] = d_before
        parts.append(jnp.sum(d_before.astype(F32), axis=0, keepdims=True))
        d_middle = d_middle + mm(d_before, w_up_ref[:, at : at + width], NT)
    normed = n1_ref[...].astype(F32)
    d_first = norm_back(d_middle, normed, f1_ref[:, 0:1], row_of(gain_ref))
    d_attn = d_first.astype(BF)
    first_ref[...] = d_first
    attn_ref[...] = d_attn
    mixed_ref[...] = mm(d_attn, w_out_ref[...], NT).astype(BF)
    sums_ref[...] = jnp.concatenate(
        [
            jnp.sum(d_middle * normed, axis=0, keepdims=True),
            jnp.sum(d_middle, axis=0, keepdims=True),
            jnp.sum(d_attn.astype(F32), axis=0, keepdims=True),
        ] + parts + [jnp.zeros((1, D), F32)],
        axis=0,
    )


def chain(me, branch, second, slope, n1, f1, gain_one, w_down, w_up, w_out):
    length = branch.shape[0]
    return kernel_call(
        functools.partial(chain_kernel, D),
        [
            near((length, FF), BF), near((length, D), F32), near((length, D), BF),
            near((length, D), BF), shape((8, D), F32),
        ],
        "chain", 6.6 * PACE, 6, scalars=1,
    )(me, branch, second, slope, n1, f1, gain_one, w_down, w_up, w_out)


def split3(values):
    high = values.astype(BF)
    rest = values - high.astype(F32)
    mid = rest.astype(BF)
    return high, mid, (rest - mid.astype(F32)).astype(BF)


def contrast_kernel(
    size, rows_count, slots_of, me_ref, count_ref, labels_ref, partner_ref, pos_ref, given_ref, gain_ref, *refs
):
    tables, refs = refs[: len(slots_of)], refs[len(slots_of) :]
    groups = [refs[i * rows_count : (i + 1) * rows_count] for i in range(2)]
    n2_refs, f2_refs = groups
    loss_ref, sums_ref = refs[2 * rows_count : 2 * rows_count + 2]
    second_refs = refs[2 * rows_count + 2 : 3 * rows_count + 2]
    branch_refs = refs[3 * rows_count + 2 : 4 * rows_count + 2]
    table = refs[-1]
    spans = tables[0].shape[1]
    total = table.shape[0]
    me = me_ref[0]
    for ref, masks in zip(tables, slots_of):
        for k, mask in enumerate(masks):
            table[pl.ds(pl.multiple_of((mask ^ me) * spans, spans), spans), :] = ref[k].astype(F32)
    rows = table[...].astype(BF)
    scale = 2.0 * D ** (-0.5)
    similar = mm(rows, rows, NT) * scale
    other = lax.broadcasted_iota(jnp.int32, (total, total), 0)
    own = lax.broadcasted_iota(jnp.int32, (total, total), 1)
    similar = jnp.where(own == other, NEG, similar)
    partner = row_of(partner_ref) == other
    top = jnp.max(similar, axis=0, keepdims=True)
    log_rows = top + jnp.log(jnp.sum(jnp.exp(similar - top), axis=0, keepdims=True))
    chosen = jnp.sum(jnp.where(partner, similar, 0.0), axis=0, keepdims=True)
    loss = jnp.sum(log_rows - chosen, axis=1, keepdims=True) / total
    loss_ref[...] = loss
    slope = (jnp.exp(similar - log_rows) - jnp.where(partner, 1.0, 0.0)).astype(BF)
    spot = lax.broadcasted_iota(jnp.int32, (spans, total), 0) + me * spans
    pick = jnp.where(spot == lax.broadcasted_iota(jnp.int32, (spans, total), 1), 1.0, 0.0).astype(BF)
    mine = mm(pick, slope, NT).astype(BF)
    across = mm(pick, slope).astype(BF)
    parts = split3((mm(mine, rows) + mm(across, rows)) * scale)

    starts = span_starts(labels_ref, spans // rows_count)
    slots = given_ref.shape[1]
    per_row = spans // rows_count
    sums = [jnp.zeros((1, D), F32)] * 3
    for row in range(rows_count):
        for at in range(0, n2_refs[row].shape[0], size):
            base = row * n2_refs[row].shape[0] + at
            here = slice(at, at + size)
            place = lax.broadcasted_iota(jnp.int32, (size, slots), 0) + at
            upstream = jnp.zeros((size, D), F32)
            for span in range(row * per_row, (row + 1) * per_row):
                used = lanes((size, slots)) < count_ref[span]
                slot = jnp.where((place == pos_ref[span : span + 1, :]) & used, 1.0, 0.0).astype(BF)
                upstream += mm(slot, given_ref[span])
            hot = picked(starts, base, size)
            upstream += mm(hot, parts[0], TN) + (mm(hot, parts[1], TN) + mm(hot, parts[2], TN))
            normed = n2_refs[row][here, :].astype(F32)
            second = norm_back(upstream, normed, f2_refs[row][here, 0:1], row_of(gain_ref))
            branch = second.astype(BF)
            second_refs[row][here, :] = second
            branch_refs[row][here, :] = branch
            for k, values in enumerate((upstream * normed, upstream, branch.astype(F32))):
                sums[k] = sums[k] + jnp.sum(values, axis=0, keepdims=True)
    sums_ref[...] = jnp.concatenate(sums + [jnp.zeros((5, D), F32)], axis=0)


def contrast(me, count, labels, partner, tables, slots_of, pos, given, n2, f2, gain_two, size=256):
    length = n2[0].shape[0]
    rows = len(n2)
    spans = tables[0].shape[1]
    devices = sum(len(masks) for masks in slots_of)
    made = kernel_call(
        functools.partial(contrast_kernel, size, rows, slots_of),
        [shape((1, 1), F32), shape((8, D), F32)]
        + [near((length, D), F32)] * rows + [near((length, D), BF)] * rows,
        "contrast", 4 * PACE, 6 if devices * spans <= 512 else 40, scalars=2,
        scratch=[VMEM((devices * spans, D), F32)],
    )(me, count, labels, partner, pos, given, gain_two, *tables, *n2, *f2)
    return made[0], made[2 : 2 + rows], made[2 + rows :], made[1]


def merge_kernel(*refs):
    for k, ref in enumerate(refs[:-1]):
        refs[-1][k] = ref[...]


def merge(parts):
    return kernel_call(
        merge_kernel, near((len(parts),) + parts[0].shape, parts[0].dtype), "merge", 0.5 * PACE, 2
    )(*parts)


def tile_place(kind, j):
    order = (0, 1, 2, 3) if kind == 0 else (1, 0, 2, 3)
    out = 0
    for bit in order:
        out = out * 2 + ((j >> bit) & 1)
    return out


def put_tiles(out_ref, kind, values, base):
    rows = values.shape[0] // 16
    for j in range(16):
        out_ref[kind, tile_place(kind, j) ^ base] = values[j * rows : (j + 1) * rows, :]


def cut(start, size):
    return pl.ds(pl.multiple_of(start, 128), size)


def product(lefts, rights, left_cut=None, right_cut=None):
    whole = slice(None)
    return sum(
        mm(left[:, left_cut or whole], right[:, right_cut or whole], TN) for left, right in zip(lefts, rights)
    ).astype(BF)


def grad_down_kernel(rel, rows, me_ref, *refs):
    hidden, branch, out_ref = refs[:rows], refs[rows : 2 * rows], refs[-1]
    for kind in range(2):
        columns = cut(((me_ref[0] ^ rel) * 2 + kind) * D, D)
        put_tiles(out_ref, kind, product(hidden, branch, columns), me_ref[1 + kind])


def grad_up_kernel(rel, rows, me_ref, *refs):
    low, before, out_ref = refs[:rows], refs[rows : 2 * rows], refs[-1]
    for kind in range(2):
        columns = cut(((me_ref[0] ^ rel) * 2 + kind) * D, D)
        put_tiles(out_ref, kind, product(low, before, None, columns), me_ref[1 + kind])


def grad_in_kernel(rel, rows, me_ref, tokens_ref, *refs):
    packed, mixed, attn, out_ref = refs[:rows], refs[rows : 2 * rows], refs[2 * rows : 3 * rows], refs[-1]
    length = packed[0].shape[0]
    half = me_ref[0] ^ rel
    tokens = [tokens_ref.at[r * length : (r + 1) * length, :] for r in range(rows)]
    left = product(tokens, packed, None, cut(half * (3 * D // 2), 3 * D // 2))
    right = product(mixed, attn, None, cut(half * (D // 2), D // 2))
    joined = jnp.concatenate([left, right], axis=1)
    for kind in range(2):
        put_tiles(out_ref, kind, joined[kind * D // 2 : (kind + 1) * D // 2, :], me_ref[1 + kind])


def grad_down(me, hidden, branch, rel):
    return kernel_call(
        functools.partial(grad_down_kernel, rel, len(hidden)), shape((2, 16, 48, D), BF), "grad_down",
        WAIT if rel == 0 else 3.3 * PACE, 6, scalars=1,
    )(me, *hidden, *branch)


def grad_up(me, low, d_before, rel):
    return kernel_call(
        functools.partial(grad_up_kernel, rel, len(low)), shape((2, 16, 48, D), BF), "grad_up",
        WAIT if rel == 0 else 3.3 * PACE, 6, scalars=1,
    )(me, *low, *d_before)


def grad_in(me, tokens, d_packed, mixed, d_attn, rel):
    return kernel_call(
        functools.partial(grad_in_kernel, rel, len(mixed)), shape((2, 16, 24, 2 * D), BF), "grad_in",
        WAIT if rel == 0 else 3.6 * PACE, 8, scalars=1,
    )(me, tokens, *d_packed, *mixed, *d_attn)


def attend_back_kernel(row, pairs, unroll, me_ref, labels_ref, packed_ref, mixed_ref, incoming_ref, lse_ref, *refs):
    out_ref, sums_ref = refs[-2:]
    length = labels_ref.shape[1]
    here = slice(None)
    hot = span_lanes(labels_ref[row : row + 1, :], length)
    lane = lanes((length, 128))
    mark_q = (hot * FAR).astype(BF)
    mark_k = jnp.where(lane < 4, hot - 1.0, jnp.where(lane < 7, -1.0, 0.0)).astype(BF)
    mark_v = jnp.where((lane >= 4) & (lane < 7), -1.0, 0.0).astype(BF)
    none = jnp.zeros((length, 128), BF)
    low_half = lane < HEAD_DIM
    scale = jnp.asarray(HEAD_DIM ** (-0.5), BF)
    sums_ref[...] = jnp.zeros_like(sums_ref)

    def pack3(column, base):
        high, mid, low = (part.astype(F32) for part in split3(column))
        filled = jnp.where(lane == 4, high, jnp.where(lane == 5, mid, jnp.where(lane == 6, low, 0.0)))
        return base + filled.astype(BF)

    def one(p):
        at = pl.multiple_of(p * 128, 128)
        query = packed_ref[here, pl.ds(at, 128)] * scale
        key = packed_ref[here, pl.ds(D + at, 128)]
        keys = jnp.concatenate([key, mark_k], axis=1)
        values = jnp.concatenate([packed_ref[here, pl.ds(2 * D + at, 128)], mark_v], axis=1)
        incoming = incoming_ref[here, pl.ds(at, 128)]
        product = incoming.astype(F32) * mixed_ref[here, pl.ds(at, 128)].astype(F32)
        logs = lse_ref[here, :]
        d_query = jnp.zeros((length, 128), F32)
        d_key = jnp.zeros((length, 128), F32)
        d_value = jnp.zeros((length, 128), F32)
        for half in range(2):
            own = low_half if half == 0 else jnp.logical_not(low_half)
            log_total = jnp.sum(jnp.where(lane == 2 * p + half, logs, 0.0), axis=1, keepdims=True)
            centred = jnp.sum(jnp.where(own, product, 0.0), axis=1, keepdims=True)
            own_query = jnp.where(own, query, none)
            own_incoming = jnp.where(own, incoming, none)
            own_key = jnp.where(own, key, none)
            queries = jnp.concatenate([own_query, pack3(log_total, mark_q)], axis=1)
            grads = jnp.concatenate([own_incoming, pack3(centred, none)], axis=1)
            weights = jnp.exp(mm(keys, queries, NT))
            d_scores = (weights * mm(values, grads, NT)).astype(BF)
            d_value += mm(weights.astype(BF), own_incoming)
            d_key += mm(d_scores, own_query)
            d_query += mm(d_scores, own_key, TN)
        d_query = (d_query * HEAD_DIM ** (-0.5)).astype(BF)
        d_value = d_value.astype(BF)
        out_ref[:, pl.ds(at, 128)] = d_query
        out_ref[:, pl.ds(D + at, 128)] = d_key.astype(BF)
        out_ref[:, pl.ds(2 * D + at, 128)] = d_value
        sums_ref[0:1, pl.ds(at, 128)] = jnp.sum(d_query.astype(F32), axis=0, keepdims=True)
        sums_ref[1:2, pl.ds(at, 128)] = jnp.sum(d_value.astype(F32), axis=0, keepdims=True)

    def some(t, carry):
        for u in range(unroll):
            one(pairs[0] + t * unroll + u)
        return carry

    lax.fori_loop(0, (pairs[1] - pairs[0]) // unroll, some, 0)


def attend_back(row, pairs, me, labels, packed, mixed, incoming, lse, before=None, unroll=3):
    length = labels.shape[1]
    olds = [] if before is None else [before]
    return kernel_call(
        functools.partial(attend_back_kernel, row, pairs, unroll),
        [near((length, 3 * D), BF), shape((8, D), F32)],
        "attend_back", 5 * PACE, 6, scalars=1, aliases={6: 0} if olds else None,
    )(me, labels, packed, mixed, incoming, lse, *olds)


def token_kernel(rows, me_ref, *refs):
    first, packed, w_ref, out_ref = refs[:rows], refs[rows : 2 * rows], refs[-2], refs[-1]
    length = packed[0].shape[0]
    for r in range(rows):
        out_ref[r * length : (r + 1) * length, :] = first[r][...] + mm(packed[r][...], w_ref[...], NT)


def grad_token(me, first, d_packed, w_in):
    rows = len(first)
    return kernel_call(
        functools.partial(token_kernel, rows), shape((rows * first[0].shape[0], D), F32), "grad_token", 5.6 * PACE, 6, scalars=1,
    )(me, *first, *d_packed, w_in)


def halve_kernel(keep_ref, got_ref, *outs):
    for kind in range(2):
        for j in range(16):
            total = keep_ref[kind, j].astype(F32) + got_ref[kind, j].astype(F32)
            outs[2 * kind + j // 8][j % 8] = total.astype(BF)


def halve(keep, got):
    part = (8,) + keep.shape[2:]
    return kernel_call(halve_kernel, [shape(part, BF)] * 4, "halve", 1 * PACE, 4)(keep, got)


SUMS = (16, 17, 10, 8, 9, 11, 2, 0, 1)


def spread_kernel(me_ref, sums_ref, *outs):
    for at, out in zip(SUMS, outs):
        for k in range(out.shape[0] // D):
            out[k * D : (k + 1) * D] = sums_ref[at + k, :]


def spread(me, sums):
    return kernel_call(
        spread_kernel, [shape((FF if at == 11 else D,), F32) for at in SUMS], "spread", 1 * PACE, 2, scalars=1
    )(me, sums)


def join_kernel(me_ref, *refs):
    length = refs[0].shape[0]
    for k, ref in enumerate(refs[:-1]):
        refs[-1][k * length : (k + 1) * length, :] = ref[...]


def join(me, parts):
    length, width = parts[0].shape
    return kernel_call(
        join_kernel, shape((len(parts) * length, width), parts[0].dtype), "join", 1 * PACE, 4, scalars=1
    )(me, *parts)


def place_kernel(rel, name, olds, me_ref, *refs):
    refs = refs[olds:]
    halves = refs[:2]
    outs, holds, sems = (refs[2:4], refs[4:6], refs[6]) if name == "in" else (refs[2:3], refs[3:4], refs[4])
    half = me_ref[0] ^ rel
    copies = []
    for kind, half_ref in enumerate(halves):
        rows = half_ref.shape[1]
        for j in range(16):
            tile = half_ref[tile_place(kind, j) ^ me_ref[1 + kind]].astype(F32)
            at = 0
            for hold in holds:
                hold[kind, j * rows : (j + 1) * rows, :] = tile[:, at : at + hold.shape[2]]
                at += hold.shape[2]
            if j % 8 != 7:
                continue
            size = 8 * rows
            for out, hold in zip(outs, holds):
                high, wide = hold.shape[1:]
                first = (j // 8) * size
                if name == "down":
                    spot = out.at[pl.ds(pl.multiple_of((half * 2 + kind) * high + first, size), size), :]
                elif name == "up":
                    spot = out.at[first : first + size, cut((half * 2 + kind) * wide, wide)]
                else:
                    spot = out.at[kind * high + first : kind * high + first + size, cut(half * wide, wide)]
                near_part = hold.at[kind, first : first + size, :]
                copies.append(pltpu.make_async_copy(near_part, spot, sems.at[len(copies)]))
                copies[-1].start()
    for copy in copies:
        copy.wait()


PLACES = {
    "down": [((FF, D), (D, D))],
    "up": [((D, FF), (D, D))],
    "in": [((D, 3 * D), (D // 2, 3 * D // 2)), ((D, D), (D // 2, D // 2))],
}


def place(name, rel, me, halves, before=None):
    outs = PLACES[name]
    olds = [] if before is None else list(before)
    return kernel_call(
        functools.partial(place_kernel, rel, name, len(olds)),
        [pltpu.HBM(whole, F32) for whole, _ in outs],
        "place", 2 * PACE, 10, scalars=1, far=len(olds), far_outs=range(len(outs)),
        scratch=[VMEM((2,) + part, F32) for _, part in outs] + [pltpu.SemaphoreType.DMA((4 * len(outs),))],
        aliases={1 + i: i for i in range(len(olds))},
    )(me, *(away(old) for old in olds), *halves)


def device_count():
    return lax.axis_size("gr") * lax.axis_size("gc")


def swap(values, mask):
    pairs = [(i, i ^ mask) for i in range(device_count())]
    return lax.ppermute(values, ("gr", "gc"), pairs)


def plus(left, *others):
    total = left.astype(F32)
    for other in others:
        total = total + other.astype(F32)
    return total.astype(BF)


def packed_slot(extra):
    high = lax.reduce_precision(extra, exponent_bits=8, mantissa_bits=7)
    return jnp.concatenate([high, extra - high]).astype(BF)[None]


def swap_with(tiles, extra, mask):
    if extra is None:
        return swap(tiles, mask), None
    got = swap(jnp.concatenate([tiles, packed_slot(extra)]), mask)
    wide = got[-1].astype(F32)
    cut_at = extra.shape[0]
    return got[:-1], extra + (wide[:cut_at] + wide[cut_at:])


def flow(send, keep_of, extra_of=None):
    (got,) = yield (swap(send, 1),)
    one, one_far, two, two_far = halve(keep_of(), got)
    one, two = yield plus(one, swap(one_far, 2)), plus(two, swap(two_far, 4))
    one, two = plus(one[:4], swap(one[4:], 4)), plus(two[:4], swap(two[4:], 2))
    ours, others = yield jnp.stack([one[:2], two[:2]], axis=1), jnp.stack([one[2:], two[2:]], axis=1)
    (both,) = yield (plus(ours, swap(others, 8)),)
    own = plus(both[0], swap(both[1], 16))
    mask = 32
    while mask < device_count():
        own = plus(own, swap(own, mask))
        mask *= 2
    (own,) = yield (own,)
    extra = None if extra_of is None else extra_of()
    mask = 32
    while extra is not None and mask < device_count():
        extra = extra + swap(extra, mask)
        mask *= 2
    got, extra = swap_with(own, extra, 16)
    both, extra = yield jnp.concatenate([own, got]), extra
    got, extra = swap_with(both, extra, 8)
    both = jnp.concatenate([both, got])
    one, two, extra = yield both[::2], both[1::2], extra
    got, extra = swap_with(one, extra, 4)
    one, two, extra = yield jnp.concatenate([one, got]), jnp.concatenate([two, swap(two, 2)]), extra
    got, extra = swap_with(one, extra, 2)
    one, two, extra = yield jnp.concatenate([one, got]), jnp.concatenate([two, swap(two, 4)]), extra
    return (one, two), (swap(one, 1), swap(two, 1)), extra


def flow_near(sums):
    yield (sums + swap(sums, 1),)


class Line:
    def __init__(self, steps, made):
        self.steps, self.made = steps, made
        self.result = None
        self.opened = False

    def go(self, made):
        try:
            self.made = self.steps(*made) if not self.opened else self.steps.send(made)
            if not self.opened:
                self.steps, self.made = self.made, next(self.made)
            self.opened = True
        except StopIteration as end:
            self.result = self.made = end.value


class Rounds:
    def __init__(self, me, token):
        self.me, self.token, self.going = me, token, []

    def begin(self, lines):
        kept = [line.made for line in self.going]
        made, kept, token = lax.optimization_barrier(([line.made for line in lines], kept, self.token))
        self.token = (kept, token)
        for line, arrays in zip(self.going, kept):
            line.made = arrays
            if line.result is not None:
                line.result = arrays
        for line, arrays in zip(lines, made):
            line.go(arrays if line not in self.going else line.made)
        self.going = lines

    def work(self, call, *args, token=lambda made: made):
        me, _ = lax.optimization_barrier((self.me, self.token))
        made = call(me, *args)
        self.token = token(made)
        return made


def bits_of(value, order):
    out = jnp.zeros_like(value)
    for bit in order:
        out = out * 2 + ((value >> bit) & 1)
    return out


def per_device(
    tokens, span_ids, mlm_pos, mlm_count, mlm_grad, positive, w_in, b_query, b_value, w_out, b_out,
    ln1_gain, ln1_bias, w_up, b_up, w_down, b_down, ln2_gain, ln2_bias,
):
    rows, length = span_ids.shape
    spans = mlm_pos.shape[0]
    index = lax.axis_index("gr") * lax.axis_size("gc") + lax.axis_index("gc")
    chip = (index >> 1) & 15
    me = jnp.stack(
        [index & 1, bits_of(chip, (0, 1, 2, 3)), bits_of(chip, (1, 0, 2, 3))]
    ).astype(jnp.int32)
    where = index.astype(jnp.int32)[None]
    me, where, b_query = lax.optimization_barrier((me, where, b_query))
    weights = (w_out, w_up, w_down)
    vectors = (b_out, ln1_gain, ln1_bias, b_up, b_down, ln2_gain, ln2_bias)

    packed, mixed, lse, weights = attend(span_ids, tokens, w_in, b_query, b_value, weights)
    cls = opening(spans, span_ids, tokens, mixed, weights, vectors)
    cls, here = lax.optimization_barrier((cls, me))
    masks = (0, 8, 16, 24)
    parts = [cls] + [swap(cls, m) for m in masks[1:]]
    made = [feed(0, here, tokens, mixed[0], weights, vectors)]
    table = merge(parts)
    table, here, _ = lax.optimization_barrier((table, me, made[0][1]))
    tables = [table] + [swap(table, m) for m in range(1, 8)]
    slots_of = [tuple(m ^ k for k in masks) for m in range(8)]
    made.append(feed(1, here, tokens, mixed[1], weights, vectors))
    bit = 32
    while bit < device_count():
        table, masks = jnp.concatenate(tables), sum(slots_of, ())
        tables = [table, swap(table, bit)]
        slots_of = [masks, tuple(m ^ bit for m in masks)]
        bit *= 2
    low, n1, f1, hidden, slope, n2, f2, layer_out = zip(*made)
    loss, second, branch, sums_two = contrast(
        where, mlm_count, span_ids, positive, tables, slots_of, mlm_pos, mlm_grad, n2, f2, ln2_gain
    )

    order = Rounds(me, sums_two)
    lines, keeps, links, sums_in, sides = {}, {}, [None] * rows, [], {}
    d_packed = [None] * rows
    part = [0] * rows

    def gradient(name, call, *args):
        if name not in lines:
            send = order.work(functools.partial(call, rel=1), *args)
            extra_of = (lambda: lines["S"].made[0]) if name == "D" else None
            lines[name] = Line(functools.partial(flow, keep_of=lambda: keeps[name], extra_of=extra_of), (send,))
        else:
            keeps[name] = order.work(functools.partial(call, rel=0), *args)

    def link(row):
        links[row] = order.work(
            chain, branch[row], second[row], slope[row], n1[row], f1[row], ln1_gain,
            weights[2], weights[1], weights[0], token=lambda made: made[4],
        )

    def back(row, parts):
        pairs = (part[row] * HEADS // 4, (part[row] + parts) * HEADS // 4)
        d_packed[row], sums = order.work(
            functools.partial(attend_back, row, pairs),
            span_ids, packed[row], mixed[row], links[row][3], lse[row], d_packed[row],
            token=lambda made: made[1],
        )
        part[row] += parts
        sums_in.append(sums)

    def settle(name, rel):
        call = functools.partial(place, {"D": "down", "U": "up", "I": "in"}[name], rel)
        sides[name] = order.work(call, lines[name].result[rel], sides.get(name))

    for going, events in PLAN:
        if "S" in going:
            sums_one = sum(made[4] for made in links)
            lines["S"] = Line(flow_near, (jnp.concatenate([sums_two, sums_one, sum(sums_in)]),))
        order.begin([lines[name] for name in going])
        for event in events:
            if event == "gd":
                gradient("D", grad_down, hidden, branch)
            elif event == "gu":
                gradient("U", grad_up, low, [made[0] for made in links])
            elif event == "gi":
                gradient("I", grad_in, tokens, d_packed, mixed, [made[2] for made in links])
            elif event == "gt":
                sides["T"] = order.work(grad_token, [made[1] for made in links], d_packed, w_in)
            elif event == "jo":
                sides["J"] = order.work(join, layer_out)
            elif event == "ou":
                sides["S"] = order.work(spread, lines["D"].result[2])
            elif event[:2] == "ch":
                link(int(event[2]))
            elif event[:2] == "ab":
                back(int(event[2]), 1)
            elif event[:2] == "aw":
                back(int(event[2]), 2)
            else:
                settle(event[1], int(event[2]))
    grad_tokens, g_down, g_up, g_in, small = (sides[name] for name in "TDUIS")

    return (
        sides["J"], grad_tokens, g_in[0], small[0], small[1], g_in[1], *small[2:5], g_up[0], small[5], g_down[0],
        *small[6:], loss.reshape(()),
    )


PLAN = (
    ("", ("gd",)),
    ("D", ("gd",)),
    ("D", ("ch0", "ch1", "gu",)),
    ("DU", ("gu", "aw0",)),
    ("DU", ("ab1", "ab1", "gi",)),
    ("DUIS", ("gi",)),
    ("DUI", ("gt",)),
    ("DUI", ()),
    ("DUI", ()),
    ("DUI", ()),
    ("DUI", ()),
    ("UI", ("pD0",)),
    ("UI", ("pD1",)),
    ("I", ("pU0", "pU1", "ou", "jo",)),
    ("I", ("pI0",)),
    ("", ("pI1",)),
)


def solution(mesh):
    split = P(("gr", "gc"))
    return jax.shard_map(
        per_device,
        mesh=mesh,
        in_specs=(split,) * 5 + (P(),) * 14,
        out_specs=(split, split) + (P(),) * 14,
        check_vma=False,
    )
```
